32 devices in a mesh: rows: 8 (over y, x, core), cols: 4 (over z).
Axes of the slice: x: 2, y: 2, z: 4, core: 2. Of those that a mesh axis runs over, the one named last changes fastest.
Arguments:
- local_weights: bfloat16 [8, 4, 48, 256, 256], P('rows', 'cols'), may hold values from -6 to 6
- local_gains: float32 [8, 4, 48, 2, 256], P('rows', 'cols'), may hold values from 1 to 48
- local_coords: int32 [8, 4, 48, 2], P('rows', 'cols'), may hold values from 0 to 15, as said below
- remote_weights: bfloat16 [8, 4, 8, 256, 256], P('rows', 'cols'), may hold values from -6 to 6
- remote_gains: float32 [8, 4, 8, 2, 256], P('rows', 'cols'), may hold values from 1 to 48
- remote_groups: int32 [8, 4, 8], P('rows', 'cols'), may hold values from 0 to 7, as said below
- remote_coords: int32 [8, 4, 8, 2], P('rows', 'cols'), may hold values from 0 to 15
- start_block: float32 [16, 32768], P(None, 'rows'), may hold values from -20 to 20
Outputs:
- embedding: float32 [16, 32768], P(None, ('rows', 'cols'))
The draws below stay inside these ranges and needn't reach their ends.
Inputs may be any that keep to these rules, and one draw needn't show every extreme that they name: For each [r, c], the row tiles local_coords[r, c, :, 0] take every value 0 to 15. For each [r, c], every group named in remote_groups[r, c, :] is named exactly 2 times; one group is named 2 times in every [r, c].
All inputs are finite; a program needn't handle non-finite values.
Results may differ from the reference program's by a relative error of at most 0.0046.
Values may be sent and summed in bfloat16 or wider, within the bound.
No kernel may reach another device: no remote copies, remote signals or barrier semaphores. Data moves between devices by JAX's collectives and lax.ppermute only.
A program may use at most 128 MiB of HBM per device.

```python
import math
import jax
import jax.numpy as jnp
from jax import lax

TILE = 256
WIDTH = 16
BR = 16
LOC = 48
MOST = 2
ITERS = 2
LT = 8
N_ROWS = 8
N_COLS = 4


def draw_remote_groups(key, part):
    hub_group = jax.random.randint(jax.random.fold_in(key, 7), (), 0, N_ROWS)
    sender_keys = jax.random.split(jax.random.fold_in(key, 11), N_ROWS * N_COLS)

    def draw_sender(sender_key):
        key_first, key_second = jax.random.split(sender_key)
        shuffled = jax.random.permutation(key_first, N_ROWS)
        position = jnp.argsort(shuffled)
        position = jnp.where(jnp.arange(N_ROWS) == hub_group, -1, position)
        ordered = jnp.argsort(position)
        slot_order = jax.random.permutation(key_second, LT)
        return ordered[slot_order // MOST]
    return jax.vmap(draw_sender)(sender_keys).reshape(N_ROWS, N_COLS, LT).astype(jnp.int32)


def draw_local_coords(key, part):
    sender_keys = jax.random.split(jax.random.fold_in(key, 13), N_ROWS * N_COLS)

    def draw_sender(sender_key):
        key_first, key_second, key_third, key_fourth = jax.random.split(sender_key, 4)
        covered = jax.random.permutation(key_first, BR).astype(jnp.int32)
        extra_rows = jax.random.randint(key_second, (LOC - BR,), 0, BR).astype(jnp.int32)
        row_tiles = jnp.concatenate([covered, extra_rows])[jax.random.permutation(key_third, LOC)]
        col_tiles = jax.random.randint(key_fourth, (LOC,), 0, BR).astype(jnp.int32)
        return jnp.stack([row_tiles, col_tiles], axis=1)
    return jax.vmap(draw_sender)(sender_keys).reshape(N_ROWS, N_COLS, LOC, 2).astype(jnp.int32)


def gain_draw(key, tile_count):
    shape_full = (N_ROWS, N_COLS, tile_count, 2, TILE)
    uniform_part = jax.random.uniform(key, shape_full, jnp.float32)
    spread = jnp.exp(math.log(10.0) * uniform_part)
    rising = 1.0 + 2.0 * jnp.arange(N_COLS, dtype=jnp.float32) / max(N_COLS - 1, 1)
    row_gain = jnp.arange(2) == 0
    factor = jnp.where(row_gain[None, None, None, :, None], rising[None, :, None, None, None], 1.0)
    return (spread * factor).astype(jnp.float32)


def draw_local_gains(key, part):
    return gain_draw(jax.random.fold_in(key, 17), LOC)


def draw_remote_gains(key, part):
    return gain_draw(jax.random.fold_in(key, 19), LT)


def draw_start_block(key, part):
    vertex_total = N_ROWS * BR * TILE
    group_of = (jnp.arange(vertex_total) // (BR * TILE)).astype(jnp.float32)
    rising = 1.0 + 4.0 * group_of / max(N_ROWS - 1, 1)
    values = jax.random.truncated_normal(jax.random.fold_in(key, 23), -4.0, 4.0, (WIDTH, vertex_total), jnp.float32)
    return (values * rising[None, :]).astype(jnp.float32)


def plant(entries, own_key, least, largest):
    longest = entries.shape.index(max(entries.shape))
    spots = []
    for shift in (0, 1):
        where = [jax.random.randint(jax.random.fold_in(own_key, axis), (), 0, length) for axis, length in enumerate(entries.shape)]
        where[longest] = (where[longest] + shift) % entries.shape[longest]
        spots.append(tuple(where))
    return entries.at[spots[0]].set(least).at[spots[1]].set(largest)


def block_levels(stream_key, shape, cuts, smallest, top_value):
    level = 1.0
    for dim, shards_of in cuts:
        draws = jax.random.uniform(jax.random.fold_in(jax.random.fold_in(stream_key, 6), dim), (shards_of,), jnp.float32, smallest / len(cuts), top_value / len(cuts))
        level = level * jnp.repeat(jnp.exp(draws), shape[dim] // shards_of).reshape((-1,) + (1,) * (len(shape) - 1 - dim))
    return level


def noise(rng, shape, deviation, reach, cuts=(), kind=jnp.bfloat16):
    factor_of = block_levels(rng, shape, cuts, -0.22, 0.18) if cuts else 1.0
    array = jax.random.normal(rng, shape, jnp.float32) * deviation * factor_of
    return jnp.minimum(jnp.maximum(array, -reach), reach).astype(kind)


def setup_inputs(seed: int = 0) -> dict:
    seeds = jax.random.split(jax.random.key(seed), 9)
    local_weights = noise(seeds[0], (N_ROWS, N_COLS, LOC, TILE, TILE), 1.0, 6.0, ((0, 8), (1, 4)))
    local_gains = draw_local_gains(jax.random.fold_in(seeds[8], 71), 0)
    local_coords = draw_local_coords(jax.random.fold_in(seeds[8], 71), 0)
    remote_weights = noise(seeds[3], (N_ROWS, N_COLS, LT, TILE, TILE), 1.0, 6.0, ((0, 8), (1, 4)))
    remote_gains = draw_remote_gains(jax.random.fold_in(seeds[8], 71), 0)
    remote_groups = draw_remote_groups(jax.random.fold_in(seeds[8], 71), 0)
    remote_coords = plant(jax.random.randint(seeds[6], (N_ROWS, N_COLS, LT, 2), 0, BR), jax.random.fold_in(seeds[6], 1), 0, BR - 1).astype(jnp.int32)
    start_block = draw_start_block(jax.random.fold_in(seeds[8], 71), 0)
    return dict(local_weights=local_weights, local_gains=local_gains, local_coords=local_coords, remote_weights=remote_weights, remote_gains=remote_gains, remote_groups=remote_groups, remote_coords=remote_coords, start_block=start_block)


def dequantize(weights, gain_pair):
    return (gain_pair[:, 0, :, None] * weights.astype(jnp.float32) * gain_pair[:, 1, None, :]).astype(jnp.bfloat16)

def reference(local_weights, local_gains, local_coords, remote_weights, remote_gains, remote_groups, remote_coords, start_block):
    devices = N_ROWS * N_COLS
    tile_total = N_ROWS * BR
    vertices = tile_total * TILE
    dev_row = (jnp.arange(devices, dtype=jnp.int32) // N_COLS).astype(jnp.int32)
    local_pairs = local_coords.reshape(devices, LOC, 2).astype(jnp.int32)
    remote_pairs = remote_coords.reshape(devices, LT, 2).astype(jnp.int32)
    local_set = (local_weights.reshape(devices, LOC, TILE, TILE), local_gains.reshape(devices, LOC, 2, TILE), (dev_row[:, None] * BR + local_pairs[:, :, 0]).astype(jnp.int32), (dev_row[:, None] * BR + local_pairs[:, :, 1]).astype(jnp.int32))
    remote_set = (remote_weights.reshape(devices, LT, TILE, TILE), remote_gains.reshape(devices, LT, 2, TILE), (dev_row[:, None] * BR + remote_pairs[:, :, 0]).astype(jnp.int32), (remote_groups.reshape(devices, LT).astype(jnp.int32) * BR + remote_pairs[:, :, 1]).astype(jnp.int32))
    both_sets = (local_set, remote_set)

    def degree_step(summed, pieces):
        weights, gain_pair, row_tiles, col_tiles = pieces
        magnitude = jnp.abs(dequantize(weights, gain_pair).astype(jnp.float32))
        summed = summed.at[row_tiles].add(lax.optimization_barrier(jnp.sum(magnitude, axis=2)))
        summed = summed.at[col_tiles].add(lax.optimization_barrier(jnp.sum(magnitude, axis=1)))
        return (summed, None)
    degree = jnp.zeros((tile_total, TILE), jnp.float32)
    for tile_set in both_sets:
        degree = lax.scan(degree_step, degree, tile_set)[0]
    inv_root = 1.0 / jnp.sqrt(degree)
    vectors = start_block.reshape(WIDTH, tile_total, TILE).transpose(1, 0, 2)
    for iteration in range(ITERS):
        scaled_block = (vectors * inv_root[:, None, :]).astype(jnp.bfloat16)

        def product_step(summed, pieces):
            weights, gain_pair, row_tiles, col_tiles = pieces
            tile_full = dequantize(weights, gain_pair).astype(jnp.float32)
            forward = jnp.einsum('tij,tkj->tki', tile_full, scaled_block[col_tiles].astype(jnp.float32))
            backward = jnp.einsum('tij,tki->tkj', tile_full, scaled_block[row_tiles].astype(jnp.float32))
            summed = summed.at[row_tiles].add(forward)
            summed = summed.at[col_tiles].add(backward)
            return (summed, None)
        image = jnp.zeros((tile_total, WIDTH, TILE), jnp.float32)
        for tile_set in both_sets:
            image = lax.scan(product_step, image, tile_set)[0]
        image = image * inv_root[:, None, :]
        gram = jnp.einsum('bki,bli->kl', image, image, precision=lax.Precision.HIGHEST) / vertices
        factor = jnp.linalg.cholesky(gram)
        inverse = jax.scipy.linalg.solve_triangular(factor, jnp.eye(WIDTH, dtype=jnp.float32), lower=True)
        vectors = jnp.einsum('kl,bli->bki', inverse, image, precision=lax.Precision.HIGHEST)
    return vectors.transpose(1, 0, 2).reshape(WIDTH, vertices)
```

```python
import functools

import jax
import jax.numpy as jnp
from jax import lax
from jax.experimental import pallas as pl
from jax.experimental.pallas import tpu as pltpu
from jax.sharding import PartitionSpec as P

TILE = 256
WIDTH = 16
BR = 16
MOST = 2
CHUNK = 8
F32 = jnp.float32
BF16 = jnp.bfloat16
HIGHEST = lax.Precision.HIGHEST
VMEM_LIMIT = 48 * 1024 * 1024

vmem = pl.BlockSpec(memory_space=pltpu.VMEM)
smem = pl.BlockSpec(memory_space=pltpu.SMEM)
hbm = pl.BlockSpec(memory_space=pl.ANY)


def shape(dims, dtype=F32):
    return jax.ShapeDtypeStruct(dims, dtype)


def call(kernel, out_shape, in_specs, scratch_shapes=(), flops=10**6, moved=10**6, name=None):
    return pl.pallas_call(
        kernel,
        out_shape=out_shape,
        in_specs=in_specs,
        out_specs=jax.tree.map(lambda _: vmem, out_shape),
        scratch_shapes=scratch_shapes,
        cost_estimate=pl.CostEstimate(flops=flops, bytes_accessed=moved, transcendentals=0),
        compiler_params=pltpu.CompilerParams(vmem_limit_bytes=VMEM_LIMIT),
        name=name,
    )


def times(left, right):
    return lax.dot_general(left, right, (((1,), (0,)), ((), ())), preferred_element_type=F32)


def times_t(left, right):
    return lax.dot_general(left, right, (((1,), (1,)), ((), ())), preferred_element_type=F32)


def slots_of(groups_ref, count_ref, tile_count, group_count):
    for g in range(group_count):
        count_ref[g] = 0
    for t in range(tile_count):
        g = groups_ref[t]
        m = count_ref[g]
        count_ref[g] = m + 1
        yield t, g, m


def scale_chunk(raw, gains):
    row_gain = jnp.transpose(gains[:, 0, :])
    return [
        (row_gain[:, k : k + 1] * raw[k].astype(F32) * gains[k, 1:2, :]).astype(BF16)
        for k in range(CHUNK)
    ]


def remote_degree_kernel(
    group_count, weights, gains, groups, coords, scaled, payload, row_degree, count
):
    tiles = weights.shape[0]
    sub = lax.broadcasted_iota(jnp.int32, (8, TILE), 0)
    blank = jnp.where((sub >= MOST) & (sub < 2 * MOST), -1.0, 0.0).astype(F32)
    for g in range(group_count):
        payload[g] = blank
    row_degree[...] = jnp.zeros(row_degree.shape, F32)
    ones = jnp.ones((16, TILE), BF16)
    places = slots_of(groups, count, tiles, group_count)
    for first in range(0, tiles, CHUNK):
        pieces = scale_chunk(weights[first : first + CHUNK], gains[first : first + CHUNK])
        for piece in pieces:
            t, g, m = next(places)
            scaled[t] = piece
            size = jnp.abs(piece)
            r, c = coords[t, 0], coords[t, 1]
            row_degree[pl.ds(r, 1), :] += times_t(ones, size)[:1]
            payload[g, pl.ds(m, 1), :] = times(ones, size)[:1]
            payload[g, pl.ds(MOST + m, 1), :] = jnp.full((1, TILE), c, jnp.int32).astype(F32)


def local_degree_kernel(weights, gains, coords, scaled, degree, sems):
    chunks = weights.shape[0] // CHUNK
    copies = [
        pltpu.make_async_copy(
            weights.at[pl.ds(n * CHUNK, CHUNK)], scaled.at[pl.ds(n * CHUNK, CHUNK)], sems.at[n]
        )
        for n in range(chunks)
    ]
    for copy in copies:
        copy.start()
    degree[...] = jnp.zeros(degree.shape, F32)
    ones = jnp.ones((16, TILE), BF16)

    def step(n, _):
        pltpu.make_async_copy(
            weights.at[pl.ds(n * CHUNK, CHUNK)], scaled.at[pl.ds(n * CHUNK, CHUNK)], sems.at[n]
        ).wait()
        base = pl.multiple_of(n * CHUNK, CHUNK)
        pieces = scale_chunk(scaled[pl.ds(base, CHUNK)], gains[pl.ds(base, CHUNK)])
        for k, piece in enumerate(pieces):
            scaled[base + k] = piece
            size = jnp.abs(piece)
            r, c = coords[base + k, 0], coords[base + k, 1]
            degree[pl.ds(r, 1), :] += times_t(ones, size)[:1]
            degree[pl.ds(c, 1), :] += times(ones, size)[:1]
        return 0

    lax.fori_loop(0, chunks, step, 0)


def join_degree_kernel(arrived, row_degree, local_degree, joined):
    total = row_degree[...] + local_degree[...]
    sub = lax.broadcasted_iota(jnp.int32, total.shape, 0).astype(F32)
    for g in range(arrived.shape[0]):
        block = arrived[g]
        for m in range(MOST):
            hit = sub == block[MOST + m : MOST + m + 1, :]
            total += jnp.where(hit, block[m : m + 1, :], 0.0)
    joined[...] = total


def outgoing(x, scaled, groups, coords, targets, payload, count):
    group_count = payload.shape[0]
    for g in range(group_count):
        payload[g, MOST : 2 * MOST] = jnp.zeros((MOST, WIDTH, TILE), BF16)
    for t, g, m in slots_of(groups, count, scaled.shape[0], group_count):
        payload[g, MOST + m] = times(x[coords[t, 0]], scaled[t]).astype(BF16)
    for g in range(group_count):
        for m in range(MOST):
            payload[g, m] = x[jnp.maximum(targets[g, m], 0)]


def first_block_kernel(
    splits, start, scaled, groups, coords, targets, *refs
):
    degrees, (inv_root, x, payload, count) = refs[:splits], refs[splits:]
    degree = degrees[0][...]
    for other in degrees[1:]:
        degree += other[...]
    inv = 1.0 / jnp.sqrt(degree)
    inv_root[...] = inv
    for k in range(BR):
        x[k] = (start[:, k * TILE : (k + 1) * TILE] * inv[k : k + 1, :]).astype(BF16)
    outgoing(x, scaled, groups, coords, targets, payload, count)


def next_block_kernel(
    splits, vertices, scaled, inv_root, groups, coords, targets, *refs
):
    quarters, (x, payload, gram_out, count) = refs[:splits], refs[splits:]
    me = lax.axis_index("cols")
    quarter = BR // splits
    for k, part in enumerate(quarters):
        base = pl.multiple_of((me ^ k) * quarter, quarter)
        x[pl.ds(base, quarter)] = part[...]
    outgoing(x, scaled, groups, coords, targets, payload, count)
    gram = jnp.zeros((WIDTH, WIDTH), F32)
    for k in range(BR):
        image = x[k].astype(F32) / inv_root[k : k + 1, :]
        gram += lax.dot_general(
            image, image, (((1,), (1,)), ((), ())), precision=HIGHEST, preferred_element_type=F32
        )
    gram = gram / vertices
    high = gram.astype(BF16)
    middle = (gram - high.astype(F32)).astype(BF16)
    low = (gram - high.astype(F32) - middle.astype(F32)).astype(BF16)
    block = jnp.concatenate(
        [high, middle, low, jnp.zeros((WIDTH, TILE - 3 * WIDTH), BF16)], axis=1
    )
    for g in range(payload.shape[0]):
        payload[g, 2 * MOST] = block
    gram_out[...] = gram


def local_products_kernel(x, scaled, coords, partial):
    partial[...] = jnp.zeros(partial.shape, F32)
    unroll = 4

    def step(n, _):
        places, results = [], []
        for k in range(unroll):
            t = n * unroll + k
            r, c = coords[t, 0], coords[t, 1]
            tile = scaled[t]
            results.append((times_t(x[c], tile), times(x[r], tile)))
            places.append((r, c))
        for (r, c), (forward, backward) in zip(places, results):
            partial[r] += forward
            partial[c] += backward
        return 0

    lax.fori_loop(0, scaled.shape[0] // unroll, step, 0)


def remote_products_kernel(
    splits, arrived, scaled, partial, groups, coords, targets, *refs
):
    outs, (total, count) = refs[:splits], refs[splits:]
    group_count = arrived.shape[0]
    total[...] = partial[...]
    for t, g, m in slots_of(groups, count, scaled.shape[0], group_count):
        total[coords[t, 0]] += times_t(arrived[g, m], scaled[t])
    for g in range(group_count):
        for m in range(MOST):
            total[jnp.maximum(targets[g, m], 0)] += arrived[g, MOST + m].astype(F32)
    me = lax.axis_index("cols")
    quarter = BR // splits
    for k, out in enumerate(outs):
        base = pl.multiple_of((me ^ k) * quarter, quarter)
        out[...] = total[pl.ds(base, quarter)].astype(out.dtype)


def quarter_sum(pieces, inv_root, me):
    quarter = pieces[0].shape[0]
    images, roots = [], []
    for k in range(quarter):
        value = pieces[0][k]
        for piece in pieces[1:]:
            value += piece[k].astype(F32)
        root = inv_root[pl.ds(me * quarter + k, 1), :]
        images.append(value * root)
        roots.append(root)
    return images, roots


def middle_quarter_kernel(splits, inv_root, *refs):
    pieces, (x,) = refs[:splits], refs[splits:]
    images, roots = quarter_sum(pieces, inv_root, lax.axis_index("cols"))
    for k, (image, root) in enumerate(zip(images, roots)):
        x[k] = (image * root).astype(BF16)


def inverse_factor(gram):
    row = lax.broadcasted_iota(jnp.int32, (WIDTH, 2 * WIDTH), 0)
    col = lax.broadcasted_iota(jnp.int32, (WIDTH, 2 * WIDTH), 1)
    eye = jnp.where(
        lax.broadcasted_iota(jnp.int32, (WIDTH, WIDTH), 0)
        == lax.broadcasted_iota(jnp.int32, (WIDTH, WIDTH), 1),
        1.0,
        0.0,
    ).astype(F32)
    work = jnp.concatenate([gram, eye], axis=1)
    for k in range(WIDTH - 1):
        pivot = work[k : k + 1, :]
        factor = work[:, k : k + 1] / work[k : k + 1, k : k + 1]
        work = work - jnp.where(row > k, factor * pivot, 0.0)
    diagonal = jnp.sum(jnp.where(row == col, work, 0.0), axis=1, keepdims=True)
    return work[:, WIDTH:] / jnp.sqrt(diagonal)


def middle_factor_kernel(arrived, inverse):
    gram = jnp.zeros((WIDTH, WIDTH), F32)
    for g in range(arrived.shape[0]):
        block = arrived[g, 2 * MOST].astype(F32)
        gram += (block[:, 2 * WIDTH : 3 * WIDTH] + block[:, WIDTH : 2 * WIDTH]) + block[:, :WIDTH]
    inverse[...] = inverse_factor(gram)


def last_quarter_kernel(splits, vertices, inv_root, inverse, *refs):
    pieces, (image_out, grams) = refs[:splits], refs[splits:]
    images, _ = quarter_sum(pieces, inv_root, lax.axis_index("cols"))
    first = inverse[...]
    gram = jnp.zeros((WIDTH, WIDTH), F32)
    for k, image in enumerate(images):
        value = jnp.dot(first, image, precision=HIGHEST, preferred_element_type=F32)
        image_out[:, k * TILE : (k + 1) * TILE] = value
        gram += lax.dot_general(
            value, value, (((1,), (1,)), ((), ())), precision=HIGHEST, preferred_element_type=F32
        )
    gram = gram / vertices
    half = WIDTH // 2
    block = jnp.concatenate(
        [gram[:half], gram[half:], jnp.zeros((half, 128 - 2 * WIDTH), F32)], axis=1
    )
    for n in range(grams.shape[0]):
        grams[n] = block


def finish_kernel(grams, image, out):
    block = grams[0]
    for n in range(1, grams.shape[0]):
        block = block + grams[n]
    gram = jnp.concatenate([block[:, :WIDTH], block[:, WIDTH : 2 * WIDTH]], axis=0)
    out[...] = jnp.dot(
        inverse_factor(gram), image[...], precision=HIGHEST, preferred_element_type=F32
    )


def per_device(
    local_weights,
    local_gains,
    local_coords,
    remote_weights,
    remote_gains,
    remote_groups,
    remote_coords,
    start_block,
):
    groups = lax.axis_size("rows")
    splits = lax.axis_size("cols")
    vertices = groups * BR * TILE
    quarter = BR // splits
    local_tiles, remote_tiles = local_weights.shape[2], remote_weights.shape[2]
    listed, coords, near = remote_groups[0, 0], remote_coords[0, 0], local_coords[0, 0]
    count = pltpu.SMEM((groups,), jnp.int32)

    def swap(value, k):
        return lax.ppermute(value, "cols", [(j, j ^ k) for j in range(splits)])

    def trade(value):
        return lax.all_to_all(value, "rows", split_axis=0, concat_axis=0, tiled=True)

    remote_scaled, sums, row_degree = call(
        functools.partial(remote_degree_kernel, groups),
        (
            shape((remote_tiles, TILE, TILE), BF16),
            shape((groups, 8, TILE)),
            shape((BR, TILE)),
        ),
        [vmem, vmem, smem, smem],
        [count],
        name="remote_degree",
    )(remote_weights[0, 0], remote_gains[0, 0], listed, coords)
    sums_in = trade(sums)
    local_scaled, local_degree = call(
        local_degree_kernel,
        (shape((local_tiles, TILE, TILE), BF16), shape((BR, TILE))),
        [hbm, vmem, smem],
        [pltpu.SemaphoreType.DMA((local_tiles // CHUNK,))],
        moved=10**7,
        name="local_degree",
    )(local_weights[0, 0], local_gains[0, 0], near)
    targets = sums_in[:, MOST : 2 * MOST, 0].astype(jnp.int32)
    joined = call(
        join_degree_kernel, shape((BR, TILE)), [vmem, vmem, vmem], name="join_degree"
    )(sums_in, row_degree, local_degree)
    degrees = [joined] + [swap(joined, k) for k in range(1, splits)]
    inv_root, x, payload = call(
        functools.partial(first_block_kernel, splits),
        (
            shape((BR, TILE)),
            shape((BR, WIDTH, TILE), BF16),
            shape((groups, 2 * MOST, WIDTH, TILE), BF16),
        ),
        [vmem, vmem, smem, smem, smem] + [vmem] * splits,
        [count],
        name="first_block",
    )(start_block, remote_scaled, listed, coords, targets, *degrees)

    def product(x, payload):
        arrived = trade(payload)
        partial = call(
            local_products_kernel,
            shape((BR, WIDTH, TILE)),
            [vmem, vmem, smem],
            moved=10**7,
            name="local_products",
        )(x, local_scaled, near)
        pieces = call(
            functools.partial(remote_products_kernel, splits),
            tuple(
                shape((quarter, WIDTH, TILE), BF16 if k else F32) for k in range(splits)
            ),
            [vmem, vmem, vmem, smem, smem, smem],
            [pltpu.VMEM((BR, WIDTH, TILE), F32), count],
            name="remote_products",
        )(arrived, remote_scaled, partial, listed, coords, targets)
        return arrived, [pieces[0]] + [swap(pieces[k], k) for k in range(1, splits)]

    _, pieces = product(x, payload)
    x_quarter = call(
        functools.partial(middle_quarter_kernel, splits),
        shape((quarter, WIDTH, TILE), BF16),
        [vmem] * (1 + splits),
        name="middle_quarter",
    )(inv_root, *pieces)
    quarters = [x_quarter] + [swap(x_quarter, k) for k in range(1, splits)]
    x, payload, _ = call(
        functools.partial(next_block_kernel, splits, vertices),
        (
            shape((BR, WIDTH, TILE), BF16),
            shape((groups, 2 * MOST + 1, WIDTH, TILE), BF16),
            shape((WIDTH, WIDTH)),
        ),
        [vmem, vmem, smem, smem, smem] + [vmem] * splits,
        [count],
        name="next_block",
    )(remote_scaled, inv_root, listed, coords, targets, *quarters)
    arrived, pieces = product(x, payload)
    inverse = call(
        middle_factor_kernel, shape((WIDTH, WIDTH)), [vmem], name="middle_factor"
    )(arrived)
    image, grams = call(
        functools.partial(last_quarter_kernel, splits, vertices),
        (shape((WIDTH, quarter * TILE)), shape((groups * splits, 8, 128))),
        [vmem] * (2 + splits),
        name="last_quarter",
    )(inv_root, inverse, *pieces)
    grams = lax.all_to_all(
        grams, ("rows", "cols"), split_axis=0, concat_axis=0, tiled=True
    )
    return call(finish_kernel, shape((WIDTH, quarter * TILE)), [vmem, vmem], name="finish")(
        grams, image
    )


def solution(mesh):
    in_specs = (
        P("rows", "cols", None, None, None),
        P("rows", "cols", None, None, None),
        P("rows", "cols", None, None),
        P("rows", "cols", None, None, None),
        P("rows", "cols", None, None, None),
        P("rows", "cols", None),
        P("rows", "cols", None, None),
        P(None, "rows"),
    )
    out_specs = P(None, ("rows", "cols"))
    return jax.shard_map(
        per_device, mesh=mesh, in_specs=in_specs, out_specs=out_specs, check_vma=False
    )
```

```python
import functools

import jax
import jax.numpy as jnp
from jax import lax
from jax.experimental import pallas as pl
from jax.experimental.pallas import tpu as pltpu
from jax.sharding import PartitionSpec as P

TILE = 256
WIDTH = 16
BR = 16
MOST = 2
CHUNK = 8
F32 = jnp.float32
BF16 = jnp.bfloat16
HIGHEST = lax.Precision.HIGHEST
VMEM_LIMIT = 48 * 1024 * 1024

vmem = pl.BlockSpec(memory_space=pltpu.VMEM)
smem = pl.BlockSpec(memory_space=pltpu.SMEM)
hbm = pl.BlockSpec(memory_space=pltpu.HBM)


def shape(dims, dtype=F32):
    return jax.ShapeDtypeStruct(dims, dtype)


def call(kernel, out_shape, in_specs, scratch_shapes=(), flops=10**6, moved=10**6, name=None):
    return pl.pallas_call(
        kernel,
        out_shape=out_shape,
        in_specs=in_specs,
        out_specs=jax.tree.map(lambda _: vmem, out_shape),
        scratch_shapes=scratch_shapes,
        cost_estimate=pl.CostEstimate(flops=flops, bytes_accessed=moved, transcendentals=0),
        compiler_params=pltpu.CompilerParams(vmem_limit_bytes=VMEM_LIMIT),
        name=name,
    )


def times(left, right):
    return lax.dot_general(left, right, (((1,), (0,)), ((), ())), preferred_element_type=F32)


def times_t(left, right):
    return lax.dot_general(left, right, (((1,), (1,)), ((), ())), preferred_element_type=F32)


def in_hbm(value):
    return pltpu.with_memory_space_constraint(value, pltpu.HBM)


def slots_of(groups_ref, count_ref, tile_count, group_count):
    for g in range(group_count):
        count_ref[g] = 0
    for t in range(tile_count):
        g = groups_ref[0, 0, t]
        m = count_ref[g]
        count_ref[g] = m + 1
        yield t, g, m


def weighted_sums(size, gains):
    sub = lax.broadcasted_iota(jnp.int32, (8, TILE), 0)
    gains = jnp.abs(gains)
    left = jnp.where(sub == 0, gains[0:1, :], jnp.where(sub == 1, gains[1:2, :], 0.0))
    high = left.astype(BF16).astype(F32)
    halves = jnp.concatenate([high, left - high], axis=0).astype(BF16)
    rows, cols = times_t(halves, size), times(halves, size)
    return (rows[1:2] + rows[9:10]) * gains[0:1, :], (cols[0:1] + cols[8:9]) * gains[1:2, :]


def remote_degree_kernel(
    group_count,
    weights,
    gains,
    groups,
    coords,
    payload,
    row_degree,
    tiles,
    tile_gains,
    tile_groups,
    tile_coords,
    count,
    sems,
):
    copies = [
        pltpu.make_async_copy(source, target, sems.at[n])
        for n, (source, target) in enumerate(
            [(groups, tile_groups), (coords, tile_coords), (gains, tile_gains), (weights, tiles)]
        )
    ]
    for copy in copies:
        copy.start()
    sub = lax.broadcasted_iota(jnp.int32, (8, TILE), 0)
    blank = jnp.where((sub >= MOST) & (sub < 2 * MOST), -1.0, 0.0).astype(F32)
    for g in range(group_count):
        payload[g] = blank
    row_degree[...] = jnp.zeros(row_degree.shape, F32)
    for copy in copies:
        copy.wait()
    places = slots_of(tile_groups, count, weights.shape[2], group_count)
    for t, g, m in places:
        r, c = tile_coords[0, 0, 0, t], tile_coords[0, 0, 1, t]
        by_row, by_col = weighted_sums(jnp.abs(tiles[0, 0, t]), tile_gains[0, 0, t])
        row_degree[pl.ds(r, 1), :] += by_row
        payload[g, pl.ds(m, 1), :] = by_col
        payload[g, pl.ds(MOST + m, 1), :] = jnp.full((1, TILE), c, jnp.int32).astype(F32)


def local_degree_kernel(
    weights, gains, coords, degree, tiles, tile_gains, tile_coords, sems, small_sems
):
    chunks = weights.shape[2] // CHUNK

    def copy_of(n):
        part = pl.ds(n * CHUNK, CHUNK)
        return pltpu.make_async_copy(weights.at[0, 0, part], tiles.at[part], sems.at[n])

    small = [
        pltpu.make_async_copy(coords, tile_coords, small_sems.at[0]),
        pltpu.make_async_copy(gains, tile_gains, small_sems.at[1]),
    ]
    for copy in small:
        copy.start()
    for n in range(chunks):
        copy_of(n).start()
    degree[...] = jnp.zeros(degree.shape, F32)
    for copy in small:
        copy.wait()

    def step(n, _):
        copy_of(n).wait()
        for k in range(CHUNK):
            t = n * CHUNK + k
            r, c = tile_coords[0, 0, 0, t], tile_coords[0, 0, 1, t]
            by_row, by_col = weighted_sums(jnp.abs(tiles[t]), tile_gains[0, 0, t])
            degree[pl.ds(r, 1), :] += by_row
            degree[pl.ds(c, 1), :] += by_col
        return 0

    lax.fori_loop(0, chunks, step, 0)


def scale_kernel(raw, gains, scaled):
    row_gain = jnp.transpose(gains[0, 0, :, 0, :])
    for k in range(raw.shape[2]):
        scaled[k] = (
            row_gain[:, k : k + 1] * raw[0, 0, k].astype(F32) * gains[0, 0, k, 1:2, :]
        ).astype(BF16)


def scale(weights, gains, name):
    count = weights.shape[2]
    return pl.pallas_call(
        scale_kernel,
        out_shape=shape((count, TILE, TILE), BF16),
        grid=(count // CHUNK,),
        in_specs=[
            pl.BlockSpec((1, 1, CHUNK, TILE, TILE), lambda n: (0, 0, n, 0, 0)),
            pl.BlockSpec((1, 1, CHUNK, 2, TILE), lambda n: (0, 0, n, 0, 0)),
        ],
        out_specs=pl.BlockSpec((CHUNK, TILE, TILE), lambda n: (n, 0, 0)),
        cost_estimate=pl.CostEstimate(
            flops=2 * count * TILE * TILE, bytes_accessed=4 * count * TILE * TILE, transcendentals=0
        ),
        compiler_params=pltpu.CompilerParams(vmem_limit_bytes=VMEM_LIMIT),
        name=name,
    )(weights, gains)


def join_degree_kernel(arrived, row_degree, local_degree, joined):
    total = row_degree[...] + local_degree[...]
    sub = lax.broadcasted_iota(jnp.int32, total.shape, 0).astype(F32)
    for g in range(arrived.shape[0]):
        block = arrived[g]
        for m in range(MOST):
            hit = sub == block[MOST + m : MOST + m + 1, :]
            total += jnp.where(hit, block[m : m + 1, :], 0.0)
    joined[...] = total


def outgoing(x, scaled, groups, coords, targets, payload, count):
    group_count = payload.shape[0]
    for g in range(group_count):
        payload[g, MOST : 2 * MOST] = jnp.zeros((MOST, WIDTH, TILE), BF16)
    for t, g, m in slots_of(groups, count, scaled.shape[0], group_count):
        payload[g, MOST + m] = times(x[coords[0, 0, 0, t]], scaled[t]).astype(BF16)
    for g in range(group_count):
        for m in range(MOST):
            payload[g, m] = x[jnp.maximum(targets[g, m], 0)]


def first_block_kernel(
    start, scaled, groups, coords, targets, mine, theirs, inv_root, x, payload, count
):
    inv = 1.0 / jnp.sqrt(mine[...] + theirs[...])
    inv_root[...] = inv
    for k in range(BR):
        x[k] = (start[:, k * TILE : (k + 1) * TILE] * inv[k : k + 1, :]).astype(BF16)
    outgoing(x, scaled, groups, coords, targets, payload, count)


def pair_sum_kernel(mine, theirs, total, sent):
    value = mine[...] + theirs[...].astype(F32)
    total[...] = value
    sent[...] = value.astype(BF16)


def next_block_kernel(
    vertices, scaled, inv_root, groups, coords, targets, mine, theirs, x, payload, count
):
    gram = jnp.zeros((2 * WIDTH, 2 * WIDTH), F32)
    for k in range(BR):
        value = mine[k] + theirs[k].astype(F32)
        root = inv_root[k : k + 1, :]
        image = value * root
        x[k] = (image * root).astype(BF16)
        high = image.astype(BF16)
        halves = jnp.concatenate([high, (image - high.astype(F32)).astype(BF16)], axis=0)
        gram += times_t(halves, halves)
    outgoing(x, scaled, groups, coords, targets, payload, count)
    low = gram[:WIDTH, WIDTH:] + gram[WIDTH:, :WIDTH] + gram[WIDTH:, WIDTH:]
    gram = (gram[:WIDTH, :WIDTH] + low) / vertices
    high = gram.astype(BF16)
    middle = (gram - high.astype(F32)).astype(BF16)
    low = (gram - high.astype(F32) - middle.astype(F32)).astype(BF16)
    block = jnp.concatenate(
        [high, middle, low, jnp.zeros((WIDTH, TILE - 3 * WIDTH), BF16)], axis=1
    )
    for g in range(payload.shape[0]):
        payload[g, 2 * MOST] = block


def local_products_kernel(x, weights, gains, coords, partial, tiles, sems):
    count, chunk = weights.shape[2], tiles.shape[0] // sems.shape[0]
    batch = 2 * CHUNK if count % (2 * CHUNK) == 0 else CHUNK

    def copy_of(n):
        part = pl.ds(n * chunk, chunk)
        return pltpu.make_async_copy(weights.at[0, 0, part], tiles.at[part], sems.at[n])

    for n in range(count // chunk):
        copy_of(n).start()
    partial[...] = jnp.zeros(partial.shape, F32)

    def step(n, _):
        for k in range(batch // chunk):
            copy_of(n * (batch // chunk) + k).wait()
        base = n * batch
        row_gains = [
            jnp.transpose(gains[0, 0, pl.ds(base + k, CHUNK), 0, :]) for k in range(0, batch, CHUNK)
        ]
        places, results = [], []
        for k in range(batch):
            t = base + k
            r, c = coords[0, 0, 0, t], coords[0, 0, 1, t]
            row_gain = row_gains[k // CHUNK][:, k % CHUNK : k % CHUNK + 1]
            tile = (row_gain * tiles[t].astype(F32) * gains[0, 0, t, 1:2, :]).astype(BF16)
            results.append((times_t(x[c], tile), times(x[r], tile)))
            places.append((r, c))
        for (r, c), (forward, backward) in zip(places, results):
            partial[r] += forward
            partial[c] += backward
        return 0

    lax.fori_loop(0, count // batch, step, 0)


def remote_products_kernel(
    splits, whole, arrived, scaled, partial, groups, coords, targets, *refs
):
    outs, (total, count) = refs[:-2], refs[-2:]
    group_count = arrived.shape[0]
    total[...] = partial[...]
    for t, g, m in slots_of(groups, count, scaled.shape[0], group_count):
        total[coords[0, 0, 0, t]] += times_t(arrived[g, m], scaled[t])
    for g in range(group_count):
        for m in range(MOST):
            total[jnp.maximum(targets[g, m], 0)] += arrived[g, MOST + m].astype(F32)
    if whole:
        for out in outs:
            out[...] = total[...].astype(out.dtype)
        return
    me = lax.axis_index("cols")
    quarter = BR // splits
    for k, out in enumerate(outs):
        base = pl.multiple_of((me ^ k) * quarter, quarter)
        out[...] = total[pl.ds(base, quarter)].astype(out.dtype)


def quarter_sum(pieces, inv_root, me):
    quarter = pieces[0].shape[0]
    images, roots = [], []
    for k in range(quarter):
        value = pieces[0][k]
        for piece in pieces[1:]:
            value += piece[k].astype(F32)
        root = inv_root[pl.ds(me * quarter + k, 1), :]
        images.append(value * root)
        roots.append(root)
    return images, roots


def inverse_factor(gram):
    row = lax.broadcasted_iota(jnp.int32, (WIDTH, 2 * WIDTH), 0)
    col = lax.broadcasted_iota(jnp.int32, (WIDTH, 2 * WIDTH), 1)
    eye = jnp.where(
        lax.broadcasted_iota(jnp.int32, (WIDTH, WIDTH), 0)
        == lax.broadcasted_iota(jnp.int32, (WIDTH, WIDTH), 1),
        1.0,
        0.0,
    ).astype(F32)
    work = jnp.concatenate([gram, eye], axis=1)
    for k in range(WIDTH - 1):
        pivot = work[k : k + 1, :]
        factor = work[:, k : k + 1] / work[k : k + 1, k : k + 1]
        work = work - jnp.where(row > k, factor * pivot, 0.0)
    diagonal = jnp.sum(jnp.where(row == col, work, 0.0), axis=1, keepdims=True)
    return work[:, WIDTH:] / jnp.sqrt(diagonal)


def middle_factor_kernel(arrived, inverse):
    gram = jnp.zeros((WIDTH, WIDTH), F32)
    for g in range(arrived.shape[0]):
        block = arrived[g, 2 * MOST].astype(F32)
        gram += (block[:, 2 * WIDTH : 3 * WIDTH] + block[:, WIDTH : 2 * WIDTH]) + block[:, :WIDTH]
    inverse[...] = inverse_factor(gram)


def last_quarter_kernel(splits, vertices, inv_root, inverse, *refs):
    pieces, (image_out, grams) = refs[:splits], refs[splits:]
    images, _ = quarter_sum(pieces, inv_root, lax.axis_index("cols"))
    first = inverse[...]
    gram = jnp.zeros((WIDTH, WIDTH), F32)
    for k, image in enumerate(images):
        value = jnp.dot(first, image, precision=HIGHEST, preferred_element_type=F32)
        image_out[:, k * TILE : (k + 1) * TILE] = value
        gram += lax.dot_general(
            value, value, (((1,), (1,)), ((), ())), precision=HIGHEST, preferred_element_type=F32
        )
    gram = gram / vertices
    block = jnp.concatenate(
        [gram[4 * n : 4 * n + 4] for n in range(4)] + [jnp.zeros((4, 128 - 4 * WIDTH), F32)], axis=1
    )
    for n in range(grams.shape[0]):
        grams[n] = block


def finish_kernel(grams, image, out):
    block = grams[0]
    for n in range(1, grams.shape[0]):
        block = block + grams[n]
    gram = jnp.concatenate([block[:, WIDTH * n : WIDTH * (n + 1)] for n in range(4)], axis=0)
    out[...] = jnp.dot(
        inverse_factor(gram), image[...], precision=HIGHEST, preferred_element_type=F32
    )


def per_device(
    local_weights,
    local_gains,
    local_coords,
    remote_weights,
    remote_gains,
    remote_groups,
    remote_coords,
    start_block,
):
    groups = lax.axis_size("rows")
    splits = lax.axis_size("cols")
    vertices = groups * BR * TILE
    quarter = BR // splits
    local_coords, remote_coords = jnp.swapaxes(local_coords, 2, 3), jnp.swapaxes(remote_coords, 2, 3)
    local_tiles, remote_tiles = local_weights.shape[2], remote_weights.shape[2]
    count = pltpu.SMEM((groups,), jnp.int32)

    def swap(value, k):
        return lax.ppermute(value, "cols", [(j, j ^ k) for j in range(splits)])

    def trade(value):
        return lax.all_to_all(value, "rows", split_axis=0, concat_axis=0, tiled=True)

    listing = (remote_weights, remote_gains, remote_groups, remote_coords)
    sums, row_degree = call(
        functools.partial(remote_degree_kernel, groups),
        (shape((groups, 8, TILE)), shape((BR, TILE))),
        [hbm, hbm, hbm, hbm],
        [
            pltpu.VMEM(remote_weights.shape, BF16),
            pltpu.VMEM(remote_gains.shape, F32),
            pltpu.SMEM(remote_groups.shape, jnp.int32),
            pltpu.SMEM(remote_coords.shape, jnp.int32),
            count,
            pltpu.SemaphoreType.DMA((4,)),
        ],
        name="remote_degree",
    )(*[in_hbm(value) for value in listing])
    sums_in = trade(sums)
    local_degree = call(
        local_degree_kernel,
        shape((BR, TILE)),
        [hbm, hbm, hbm],
        [
            pltpu.VMEM((local_tiles, TILE, TILE), BF16),
            pltpu.VMEM(local_gains.shape, F32),
            pltpu.SMEM(local_coords.shape, jnp.int32),
            pltpu.SemaphoreType.DMA((local_tiles // CHUNK,)),
            pltpu.SemaphoreType.DMA((2,)),
        ],
        moved=10**7,
        name="local_degree",
    )(*[in_hbm(value) for value in (local_weights, local_gains, local_coords)])
    targets = sums_in[:, MOST : 2 * MOST, 0].astype(jnp.int32)
    joined = call(
        join_degree_kernel, shape((BR, TILE)), [vmem, vmem, vmem], name="join_degree"
    )(sums_in, row_degree, local_degree)
    step = 1
    while 2 * step < splits:
        joined = joined + swap(joined, step)
        step *= 2
    degrees = [joined, swap(joined, step)]
    remote_scaled = scale(remote_weights, remote_gains, "remote_scale")
    inv_root, x, payload = call(
        first_block_kernel,
        (
            shape((BR, TILE)),
            shape((BR, WIDTH, TILE), BF16),
            shape((groups, 2 * MOST, WIDTH, TILE), BF16),
        ),
        [vmem, vmem, smem, smem, smem, vmem, vmem],
        [count],
        name="first_block",
    )(start_block, remote_scaled, remote_groups, remote_coords, targets, *degrees)

    def product(x, payload, out_shape, whole):
        arrived = trade(payload)
        partial = call(
            local_products_kernel,
            shape((BR, WIDTH, TILE)),
            [vmem, hbm, vmem, smem],
            [
                pltpu.VMEM((local_tiles, TILE, TILE), BF16),
                pltpu.SemaphoreType.DMA((local_tiles // 4,)),
            ],
            moved=10**7,
            name="local_products",
        )(x, local_weights, local_gains, local_coords)
        return arrived, call(
            functools.partial(remote_products_kernel, splits, whole),
            out_shape,
            [vmem, vmem, vmem, smem, smem, smem],
            [pltpu.VMEM((BR, WIDTH, TILE), F32), count],
            name="remote_products",
        )(arrived, remote_scaled, partial, remote_groups, remote_coords, targets)

    _, (own, sent) = product(
        x, payload, (shape((BR, WIDTH, TILE)), shape((BR, WIDTH, TILE), BF16)), True
    )
    step = 1
    while 2 * step < splits:
        own, sent = call(
            pair_sum_kernel,
            (shape((BR, WIDTH, TILE)), shape((BR, WIDTH, TILE), BF16)),
            [vmem, vmem],
            name="pair_sum",
        )(own, swap(sent, step))
        step *= 2
    pieces = [own, swap(sent, step)]
    x, payload = call(
        functools.partial(next_block_kernel, vertices),
        (
            shape((BR, WIDTH, TILE), BF16),
            shape((groups, 2 * MOST + 1, WIDTH, TILE), BF16),
        ),
        [vmem, vmem, smem, smem, smem, vmem, vmem],
        [count],
        name="next_block",
    )(remote_scaled, inv_root, remote_groups, remote_coords, targets, *pieces)
    arrived, sent = product(
        x,
        payload,
        tuple(shape((quarter, WIDTH, TILE), BF16 if k else F32) for k in range(splits)),
        False,
    )
    pieces = [sent[0]] + [swap(sent[k], k) for k in range(1, splits)]
    inverse = call(
        middle_factor_kernel, shape((WIDTH, WIDTH)), [vmem], name="middle_factor"
    )(arrived)
    image, grams = call(
        functools.partial(last_quarter_kernel, splits, vertices),
        (shape((WIDTH, quarter * TILE)), shape((groups * splits, 4, 128))),
        [vmem] * (2 + splits),
        name="last_quarter",
    )(inv_root, inverse, *pieces)
    grams = lax.all_to_all(
        grams, ("rows", "cols"), split_axis=0, concat_axis=0, tiled=True
    )
    return call(finish_kernel, shape((WIDTH, quarter * TILE)), [vmem, vmem], name="finish")(
        grams, image
    )


def solution(mesh):
    in_specs = (
        P("rows", "cols", None, None, None),
        P("rows", "cols", None, None, None),
        P("rows", "cols", None, None),
        P("rows", "cols", None, None, None),
        P("rows", "cols", None, None, None),
        P("rows", "cols", None),
        P("rows", "cols", None, None),
        P(None, "rows"),
    )
    out_specs = P(None, ("rows", "cols"))
    return jax.shard_map(
        per_device, mesh=mesh, in_specs=in_specs, out_specs=out_specs, check_vma=False
    )
```

```python
import functools

import jax
import jax.numpy as jnp
from jax import lax
from jax.experimental import pallas as pl
from jax.experimental.pallas import tpu as pltpu
from jax.sharding import PartitionSpec as P

TILE = 256
WIDTH = 16
BR = 16
MOST = 2
CHUNK = 8
LANES = 128
F32 = jnp.float32
BF16 = jnp.bfloat16
HIGHEST = lax.Precision.HIGHEST
VMEM_LIMIT = 48 * 1024 * 1024

vmem = pl.BlockSpec(memory_space=pltpu.VMEM)
smem = pl.BlockSpec(memory_space=pltpu.SMEM)
hbm = pl.BlockSpec(memory_space=pltpu.HBM)
anywhere = pl.BlockSpec(memory_space=pl.ANY)


def shape(dims, dtype=F32):
    return jax.ShapeDtypeStruct(dims, dtype)


def call(kernel, out_shape, in_specs, scratch_shapes=(), flops=10**6, moved=10**6, name=None):
    return pl.pallas_call(
        kernel,
        out_shape=out_shape,
        in_specs=in_specs,
        out_specs=jax.tree.map(lambda _: vmem, out_shape),
        scratch_shapes=scratch_shapes,
        cost_estimate=pl.CostEstimate(flops=flops, bytes_accessed=moved, transcendentals=0),
        compiler_params=pltpu.CompilerParams(vmem_limit_bytes=VMEM_LIMIT),
        name=name,
    )


def times(left, right):
    return lax.dot_general(left, right, (((1,), (0,)), ((), ())), preferred_element_type=F32)


def times_t(left, right):
    return lax.dot_general(left, right, (((1,), (1,)), ((), ())), preferred_element_type=F32)


def in_hbm(value):
    return pltpu.with_memory_space_constraint(value, pltpu.HBM)


def fetch(sources, targets, sems):
    copies = [
        pltpu.make_async_copy(source, target, sems.at[n])
        for n, (source, target) in enumerate(zip(sources, targets))
    ]
    for copy in copies:
        copy.start()

    def wait():
        for copy in copies:
            copy.wait()

    return wait


def slots_of(groups_ref, count_ref, tile_count, group_count):
    for g in range(group_count):
        count_ref[g] = 0
    for t in range(tile_count):
        g = groups_ref[0, 0, t]
        m = count_ref[g]
        count_ref[g] = m + 1
        yield t, g, m


def weighted_sums(size, gains):
    sub = lax.broadcasted_iota(jnp.int32, (8, TILE), 0)
    gains = jnp.abs(gains)
    left = jnp.where(sub == 0, gains[0:1, :], jnp.where(sub == 1, gains[1:2, :], 0.0))
    high = left.astype(BF16).astype(F32)
    halves = jnp.concatenate([high, left - high], axis=0).astype(BF16)
    rows, cols = times_t(halves, size), times(halves, size)
    return (rows[1:2] + rows[9:10]) * gains[0:1, :], (cols[0:1] + cols[8:9]) * gains[1:2, :]


def remote_degree_kernel(
    group_count,
    weights,
    gains,
    groups,
    coords,
    payload,
    row_degree,
    tiles,
    tile_gains,
    tile_groups,
    tile_coords,
    count,
    sems,
):
    wait = fetch(
        (groups, coords, gains, weights), (tile_groups, tile_coords, tile_gains, tiles), sems
    )
    sub = lax.broadcasted_iota(jnp.int32, (8, TILE), 0)
    blank = jnp.where((sub >= MOST) & (sub < 2 * MOST), -1.0, 0.0).astype(F32)
    for g in range(group_count):
        payload[g] = blank
    row_degree[...] = jnp.zeros(row_degree.shape, F32)
    wait()
    places = slots_of(tile_groups, count, weights.shape[2], group_count)
    for t, g, m in places:
        r, c = tile_coords[0, 0, 0, t], tile_coords[0, 0, 1, t]
        by_row, by_col = weighted_sums(jnp.abs(tiles[0, 0, t]), tile_gains[0, 0, t])
        row_degree[pl.ds(r, 1), :] += by_row
        payload[g, pl.ds(m, 1), :] = by_col
        payload[g, pl.ds(MOST + m, 1), :] = jnp.full((1, TILE), c, jnp.int32).astype(F32)


def local_degree_kernel(
    weights, gains, coords, degree, tiles, tile_gains, tile_coords, sems, small_sems
):
    chunk = CHUNK
    chunks = weights.shape[2] // chunk
    batch = 2 * chunk if chunks % 2 == 0 else chunk

    def copy_of(n):
        part = pl.ds(n * chunk, chunk)
        return pltpu.make_async_copy(weights.at[0, 0, part], tiles.at[part], sems.at[n])

    small = [
        pltpu.make_async_copy(coords, tile_coords, small_sems.at[0]),
        pltpu.make_async_copy(gains, tile_gains, small_sems.at[1]),
    ]
    for copy in small:
        copy.start()
    for n in range(chunks):
        copy_of(n).start()
    degree[...] = jnp.zeros(degree.shape, F32)
    for copy in small:
        copy.wait()

    def step(n, _):
        for k in range(batch // chunk):
            copy_of(n * (batch // chunk) + k).wait()
        for k in range(batch):
            t = n * batch + k
            r, c = tile_coords[0, 0, 0, t], tile_coords[0, 0, 1, t]
            by_row, by_col = weighted_sums(jnp.abs(tiles[t]), tile_gains[0, 0, t])
            degree[pl.ds(r, 1), :] += by_row
            degree[pl.ds(c, 1), :] += by_col
        return 0

    lax.fori_loop(0, chunks * chunk // batch, step, 0)


def scale_kernel(raw, gains, scaled):
    row_gain = jnp.transpose(gains[0, 0, :, 0, :])
    for k in range(raw.shape[2]):
        scaled[k] = (
            row_gain[:, k : k + 1] * raw[0, 0, k].astype(F32) * gains[0, 0, k, 1:2, :]
        ).astype(BF16)


def scale(weights, gains, name):
    count = weights.shape[2]
    return pl.pallas_call(
        scale_kernel,
        out_shape=shape((count, TILE, TILE), BF16),
        grid=(count // CHUNK,),
        in_specs=[
            pl.BlockSpec((1, 1, CHUNK, TILE, TILE), lambda n: (0, 0, n, 0, 0)),
            pl.BlockSpec((1, 1, CHUNK, 2, TILE), lambda n: (0, 0, n, 0, 0)),
        ],
        out_specs=pl.BlockSpec((CHUNK, TILE, TILE), lambda n: (n, 0, 0)),
        cost_estimate=pl.CostEstimate(
            flops=2 * count * TILE * TILE, bytes_accessed=4 * count * TILE * TILE, transcendentals=0
        ),
        compiler_params=pltpu.CompilerParams(vmem_limit_bytes=VMEM_LIMIT),
        name=name,
    )(weights, gains)


def join_degree_kernel(arrived, row_degree, local_degree, joined):
    total = row_degree[...] + local_degree[...]
    sub = lax.broadcasted_iota(jnp.int32, total.shape, 0).astype(F32)
    for g in range(arrived.shape[0]):
        block = arrived[g]
        for m in range(MOST):
            hit = sub == block[MOST + m : MOST + m + 1, :]
            total += jnp.where(hit, block[m : m + 1, :], 0.0)
    joined[...] = total


def by_chips(groups):
    return groups // 2 <= 4


def place_of(group, group_count, core):
    if not by_chips(group_count):
        return group
    return ((group + core) % 2) * (group_count // 2) + group // 2


def outgoing(x, scaled, groups, coords, targets, staged, count, gram=None):
    group_count = staged.shape[0]
    core = lax.axis_index("rows") % 2
    for g in range(group_count):
        staged[g, MOST : 2 * MOST] = jnp.zeros((MOST, WIDTH, TILE), BF16)
        if gram is not None:
            staged[g, 2 * MOST] = gram
    for t, g, m in slots_of(groups, count, scaled.shape[0], group_count):
        place = place_of(g, group_count, core)
        staged[place, MOST + m] = times(x[coords[0, 0, 0, t]], scaled[t]).astype(BF16)
    for g in range(group_count):
        place = place_of(g, group_count, core)
        for m in range(MOST):
            staged[place, m] = x[jnp.maximum(targets[g, m], 0)]


def split_out(staged, outs):
    size = outs[0].shape[0]
    for k, out in enumerate(outs):
        out[...] = staged[k * size : (k + 1) * size]


def forward_kernel(near, passed, *pieces):
    chips = near.shape[0]
    me = lax.axis_index("rows")
    chip, core = me // 2, me % 2
    for k, piece in enumerate(pieces):
        piece[core] = near[chip ^ k]
        piece[1 - core] = passed[chip ^ k]


def by_group(arrived, joined):
    if len(arrived) == 1:
        joined[...] = arrived[0][...]
        return
    chip = lax.axis_index("rows") // 2
    for k, piece in enumerate(arrived):
        joined[pl.ds((chip ^ k) * 2, 2)] = piece[...]


def first_block_kernel(
    start, scaled, groups, coords, targets, mine, theirs, inv_root, x, *refs
):
    *outs, tile_groups, tile_coords, tile_targets, count, sems, staged = refs
    routes = (tile_groups, tile_coords, tile_targets)
    wait = fetch((groups, coords, targets), routes, sems)
    inv = 1.0 / jnp.sqrt(mine[...] + theirs[...])
    inv_root[...] = inv
    for k in range(BR):
        x[k] = (start[:, k * TILE : (k + 1) * TILE] * inv[k : k + 1, :]).astype(BF16)
    wait()
    outgoing(x, scaled, *routes, staged, count)
    split_out(staged, outs)


def pair_sum_kernel(mine, theirs, total, sent):
    value = mine[...] + theirs[...].astype(F32)
    total[...] = value
    sent[...] = value.astype(BF16)


def next_block_kernel(
    vertices, scaled, inv_root, groups, coords, targets, mine, theirs, x, *refs
):
    *outs, tile_groups, tile_coords, tile_targets, count, sems, staged = refs
    routes = (tile_groups, tile_coords, tile_targets)
    wait = fetch((groups, coords, targets), routes, sems)
    gram = jnp.zeros((2 * WIDTH, 2 * WIDTH), F32)
    for k in range(BR):
        value = mine[k] + theirs[k].astype(F32)
        root = inv_root[k : k + 1, :]
        image = value * root
        x[k] = (image * root).astype(BF16)
        high = image.astype(BF16)
        halves = jnp.concatenate([high, (image - high.astype(F32)).astype(BF16)], axis=0)
        gram += times_t(halves, halves)
    low = gram[:WIDTH, WIDTH:] + gram[WIDTH:, :WIDTH] + gram[WIDTH:, WIDTH:]
    gram = (gram[:WIDTH, :WIDTH] + low) / vertices
    high = gram.astype(BF16)
    middle = (gram - high.astype(F32)).astype(BF16)
    low = (gram - high.astype(F32) - middle.astype(F32)).astype(BF16)
    block = jnp.concatenate(
        [high, middle, low, jnp.zeros((WIDTH, TILE - 3 * WIDTH), BF16)], axis=1
    )
    wait()
    outgoing(x, scaled, *routes, staged, count, block)
    split_out(staged, outs)


def local_products_kernel(
    x, weights, gains, coords, partial, tiles, sems, tile_coords, coord_sems
):
    count, chunk = tiles.shape[0], CHUNK
    batch = 2 * chunk if count % (2 * chunk) == 0 else chunk

    def copy_of(n):
        part = pl.ds(n * chunk, chunk)
        return pltpu.make_async_copy(weights.at[0, 0, part], tiles.at[part], sems.at[n])

    wait = fetch((coords,), (tile_coords,), coord_sems)
    for n in range(count // chunk):
        copy_of(n).start()
    partial[...] = jnp.zeros(partial.shape, F32)
    wait()

    def step(n, _):
        for k in range(batch // chunk):
            copy_of(n * (batch // chunk) + k).wait()
        base = n * batch
        row_gains = [
            jnp.transpose(gains[0, 0, pl.ds(base + k, CHUNK), 0, :]) for k in range(0, batch, CHUNK)
        ]
        places, results = [], []
        for k in range(batch):
            t = base + k
            r, c = tile_coords[0, 0, 0, t], tile_coords[0, 0, 1, t]
            row_gain = row_gains[k // CHUNK][:, k % CHUNK : k % CHUNK + 1]
            tile = (row_gain * tiles[t].astype(F32) * gains[0, 0, t, 1:2, :]).astype(BF16)
            results.append((times_t(x[c], tile), times(x[r], tile)))
            places.append((r, c))
        for (r, c), (forward, backward) in zip(places, results):
            partial[r] += forward
            partial[c] += backward
        return 0

    lax.fori_loop(0, count // batch, step, 0)


def remote_products_kernel(splits, whole, pieces, scaled, partial, groups, coords, targets, *refs):
    arrived, refs = refs[:pieces], refs[pieces:]
    *outs, total, tile_groups, tile_coords, tile_targets, count, sems, joined = refs
    wait = fetch((groups, coords, targets), (tile_groups, tile_coords, tile_targets), sems)
    group_count = joined.shape[0]
    by_group(arrived, joined)
    total[...] = partial[...]
    wait()
    for t, g, m in slots_of(tile_groups, count, scaled.shape[0], group_count):
        total[tile_coords[0, 0, 0, t]] += times_t(joined[g, m], scaled[t])
    for g in range(group_count):
        for m in range(MOST):
            total[jnp.maximum(tile_targets[g, m], 0)] += joined[g, MOST + m].astype(F32)
    if whole:
        for out in outs:
            out[...] = total[...].astype(out.dtype)
        return
    me = lax.axis_index("cols")
    quarter = BR // splits
    for k, out in enumerate(outs):
        base = pl.multiple_of((me ^ k) * quarter, quarter)
        out[...] = total[pl.ds(base, quarter)].astype(out.dtype)


def quarter_sum(pieces, inv_root, me):
    quarter = pieces[0].shape[0]
    images, roots = [], []
    for k in range(quarter):
        value = pieces[0][k]
        for piece in pieces[1:]:
            value += piece[k].astype(F32)
        root = inv_root[pl.ds(me * quarter + k, 1), :]
        images.append(value * root)
        roots.append(root)
    return images, roots


def eliminate(gram, right):
    shape = (WIDTH, LANES)
    row = lax.broadcasted_iota(jnp.int32, shape, 0)
    lane = lax.broadcasted_iota(jnp.int32, shape, 1)
    gram = jnp.concatenate([gram, jnp.zeros((WIDTH, LANES - WIDTH), F32)], axis=1)
    for k in range(0, WIDTH, 2):
        first = jnp.broadcast_to(gram[:, k : k + 1], shape)
        second = jnp.broadcast_to(gram[:, k + 1 : k + 2], shape)
        factor = first / first[k : k + 1]
        second = second - factor * second[k : k + 1]
        then = jnp.where(row > k + 1, second / second[k + 1 : k + 2], 0.0)
        link = factor[k + 1 : k + 2]
        factor = jnp.where(row > k, factor, 0.0)

        def step(work):
            top = work[k : k + 1, :]
            return work - factor * top - then * (work[k + 1 : k + 2, :] - link * top)

        gram, right = step(gram), [step(block) for block in right]
    pivots = jnp.sum(jnp.where(row == lane, gram, 0.0), axis=1, keepdims=True)
    root = jnp.broadcast_to(1.0 / jnp.sqrt(pivots), shape)
    return [block * root for block in right]


def middle_factor_kernel(*refs):
    *arrived, inverse = refs
    gram = jnp.zeros((WIDTH, WIDTH), F32)
    for block in [piece[g, 2 * MOST] for piece in arrived for g in range(piece.shape[0])]:
        block = block.astype(F32)
        gram += (block[:, 2 * WIDTH : 3 * WIDTH] + block[:, WIDTH : 2 * WIDTH]) + block[:, :WIDTH]
    eye = lax.broadcasted_iota(jnp.int32, (WIDTH, LANES), 0) == lax.broadcasted_iota(
        jnp.int32, (WIDTH, LANES), 1
    )
    (result,) = eliminate(gram, [eye.astype(F32)])
    inverse[...] = result[:, :WIDTH]


def last_quarter_kernel(splits, vertices, inv_root, inverse, *refs):
    pieces, (image_out, grams) = refs[:splits], refs[splits:]
    images, _ = quarter_sum(pieces, inv_root, lax.axis_index("cols"))
    first = inverse[...]
    gram = jnp.zeros((WIDTH, WIDTH), F32)
    for k, image in enumerate(images):
        value = jnp.dot(first, image, precision=HIGHEST, preferred_element_type=F32)
        image_out[:, k * TILE : (k + 1) * TILE] = value
        gram += lax.dot_general(
            value, value, (((1,), (1,)), ((), ())), precision=HIGHEST, preferred_element_type=F32
        )
    gram = gram / vertices
    block = jnp.concatenate(
        [gram[4 * n : 4 * n + 4] for n in range(4)] + [jnp.zeros((4, LANES - 4 * WIDTH), F32)], axis=1
    )
    for n in range(grams.shape[0]):
        grams[n] = block


def finish_kernel(grams, image, out):
    block = grams[0]
    for n in range(1, grams.shape[0]):
        block = block + grams[n]
    gram = jnp.concatenate([block[:, WIDTH * n : WIDTH * (n + 1)] for n in range(4)], axis=0)
    starts = range(0, out.shape[1], LANES)
    for n, block in zip(starts, eliminate(gram, [image[:, n : n + LANES] for n in starts])):
        out[:, n : n + LANES] = block


def per_device(
    local_weights,
    local_gains,
    local_coords,
    remote_weights,
    remote_gains,
    remote_groups,
    remote_coords,
    start_block,
):
    groups = lax.axis_size("rows")
    splits = lax.axis_size("cols")
    vertices = groups * BR * TILE
    quarter = BR // splits
    local_coords, remote_coords = jnp.swapaxes(local_coords, 2, 3), jnp.swapaxes(remote_coords, 2, 3)
    local_tiles, remote_tiles = local_weights.shape[2], remote_weights.shape[2]
    count = pltpu.SMEM((groups,), jnp.int32)
    routes = [
        pltpu.SMEM(remote_groups.shape, jnp.int32),
        pltpu.SMEM(remote_coords.shape, jnp.int32),
        pltpu.SMEM((groups, MOST), jnp.int32),
        count,
        pltpu.SemaphoreType.DMA((3,)),
    ]

    partners = [2 * 2**k - 1 for k in range(splits.bit_length() - 1)]

    def swap(value, k):
        return lax.ppermute(value, "cols", [(j, j ^ k) for j in range(splits)])

    def trade(value):
        return lax.all_to_all(value, "rows", split_axis=0, concat_axis=0, tiled=True)

    listing = (remote_weights, remote_gains, remote_groups, remote_coords)
    sums, row_degree = call(
        functools.partial(remote_degree_kernel, groups),
        (shape((groups, 8, TILE)), shape((BR, TILE))),
        [hbm, hbm, hbm, hbm],
        [
            pltpu.VMEM(remote_weights.shape, BF16),
            pltpu.VMEM(remote_gains.shape, F32),
            pltpu.SMEM(remote_groups.shape, jnp.int32),
            pltpu.SMEM(remote_coords.shape, jnp.int32),
            count,
            pltpu.SemaphoreType.DMA((4,)),
        ],
        name="remote_degree",
    )(*[in_hbm(value) for value in listing])
    sums_in = trade(sums)
    local_degree = call(
        local_degree_kernel,
        shape((BR, TILE)),
        [hbm, hbm, hbm],
        [
            pltpu.VMEM((local_tiles, TILE, TILE), BF16),
            pltpu.VMEM(local_gains.shape, F32),
            pltpu.SMEM(local_coords.shape, jnp.int32),
            pltpu.SemaphoreType.DMA((local_tiles // CHUNK,)),
            pltpu.SemaphoreType.DMA((2,)),
        ],
        moved=10**7,
        name="local_degree",
    )(*[in_hbm(value) for value in (local_weights, local_gains, local_coords)])
    targets = sums_in[:, MOST : 2 * MOST, 0].astype(jnp.int32)
    joined = call(
        join_degree_kernel, shape((BR, TILE)), [vmem, vmem, vmem], name="join_degree"
    )(sums_in, row_degree, local_degree)
    for k in partners[:-1]:
        joined = joined + swap(joined, k)
    degrees = [joined, swap(joined, partners[-1])]
    remote_scaled = scale(remote_weights, remote_gains, "remote_scale")
    def sent_blocks(blocks):
        if by_chips(groups):
            return (shape((groups // 2, blocks, WIDTH, TILE), BF16),) * 2
        return (shape((groups, blocks, WIDTH, TILE), BF16),)

    def staging(blocks):
        return pltpu.VMEM((groups, blocks, WIDTH, TILE), BF16)

    inv_root, x, *sent = call(
        first_block_kernel,
        (shape((BR, TILE)), shape((BR, WIDTH, TILE), BF16)) + sent_blocks(2 * MOST),
        [vmem, vmem, anywhere, anywhere, anywhere, vmem, vmem],
        routes + [staging(2 * MOST)],
        name="first_block",
    )(start_block, remote_scaled, remote_groups, remote_coords, targets, *degrees)

    def local_products(x):
        return call(
            local_products_kernel,
            shape((BR, WIDTH, TILE)),
            [vmem, hbm, vmem, anywhere],
            [
                pltpu.VMEM((local_tiles, TILE, TILE), BF16),
                pltpu.SemaphoreType.DMA((local_tiles // CHUNK,)),
                pltpu.SMEM(local_coords.shape, jnp.int32),
                pltpu.SemaphoreType.DMA((1,)),
            ],
            flops=4 * local_tiles * TILE * TILE * WIDTH,
            moved=2 * local_tiles * TILE * TILE,
            name="local_products",
        )(x, local_weights, local_gains, local_coords)

    def product(x, sent, out_shape, whole):
        blocks = sent[0].shape[1]
        if by_chips(groups):
            near, far = sent
            passed = lax.ppermute(far, "rows", [(j, j ^ 1) for j in range(groups)])
            own, *others = call(
                forward_kernel,
                (shape((2, blocks, WIDTH, TILE), BF16),) * (groups // 2),
                [vmem, vmem],
                name="forward",
            )(near, passed)
            arrived = [own] + [
                lax.ppermute(piece, "rows", [(j, j ^ (2 * k)) for j in range(groups)])
                for k, piece in enumerate(others, 1)
            ]
            partial = local_products(x)
        else:
            arrived = [trade(sent[0])]
            partial = local_products(x)
        return arrived, call(
            functools.partial(remote_products_kernel, splits, whole, len(arrived)),
            out_shape,
            [vmem, vmem, anywhere, anywhere, anywhere] + [vmem] * len(arrived),
            [pltpu.VMEM((BR, WIDTH, TILE), F32)] + routes + [staging(blocks)],
            name="remote_products",
        )(remote_scaled, partial, remote_groups, remote_coords, targets, *arrived)

    _, (own, sent) = product(
        x, sent, (shape((BR, WIDTH, TILE)), shape((BR, WIDTH, TILE), BF16)), True
    )
    for k in partners[:-1]:
        own, sent = call(
            pair_sum_kernel,
            (shape((BR, WIDTH, TILE)), shape((BR, WIDTH, TILE), BF16)),
            [vmem, vmem],
            name="pair_sum",
        )(own, swap(sent, k))
    x, *sent = call(
        functools.partial(next_block_kernel, vertices),
        (shape((BR, WIDTH, TILE), BF16),) + sent_blocks(2 * MOST + 1),
        [vmem, vmem, anywhere, anywhere, anywhere, vmem, vmem],
        routes + [staging(2 * MOST + 1)],
        name="next_block",
    )(
        remote_scaled,
        inv_root,
        remote_groups,
        remote_coords,
        targets,
        own,
        swap(sent, partners[-1]),
    )
    arrived, sent = product(
        x,
        sent,
        tuple(shape((quarter, WIDTH, TILE), BF16 if k else F32) for k in range(splits)),
        False,
    )
    pieces = [sent[0]] + [swap(sent[k], k) for k in range(1, splits)]
    inverse = call(
        middle_factor_kernel,
        shape((WIDTH, WIDTH)),
        [vmem] * len(arrived),
        name="middle_factor",
    )(*arrived)
    image, grams = call(
        functools.partial(last_quarter_kernel, splits, vertices),
        (shape((WIDTH, quarter * TILE)), shape((groups * splits, 4, LANES))),
        [vmem] * (2 + splits),
        name="last_quarter",
    )(inv_root, inverse, *pieces)
    grams = lax.all_to_all(
        grams, ("rows", "cols"), split_axis=0, concat_axis=0, tiled=True
    )
    return call(finish_kernel, shape((WIDTH, quarter * TILE)), [vmem, vmem], name="finish")(
        grams, image
    )


def solution(mesh):
    in_specs = (
        P("rows", "cols", None, None, None),
        P("rows", "cols", None, None, None),
        P("rows", "cols", None, None),
        P("rows", "cols", None, None, None),
        P("rows", "cols", None, None, None),
        P("rows", "cols", None),
        P("rows", "cols", None, None),
        P(None, "rows"),
    )
    out_specs = P(None, ("rows", "cols"))
    return jax.shard_map(
        per_device, mesh=mesh, in_specs=in_specs, out_specs=out_specs, check_vma=False
    )
```

```python
import functools

import jax
import jax.numpy as jnp
from jax import lax
from jax.experimental import pallas as pl
from jax.experimental.pallas import tpu as pltpu
from jax.sharding import PartitionSpec as P

TILE = 256
WIDTH = 16
BR = 16
MOST = 2
CHUNK = 8
HELD = 16
LANES = 128
F32 = jnp.float32
BF16 = jnp.bfloat16
HIGHEST = lax.Precision.HIGHEST
VMEM_LIMIT = 48 * 1024 * 1024

vmem = pl.BlockSpec(memory_space=pltpu.VMEM)
smem = pl.BlockSpec(memory_space=pltpu.SMEM)
hbm = pl.BlockSpec(memory_space=pltpu.HBM)
anywhere = pl.BlockSpec(memory_space=pl.ANY)


def shape(dims, dtype=F32):
    return jax.ShapeDtypeStruct(dims, dtype)


def call(kernel, out_shape, in_specs, scratch_shapes=(), flops=10**6, moved=10**6, name=None):
    return pl.pallas_call(
        kernel,
        out_shape=out_shape,
        in_specs=in_specs,
        out_specs=jax.tree.map(lambda _: vmem, out_shape),
        scratch_shapes=scratch_shapes,
        cost_estimate=pl.CostEstimate(flops=flops, bytes_accessed=moved, transcendentals=0),
        compiler_params=pltpu.CompilerParams(vmem_limit_bytes=VMEM_LIMIT),
        name=name,
    )


def times(left, right):
    return lax.dot_general(left, right, (((1,), (0,)), ((), ())), preferred_element_type=F32)


def times_t(left, right):
    return lax.dot_general(left, right, (((1,), (1,)), ((), ())), preferred_element_type=F32)


def in_hbm(value):
    return pltpu.with_memory_space_constraint(value, pltpu.HBM)


def fetch(sources, targets, sems):
    copies = [
        pltpu.make_async_copy(source, target, sems.at[n])
        for n, (source, target) in enumerate(zip(sources, targets))
    ]
    for copy in copies:
        copy.start()

    def wait():
        for copy in copies:
            copy.wait()

    return wait


def slots_of(groups_ref, count_ref, tile_count, group_count):
    for g in range(group_count):
        count_ref[g] = 0
    for t in range(tile_count):
        g = groups_ref[0, 0, t]
        m = count_ref[g]
        count_ref[g] = m + 1
        yield t, g, m


def weighted_sums(size, gains):
    sub = lax.broadcasted_iota(jnp.int32, (8, TILE), 0)
    gains = jnp.abs(gains)
    left = jnp.where(sub == 0, gains[0:1, :], jnp.where(sub == 1, gains[1:2, :], 0.0))
    high = left.astype(BF16).astype(F32)
    halves = jnp.concatenate([high, left - high], axis=0).astype(BF16)
    rows, cols = times_t(halves, size), times(halves, size)
    return (rows[1:2] + rows[9:10]) * gains[0:1, :], (cols[0:1] + cols[8:9]) * gains[1:2, :]


def remote_degree_kernel(
    group_count,
    weights,
    gains,
    groups,
    coords,
    payload,
    row_degree,
    tiles,
    tile_gains,
    tile_groups,
    tile_coords,
    count,
    sems,
):
    wait = fetch(
        (groups, coords, gains, weights), (tile_groups, tile_coords, tile_gains, tiles), sems
    )
    sub = lax.broadcasted_iota(jnp.int32, (8, TILE), 0)
    blank = jnp.where((sub >= MOST) & (sub < 2 * MOST), -1.0, 0.0).astype(F32)
    for g in range(group_count):
        payload[g] = blank
    row_degree[...] = jnp.zeros(row_degree.shape, F32)
    wait()
    places = slots_of(tile_groups, count, weights.shape[2], group_count)
    for t, g, m in places:
        r, c = tile_coords[0, 0, 0, t], tile_coords[0, 0, 1, t]
        by_row, by_col = weighted_sums(jnp.abs(tiles[0, 0, t]), tile_gains[0, 0, t])
        row_degree[pl.ds(r, 1), :] += by_row
        payload[g, pl.ds(m, 1), :] = by_col
        payload[g, pl.ds(MOST + m, 1), :] = jnp.full((1, TILE), c, jnp.int32).astype(F32)


def halves_of(value):
    high = value.astype(BF16)
    return high, (value - high.astype(F32)).astype(BF16)


def add_by_place(places, values):
    shape = (BR, places.shape[1])
    chosen = (lax.broadcasted_iota(jnp.int32, shape, 0) == places).astype(BF16)
    high, low = halves_of(values)
    return times(chosen, high) + times(chosen, low)


def local_degree_kernel(
    weights, gains, coords, degree, ready, tiles, tile_gains, places, by_row, by_col, sems, small_sems
):
    count, held = weights.shape[2], ready.shape[0]

    def copy_of(n, base, target):
        source = weights.at[0, 0, pl.ds(base + n * CHUNK, CHUNK)]
        return pltpu.make_async_copy(
            source, target.at[pl.ds(n * CHUNK, CHUNK)], sems.at[base // CHUNK + n]
        )

    wait = fetch((gains, coords), (tile_gains, places), small_sems)
    parts = ((0, ready), (held, tiles))
    for base, target in parts:
        for n in range(target.shape[0] // CHUNK):
            copy_of(n, base, target).start()
    by_row[...] = jnp.zeros(by_row.shape, F32)
    first = lax.broadcasted_iota(jnp.int32, (8, TILE), 0) == 0
    lane = lax.broadcasted_iota(jnp.int32, by_row.shape, 1)
    wait()

    def step(base, target, n, _):
        copy_of(n, base, target).wait()
        for k in range(CHUNK):
            t = base + n * CHUNK + k
            size = jnp.abs(target[n * CHUNK + k])
            pair = jnp.abs(tile_gains[0, 0, t])
            left = jnp.where(first, pair[0:1, :], 0.0)
            high = left.astype(BF16).astype(F32)
            sums = times(jnp.concatenate([high, left - high], axis=0).astype(BF16), size)
            by_col[pl.ds(t, 1), :] = (sums[0:1] + sums[8:9]) * pair[1:2, :]
            sums = jnp.sum(size.astype(F32) * pair[1:2, :], axis=1, keepdims=True)
            by_row[...] = jnp.where(lane == t, sums, by_row[...])
        return 0

    for base, target in parts:
        lax.fori_loop(0, target.shape[0] // CHUNK, functools.partial(step, base, target), 0)
    row_sums = jnp.transpose(by_row[...])[:count] * jnp.abs(tile_gains[0, 0, :, 0, :])
    degree[...] = add_by_place(places[0, 0, 0:1, :], row_sums) + add_by_place(
        places[0, 0, 1:2, :], by_col[...]
    )


def scale_kernel(raw, gains, scaled):
    row_gain = jnp.transpose(gains[0, 0, :, 0, :])
    for k in range(raw.shape[2]):
        scaled[k] = (
            row_gain[:, k : k + 1] * raw[0, 0, k].astype(F32) * gains[0, 0, k, 1:2, :]
        ).astype(BF16)


def scale(weights, gains, name):
    count = weights.shape[2]
    return pl.pallas_call(
        scale_kernel,
        out_shape=shape((count, TILE, TILE), BF16),
        grid=(count // CHUNK,),
        in_specs=[
            pl.BlockSpec((1, 1, CHUNK, TILE, TILE), lambda n: (0, 0, n, 0, 0)),
            pl.BlockSpec((1, 1, CHUNK, 2, TILE), lambda n: (0, 0, n, 0, 0)),
        ],
        out_specs=pl.BlockSpec((CHUNK, TILE, TILE), lambda n: (n, 0, 0)),
        cost_estimate=pl.CostEstimate(
            flops=2 * count * TILE * TILE, bytes_accessed=4 * count * TILE * TILE, transcendentals=0
        ),
        compiler_params=pltpu.CompilerParams(vmem_limit_bytes=VMEM_LIMIT),
        name=name,
    )(in_hbm(weights), gains)


def join_degree_kernel(arrived, row_degree, local_degree, joined):
    total = row_degree[...] + local_degree[...]
    sub = lax.broadcasted_iota(jnp.int32, total.shape, 0).astype(F32)
    for g in range(arrived.shape[0]):
        block = arrived[g]
        for m in range(MOST):
            hit = sub == block[MOST + m : MOST + m + 1, :]
            total += jnp.where(hit, block[m : m + 1, :], 0.0)
    joined[...] = total


def by_chips(groups):
    return groups // 2 <= 4


def place_of(group, group_count, core):
    if not by_chips(group_count):
        return group
    return ((group + core) % 2) * (group_count // 2) + group // 2


def outgoing(x, scaled, groups, coords, targets, staged, count, gram=None):
    group_count = staged.shape[0]
    core = lax.axis_index("rows") % 2
    for g in range(group_count):
        staged[g, MOST : 2 * MOST] = jnp.zeros((MOST, WIDTH, TILE), BF16)
        if gram is not None:
            staged[g, 2 * MOST] = gram
    for t, g, m in slots_of(groups, count, scaled.shape[0], group_count):
        place = place_of(g, group_count, core)
        staged[place, MOST + m] = times(x[coords[0, 0, 0, t]], scaled[t]).astype(BF16)
    for g in range(group_count):
        place = place_of(g, group_count, core)
        for m in range(MOST):
            staged[place, m] = x[jnp.maximum(targets[g, m], 0)]


def split_out(staged, outs):
    size = outs[0].shape[0]
    for k, out in enumerate(outs):
        out[...] = staged[k * size : (k + 1) * size]


def forward_kernel(near, passed, *pieces):
    chips = near.shape[0]
    me = lax.axis_index("rows")
    chip, core = me // 2, me % 2
    for k, piece in enumerate(pieces):
        piece[core] = near[chip ^ k]
        piece[1 - core] = passed[chip ^ k]


def by_group(arrived, joined):
    if len(arrived) == 1:
        joined[...] = arrived[0][...]
        return
    chip = lax.axis_index("rows") // 2
    for k, piece in enumerate(arrived):
        joined[pl.ds((chip ^ k) * 2, 2)] = piece[...]


def first_block_kernel(splits, start, scaled, groups, coords, targets, *refs):
    parts, (inv_root, x, *refs) = refs[:splits], refs[splits:]
    *outs, tile_groups, tile_coords, tile_targets, count, sems, staged = refs
    routes = (tile_groups, tile_coords, tile_targets)
    wait = fetch((groups, coords, targets), routes, sems)
    degree = parts[0][...]
    for part in parts[1:]:
        degree += part[...]
    inv = 1.0 / jnp.sqrt(degree)
    inv_root[...] = inv
    for k in range(BR):
        x[k] = (start[:, k * TILE : (k + 1) * TILE] * inv[k : k + 1, :]).astype(BF16)
    wait()
    outgoing(x, scaled, *routes, staged, count)
    split_out(staged, outs)


def pair_sum_kernel(mine, theirs, total, sent):
    value = mine[...] + theirs[...].astype(F32)
    total[...] = value
    sent[...] = value.astype(BF16)


def next_block_kernel(
    vertices, scaled, inv_root, groups, coords, targets, mine, theirs, x, *refs
):
    *outs, tile_groups, tile_coords, tile_targets, count, sems, staged = refs
    routes = (tile_groups, tile_coords, tile_targets)
    wait = fetch((groups, coords, targets), routes, sems)
    gram = jnp.zeros((2 * WIDTH, 2 * WIDTH), F32)
    for k in range(BR):
        value = mine[k] + theirs[k].astype(F32)
        root = inv_root[k : k + 1, :]
        image = value * root
        x[k] = (image * root).astype(BF16)
        high = image.astype(BF16)
        halves = jnp.concatenate([high, (image - high.astype(F32)).astype(BF16)], axis=0)
        gram += times_t(halves, halves)
    low = gram[:WIDTH, WIDTH:] + gram[WIDTH:, :WIDTH] + gram[WIDTH:, WIDTH:]
    gram = (gram[:WIDTH, :WIDTH] + low) / vertices
    high = gram.astype(BF16)
    middle = (gram - high.astype(F32)).astype(BF16)
    low = (gram - high.astype(F32) - middle.astype(F32)).astype(BF16)
    block = jnp.concatenate(
        [high, middle, low, jnp.zeros((WIDTH, TILE - 3 * WIDTH), BF16)], axis=1
    )
    wait()
    outgoing(x, scaled, *routes, staged, count, block)
    split_out(staged, outs)


def local_products_kernel(
    x, ready, weights, gains, coords, partial, tiles, sems, tile_coords, coord_sems
):
    held, count, chunk = ready.shape[0], tiles.shape[0], CHUNK
    batch = 2 * chunk if count % (2 * chunk) == 0 else chunk

    def copy_of(n):
        source = weights.at[0, 0, pl.ds(held + n * chunk, chunk)]
        return pltpu.make_async_copy(source, tiles.at[pl.ds(n * chunk, chunk)], sems.at[n])

    wait = fetch((coords,), (tile_coords,), coord_sems)
    for n in range(count // chunk):
        copy_of(n).start()
    partial[...] = jnp.zeros(partial.shape, F32)
    wait()

    def add(base, raw):
        row_gains = [
            jnp.transpose(gains[0, 0, pl.ds(base + k, CHUNK), 0, :])
            for k in range(0, len(raw), CHUNK)
        ]
        places, results = [], []
        for k, tile in enumerate(raw):
            t = base + k
            r, c = tile_coords[0, 0, 0, t], tile_coords[0, 0, 1, t]
            row_gain = row_gains[k // CHUNK][:, k % CHUNK : k % CHUNK + 1]
            tile = (row_gain * tile().astype(F32) * gains[0, 0, t, 1:2, :]).astype(BF16)
            results.append((times_t(x[c], tile), times(x[r], tile)))
            places.append((r, c))
        for (r, c), (forward, backward) in zip(places, results):
            partial[r] += forward
            partial[c] += backward

    add(0, [lambda k=k: ready[k] for k in range(held)])

    def step(n, _):
        for k in range(batch // chunk):
            copy_of(n * (batch // chunk) + k).wait()
        add(held + n * batch, [lambda k=k: tiles[n * batch + k] for k in range(batch)])
        return 0

    lax.fori_loop(0, count // batch, step, 0)


def remote_products_kernel(splits, whole, pieces, scaled, partial, groups, coords, targets, *refs):
    arrived, refs = refs[:pieces], refs[pieces:]
    *outs, total, tile_groups, tile_coords, tile_targets, count, sems, joined = refs
    wait = fetch((groups, coords, targets), (tile_groups, tile_coords, tile_targets), sems)
    group_count = joined.shape[0]
    by_group(arrived, joined)
    total[...] = partial[...]
    wait()
    for t, g, m in slots_of(tile_groups, count, scaled.shape[0], group_count):
        total[tile_coords[0, 0, 0, t]] += times_t(joined[g, m], scaled[t])
    for g in range(group_count):
        for m in range(MOST):
            total[jnp.maximum(tile_targets[g, m], 0)] += joined[g, MOST + m].astype(F32)
    if whole:
        for out in outs:
            out[...] = total[...].astype(out.dtype)
        return
    me = lax.axis_index("cols")
    quarter = BR // splits
    for k, out in enumerate(outs):
        base = pl.multiple_of((me ^ k) * quarter, quarter)
        out[...] = total[pl.ds(base, quarter)].astype(out.dtype)


def quarter_sum(pieces, inv_root, me):
    quarter = pieces[0].shape[0]
    images, roots = [], []
    for k in range(quarter):
        value = pieces[0][k]
        for piece in pieces[1:]:
            value += piece[k].astype(F32)
        root = inv_root[pl.ds(me * quarter + k, 1), :]
        images.append(value * root)
        roots.append(root)
    return images, roots


def eliminate(gram, right):
    shape = (WIDTH, LANES)
    row = lax.broadcasted_iota(jnp.int32, shape, 0)
    lane = lax.broadcasted_iota(jnp.int32, shape, 1)
    gram = jnp.concatenate([gram, jnp.zeros((WIDTH, LANES - WIDTH), F32)], axis=1)
    for k in range(0, WIDTH, 2):
        first = jnp.broadcast_to(gram[:, k : k + 1], shape)
        second = jnp.broadcast_to(gram[:, k + 1 : k + 2], shape)
        factor = first / first[k : k + 1]
        second = second - factor * second[k : k + 1]
        then = jnp.where(row > k + 1, second / second[k + 1 : k + 2], 0.0)
        link = factor[k + 1 : k + 2]
        factor = jnp.where(row > k, factor, 0.0)

        def step(work):
            top = work[k : k + 1, :]
            return work - factor * top - then * (work[k + 1 : k + 2, :] - link * top)

        gram, right = step(gram), [step(block) for block in right]
    pivots = jnp.sum(jnp.where(row == lane, gram, 0.0), axis=1, keepdims=True)
    root = jnp.broadcast_to(1.0 / jnp.sqrt(pivots), shape)
    return [block * root for block in right]


def middle_factor_kernel(*refs):
    *arrived, inverse = refs
    gram = jnp.zeros((WIDTH, WIDTH), F32)
    for block in [piece[g, 2 * MOST] for piece in arrived for g in range(piece.shape[0])]:
        block = block.astype(F32)
        gram += (block[:, 2 * WIDTH : 3 * WIDTH] + block[:, WIDTH : 2 * WIDTH]) + block[:, :WIDTH]
    eye = lax.broadcasted_iota(jnp.int32, (WIDTH, LANES), 0) == lax.broadcasted_iota(
        jnp.int32, (WIDTH, LANES), 1
    )
    (result,) = eliminate(gram, [eye.astype(F32)])
    inverse[...] = result[:, :WIDTH]


def last_quarter_kernel(splits, vertices, inv_root, inverse, *refs):
    pieces, (image_out, grams) = refs[:splits], refs[splits:]
    images, _ = quarter_sum(pieces, inv_root, lax.axis_index("cols"))
    first = inverse[...]
    gram = jnp.zeros((WIDTH, WIDTH), F32)
    for k, image in enumerate(images):
        value = jnp.dot(first, image, precision=HIGHEST, preferred_element_type=F32)
        image_out[:, k * TILE : (k + 1) * TILE] = value
        gram += lax.dot_general(
            value, value, (((1,), (1,)), ((), ())), precision=HIGHEST, preferred_element_type=F32
        )
    gram = gram / vertices
    block = jnp.concatenate(
        [gram[4 * n : 4 * n + 4] for n in range(4)] + [jnp.zeros((4, LANES - 4 * WIDTH), F32)], axis=1
    )
    for n in range(grams.shape[0]):
        grams[n] = block


def finish_kernel(grams, image, out):
    block = grams[0]
    for n in range(1, grams.shape[0]):
        block = block + grams[n]
    gram = jnp.concatenate([block[:, WIDTH * n : WIDTH * (n + 1)] for n in range(4)], axis=0)
    starts = range(0, out.shape[1], LANES)
    for n, block in zip(starts, eliminate(gram, [image[:, n : n + LANES] for n in starts])):
        out[:, n : n + LANES] = block


def per_device(
    local_weights,
    local_gains,
    local_coords,
    remote_weights,
    remote_gains,
    remote_groups,
    remote_coords,
    start_block,
):
    groups = lax.axis_size("rows")
    splits = lax.axis_size("cols")
    vertices = groups * BR * TILE
    quarter = BR // splits
    local_coords, remote_coords = jnp.swapaxes(local_coords, 2, 3), jnp.swapaxes(remote_coords, 2, 3)
    local_tiles, remote_tiles = local_weights.shape[2], remote_weights.shape[2]
    count = pltpu.SMEM((groups,), jnp.int32)
    routes = [
        pltpu.SMEM(remote_groups.shape, jnp.int32),
        pltpu.SMEM(remote_coords.shape, jnp.int32),
        pltpu.SMEM((groups, MOST), jnp.int32),
        count,
        pltpu.SemaphoreType.DMA((3,)),
    ]

    partners = [2 * 2**k - 1 for k in range(splits.bit_length() - 1)]

    def swap(value, k):
        return lax.ppermute(value, "cols", [(j, j ^ k) for j in range(splits)])

    def trade(value):
        return lax.all_to_all(value, "rows", split_axis=0, concat_axis=0, tiled=True)

    listing = (remote_weights, remote_gains, remote_groups, remote_coords)
    sums, row_degree = call(
        functools.partial(remote_degree_kernel, groups),
        (shape((groups, 8, TILE)), shape((BR, TILE))),
        [hbm, hbm, hbm, hbm],
        [
            pltpu.VMEM(remote_weights.shape, BF16),
            pltpu.VMEM(remote_gains.shape, F32),
            pltpu.SMEM(remote_groups.shape, jnp.int32),
            pltpu.SMEM(remote_coords.shape, jnp.int32),
            count,
            pltpu.SemaphoreType.DMA((4,)),
        ],
        name="remote_degree",
    )(*[in_hbm(value) for value in listing])
    sums_in = trade(sums)
    local_degree, ready = call(
        local_degree_kernel,
        (shape((BR, TILE)), shape((HELD, TILE, TILE), BF16)),
        [hbm, hbm, hbm],
        [
            pltpu.VMEM((local_tiles - HELD, TILE, TILE), BF16),
            pltpu.VMEM(local_gains.shape, F32),
            pltpu.VMEM(local_coords.shape, jnp.int32),
            pltpu.VMEM((TILE, -(-local_tiles // LANES) * LANES), F32),
            pltpu.VMEM((local_tiles, TILE), F32),
            pltpu.SemaphoreType.DMA((local_tiles // CHUNK,)),
            pltpu.SemaphoreType.DMA((2,)),
        ],
        moved=10**7,
        name="local_degree",
    )(*[in_hbm(value) for value in (local_weights, local_gains, local_coords)])
    targets = sums_in[:, MOST : 2 * MOST, 0].astype(jnp.int32)
    joined = call(
        join_degree_kernel, shape((BR, TILE)), [vmem, vmem, vmem], name="join_degree"
    )(sums_in, row_degree, local_degree)
    joined, remote_gains = lax.optimization_barrier((joined, remote_gains))
    degrees = [joined] + [swap(joined, k) for k in range(1, splits)]
    remote_scaled = scale(remote_weights, remote_gains, "remote_scale")
    def sent_blocks(blocks):
        if by_chips(groups):
            return (shape((groups // 2, blocks, WIDTH, TILE), BF16),) * 2
        return (shape((groups, blocks, WIDTH, TILE), BF16),)

    def staging(blocks):
        return pltpu.VMEM((groups, blocks, WIDTH, TILE), BF16)

    inv_root, x, *sent = call(
        functools.partial(first_block_kernel, splits),
        (shape((BR, TILE)), shape((BR, WIDTH, TILE), BF16)) + sent_blocks(2 * MOST),
        [vmem, vmem, anywhere, anywhere, anywhere] + [vmem] * splits,
        routes + [staging(2 * MOST)],
        name="first_block",
    )(start_block, remote_scaled, remote_groups, remote_coords, targets, *degrees)

    def local_products(x):
        return call(
            local_products_kernel,
            shape((BR, WIDTH, TILE)),
            [vmem, vmem, hbm, vmem, anywhere],
            [
                pltpu.VMEM((local_tiles - HELD, TILE, TILE), BF16),
                pltpu.SemaphoreType.DMA((local_tiles // CHUNK - HELD // CHUNK,)),
                pltpu.SMEM(local_coords.shape, jnp.int32),
                pltpu.SemaphoreType.DMA((1,)),
            ],
            flops=4 * local_tiles * TILE * TILE * WIDTH,
            moved=2 * local_tiles * TILE * TILE,
            name="local_products",
        )(x, ready, local_weights, local_gains, local_coords)

    def product(x, sent, out_shape, whole):
        blocks = sent[0].shape[1]
        if by_chips(groups):
            near, far = sent
            passed = lax.ppermute(far, "rows", [(j, j ^ 1) for j in range(groups)])
            own, *others = call(
                forward_kernel,
                (shape((2, blocks, WIDTH, TILE), BF16),) * (groups // 2),
                [vmem, vmem],
                name="forward",
            )(near, passed)
            arrived = [own] + [
                lax.ppermute(piece, "rows", [(j, j ^ (2 * k)) for j in range(groups)])
                for k, piece in enumerate(others, 1)
            ]
            partial = local_products(x)
        else:
            arrived = [trade(sent[0])]
            partial = local_products(x)
        return arrived, call(
            functools.partial(remote_products_kernel, splits, whole, len(arrived)),
            out_shape,
            [vmem, vmem, anywhere, anywhere, anywhere] + [vmem] * len(arrived),
            [pltpu.VMEM((BR, WIDTH, TILE), F32)] + routes + [staging(blocks)],
            name="remote_products",
        )(remote_scaled, partial, remote_groups, remote_coords, targets, *arrived)

    _, (own, sent) = product(
        x, sent, (shape((BR, WIDTH, TILE)), shape((BR, WIDTH, TILE), BF16)), True
    )
    for k in partners[:-1]:
        own, sent = call(
            pair_sum_kernel,
            (shape((BR, WIDTH, TILE)), shape((BR, WIDTH, TILE), BF16)),
            [vmem, vmem],
            name="pair_sum",
        )(own, swap(sent, k))
    x, *sent = call(
        functools.partial(next_block_kernel, vertices),
        (shape((BR, WIDTH, TILE), BF16),) + sent_blocks(2 * MOST + 1),
        [vmem, vmem, anywhere, anywhere, anywhere, vmem, vmem],
        routes + [staging(2 * MOST + 1)],
        name="next_block",
    )(
        remote_scaled,
        inv_root,
        remote_groups,
        remote_coords,
        targets,
        own,
        swap(sent, partners[-1]),
    )
    arrived, sent = product(
        x,
        sent,
        tuple(shape((quarter, WIDTH, TILE), BF16 if k else F32) for k in range(splits)),
        False,
    )
    pieces = [sent[0]] + [swap(sent[k], k) for k in range(1, splits)]
    inverse = call(
        middle_factor_kernel,
        shape((WIDTH, WIDTH)),
        [vmem] * len(arrived),
        name="middle_factor",
    )(*arrived)
    image, grams = call(
        functools.partial(last_quarter_kernel, splits, vertices),
        (shape((WIDTH, quarter * TILE)), shape((groups * splits, 4, LANES))),
        [vmem] * (2 + splits),
        name="last_quarter",
    )(inv_root, inverse, *pieces)
    grams = lax.all_to_all(
        grams, ("rows", "cols"), split_axis=0, concat_axis=0, tiled=True
    )
    return call(finish_kernel, shape((WIDTH, quarter * TILE)), [vmem, vmem], name="finish")(
        grams, image
    )


def solution(mesh):
    in_specs = (
        P("rows", "cols", None, None, None),
        P("rows", "cols", None, None, None),
        P("rows", "cols", None, None),
        P("rows", "cols", None, None, None),
        P("rows", "cols", None, None, None),
        P("rows", "cols", None),
        P("rows", "cols", None, None),
        P(None, "rows"),
    )
    out_specs = P(None, ("rows", "cols"))
    return jax.shard_map(
        per_device, mesh=mesh, in_specs=in_specs, out_specs=out_specs, check_vma=False
    )
```

```python
import functools

import jax
import jax.numpy as jnp
from jax import lax
from jax.experimental import pallas as pl
from jax.experimental.pallas import tpu as pltpu
from jax.sharding import PartitionSpec as P

TILE = 256
WIDTH = 16
BR = 16
MOST = 2
CHUNK = 8
HELD = 16
LANES = 128
F32 = jnp.float32
BF16 = jnp.bfloat16
HIGHEST = lax.Precision.HIGHEST
VMEM_LIMIT = 48 * 1024 * 1024

vmem = pl.BlockSpec(memory_space=pltpu.VMEM)
hbm = pl.BlockSpec(memory_space=pltpu.HBM)
anywhere = pl.BlockSpec(memory_space=pl.ANY)


def shape(dims, dtype=F32):
    return jax.ShapeDtypeStruct(dims, dtype)


def call(kernel, out_shape, in_specs, scratch_shapes=(), flops=10**6, moved=10**6, name=None):
    return pl.pallas_call(
        kernel,
        out_shape=out_shape,
        in_specs=in_specs,
        out_specs=jax.tree.map(lambda _: vmem, out_shape),
        scratch_shapes=scratch_shapes,
        cost_estimate=pl.CostEstimate(flops=flops, bytes_accessed=moved, transcendentals=0),
        compiler_params=pltpu.CompilerParams(vmem_limit_bytes=VMEM_LIMIT),
        name=name,
    )


def times(left, right):
    return lax.dot_general(left, right, (((1,), (0,)), ((), ())), preferred_element_type=F32)


def times_t(left, right):
    return lax.dot_general(left, right, (((1,), (1,)), ((), ())), preferred_element_type=F32)


def in_hbm(value):
    return pltpu.with_memory_space_constraint(value, pltpu.HBM)


def fetch(sources, targets, sems):
    copies = [
        pltpu.make_async_copy(source, target, sems.at[n])
        for n, (source, target) in enumerate(zip(sources, targets))
    ]
    for copy in copies:
        copy.start()

    def wait():
        for copy in copies:
            copy.wait()

    return wait


def slots_of(groups_ref, count_ref, tile_count, group_count):
    for g in range(group_count):
        count_ref[g] = 0
    for t in range(tile_count):
        g = groups_ref[0, 0, t]
        m = count_ref[g]
        count_ref[g] = m + 1
        yield t, g, m


def weighted_sums(size, gains):
    sub = lax.broadcasted_iota(jnp.int32, (8, TILE), 0)
    gains = jnp.abs(gains)
    left = jnp.where(sub == 0, gains[0:1, :], jnp.where(sub == 1, gains[1:2, :], 0.0))
    high = left.astype(BF16).astype(F32)
    halves = jnp.concatenate([high, left - high], axis=0).astype(BF16)
    rows, cols = times_t(halves, size), times(halves, size)
    return (rows[1:2] + rows[9:10]) * gains[0:1, :], (cols[0:1] + cols[8:9]) * gains[1:2, :]


def remote_degree_kernel(
    group_count,
    weights,
    gains,
    groups,
    coords,
    payload,
    row_degree,
    tiles,
    tile_gains,
    tile_groups,
    tile_coords,
    count,
    sems,
):
    wait = fetch(
        (groups, coords, gains, weights), (tile_groups, tile_coords, tile_gains, tiles), sems
    )
    sub = lax.broadcasted_iota(jnp.int32, (8, TILE), 0)
    blank = jnp.where((sub >= MOST) & (sub < 2 * MOST), -1.0, 0.0).astype(F32)
    for g in range(group_count):
        payload[g] = blank
    row_degree[...] = jnp.zeros(row_degree.shape, F32)
    wait()
    places = slots_of(tile_groups, count, weights.shape[2], group_count)
    for t, g, m in places:
        r, c = tile_coords[0, 0, 0, t], tile_coords[0, 0, 1, t]
        by_row, by_col = weighted_sums(jnp.abs(tiles[0, 0, t]), tile_gains[0, 0, t])
        row_degree[pl.ds(r, 1), :] += by_row
        payload[g, pl.ds(m, 1), :] = by_col
        payload[g, pl.ds(MOST + m, 1), :] = jnp.full((1, TILE), c, jnp.int32).astype(F32)


def halves_of(value):
    high = value.astype(BF16)
    return high, (value - high.astype(F32)).astype(BF16)


def add_by_place(places, values):
    shape = (BR, places.shape[1])
    chosen = (lax.broadcasted_iota(jnp.int32, shape, 0) == places).astype(BF16)
    high, low = halves_of(values)
    return times(chosen, high) + times(chosen, low)


def local_degree_kernel(
    weights, gains, coords, degree, ready, tiles, tile_gains, places, by_row, by_col, sems, small_sems
):
    count, held = weights.shape[2], ready.shape[0]

    def copy_of(n, base, target):
        source = weights.at[0, 0, pl.ds(base + n * CHUNK, CHUNK)]
        return pltpu.make_async_copy(
            source, target.at[pl.ds(n * CHUNK, CHUNK)], sems.at[base // CHUNK + n]
        )

    wait = fetch((gains, coords), (tile_gains, places), small_sems)
    parts = ((0, ready), (held, tiles))
    for base, target in parts:
        for n in range(target.shape[0] // CHUNK):
            copy_of(n, base, target).start()
    by_row[...] = jnp.zeros(by_row.shape, F32)
    first = lax.broadcasted_iota(jnp.int32, (8, TILE), 0) == 0
    lane = lax.broadcasted_iota(jnp.int32, by_row.shape, 1)
    wait()

    def step(base, target, n, _):
        copy_of(n, base, target).wait()
        for k in range(CHUNK):
            t = base + n * CHUNK + k
            size = jnp.abs(target[n * CHUNK + k])
            pair = jnp.abs(tile_gains[0, 0, t])
            left = jnp.where(first, pair[0:1, :], 0.0)
            high = left.astype(BF16).astype(F32)
            sums = times(jnp.concatenate([high, left - high], axis=0).astype(BF16), size)
            by_col[pl.ds(t, 1), :] = (sums[0:1] + sums[8:9]) * pair[1:2, :]
            sums = jnp.sum(size.astype(F32) * pair[1:2, :], axis=1, keepdims=True)
            by_row[...] = jnp.where(lane == t, sums, by_row[...])
        return 0

    for base, target in parts:
        lax.fori_loop(0, target.shape[0] // CHUNK, functools.partial(step, base, target), 0)
    row_sums = jnp.transpose(by_row[...])[:count] * jnp.abs(tile_gains[0, 0, :, 0, :])
    degree[...] = add_by_place(places[0, 0, 0:1, :], row_sums) + add_by_place(
        places[0, 0, 1:2, :], by_col[...]
    )


def scale_kernel(raw, gains, scaled):
    row_gain = jnp.transpose(gains[0, 0, :, 0, :])
    for k in range(raw.shape[2]):
        scaled[k] = (
            row_gain[:, k : k + 1] * raw[0, 0, k].astype(F32) * gains[0, 0, k, 1:2, :]
        ).astype(BF16)


def scale(weights, gains, name):
    count = weights.shape[2]
    return pl.pallas_call(
        scale_kernel,
        out_shape=shape((count, TILE, TILE), BF16),
        grid=(count // CHUNK,),
        in_specs=[
            pl.BlockSpec((1, 1, CHUNK, TILE, TILE), lambda n: (0, 0, n, 0, 0)),
            pl.BlockSpec((1, 1, CHUNK, 2, TILE), lambda n: (0, 0, n, 0, 0)),
        ],
        out_specs=pl.BlockSpec((CHUNK, TILE, TILE), lambda n: (n, 0, 0)),
        cost_estimate=pl.CostEstimate(
            flops=2 * count * TILE * TILE, bytes_accessed=4 * count * TILE * TILE, transcendentals=0
        ),
        compiler_params=pltpu.CompilerParams(vmem_limit_bytes=VMEM_LIMIT),
        name=name,
    )(in_hbm(weights), gains)


def join_degree_kernel(arrived, row_degree, local_degree, joined):
    total = row_degree[...] + local_degree[...]
    sub = lax.broadcasted_iota(jnp.int32, total.shape, 0).astype(F32)
    for g in range(arrived.shape[0]):
        block = arrived[g]
        for m in range(MOST):
            hit = sub == block[MOST + m : MOST + m + 1, :]
            total += jnp.where(hit, block[m : m + 1, :], 0.0)
    joined[...] = total


def by_chips(groups):
    return groups // 2 <= 4


def place_of(group, group_count, core):
    if not by_chips(group_count):
        return group
    return ((group + core) % 2) * (group_count // 2) + group // 2


def outgoing(x, scaled, groups, coords, targets, staged, count, gram=None):
    group_count = staged.shape[0]
    core = lax.axis_index("rows") % 2
    for g in range(group_count):
        staged[g, MOST : 2 * MOST] = jnp.zeros((MOST, WIDTH, TILE), BF16)
        if gram is not None:
            staged[g, 2 * MOST] = gram
    for t, g, m in slots_of(groups, count, scaled.shape[0], group_count):
        place = place_of(g, group_count, core)
        staged[place, MOST + m] = times(x[coords[0, 0, 0, t]], scaled[t]).astype(BF16)
    for g in range(group_count):
        place = place_of(g, group_count, core)
        for m in range(MOST):
            staged[place, m] = x[jnp.maximum(targets[g, m], 0)]


def split_out(staged, outs):
    size = outs[0].shape[0]
    for k, out in enumerate(outs):
        out[...] = staged[k * size : (k + 1) * size]


def forward_kernel(near, passed, *pieces):
    chips = near.shape[0]
    me = lax.axis_index("rows")
    chip, core = me // 2, me % 2
    for k, piece in enumerate(pieces):
        piece[core] = near[chip ^ k]
        piece[1 - core] = passed[chip ^ k]


def by_group(arrived, joined):
    if len(arrived) == 1:
        joined[...] = arrived[0][...]
        return
    chip = lax.axis_index("rows") // 2
    for k, piece in enumerate(arrived):
        joined[pl.ds((chip ^ k) * 2, 2)] = piece[...]


def first_block_kernel(splits, start, scaled, groups, coords, targets, *refs):
    parts, (inv_root, x, *refs) = refs[:splits], refs[splits:]
    *outs, count, staged = refs
    routes = (groups, coords, targets)
    degree = parts[0][...]
    for part in parts[1:]:
        degree += part[...]
    inv = 1.0 / jnp.sqrt(degree)
    inv_root[...] = inv
    for k in range(BR):
        x[k] = (start[:, k * TILE : (k + 1) * TILE] * inv[k : k + 1, :]).astype(BF16)
    outgoing(x, scaled, *routes, staged, count)
    split_out(staged, outs)


def pair_sum_kernel(mine, theirs, total, sent):
    value = mine[...] + theirs[...].astype(F32)
    total[...] = value
    sent[...] = value.astype(BF16)


def next_block_kernel(
    vertices, scaled, inv_root, groups, coords, targets, mine, theirs, x, *refs
):
    *outs, count, staged = refs
    routes = (groups, coords, targets)
    gram = jnp.zeros((2 * WIDTH, 2 * WIDTH), F32)
    for k in range(BR):
        value = mine[k] + theirs[k].astype(F32)
        root = inv_root[k : k + 1, :]
        image = value * root
        x[k] = (image * root).astype(BF16)
        high = image.astype(BF16)
        halves = jnp.concatenate([high, (image - high.astype(F32)).astype(BF16)], axis=0)
        gram += times_t(halves, halves)
    low = gram[:WIDTH, WIDTH:] + gram[WIDTH:, :WIDTH] + gram[WIDTH:, WIDTH:]
    gram = (gram[:WIDTH, :WIDTH] + low) / vertices
    high = gram.astype(BF16)
    middle = (gram - high.astype(F32)).astype(BF16)
    low = (gram - high.astype(F32) - middle.astype(F32)).astype(BF16)
    block = jnp.concatenate(
        [high, middle, low, jnp.zeros((WIDTH, TILE - 3 * WIDTH), BF16)], axis=1
    )
    outgoing(x, scaled, *routes, staged, count, block)
    split_out(staged, outs)


def local_products_kernel(
    x, ready, weights, gains, coords, partial, tiles, sems, tile_coords, coord_sems
):
    held, count, chunk = ready.shape[0], tiles.shape[0], CHUNK
    batch = 2 * chunk if count % (2 * chunk) == 0 else chunk

    def copy_of(n):
        source = weights.at[0, 0, pl.ds(held + n * chunk, chunk)]
        return pltpu.make_async_copy(source, tiles.at[pl.ds(n * chunk, chunk)], sems.at[n])

    wait = fetch((coords,), (tile_coords,), coord_sems)
    for n in range(count // chunk):
        copy_of(n).start()
    partial[...] = jnp.zeros(partial.shape, F32)
    wait()

    def add(base, raw):
        row_gains = [
            jnp.transpose(gains[0, 0, pl.ds(base + k, CHUNK), 0, :])
            for k in range(0, len(raw), CHUNK)
        ]
        places, results = [], []
        for k, tile in enumerate(raw):
            t = base + k
            r, c = tile_coords[0, 0, 0, t], tile_coords[0, 0, 1, t]
            row_gain = row_gains[k // CHUNK][:, k % CHUNK : k % CHUNK + 1]
            tile = (row_gain * tile().astype(F32) * gains[0, 0, t, 1:2, :]).astype(BF16)
            results.append((times_t(x[c], tile), times(x[r], tile)))
            places.append((r, c))
        for (r, c), (forward, backward) in zip(places, results):
            partial[r] += forward
            partial[c] += backward

    add(0, [lambda k=k: ready[k] for k in range(held)])

    def step(n, _):
        for k in range(batch // chunk):
            copy_of(n * (batch // chunk) + k).wait()
        add(held + n * batch, [lambda k=k: tiles[n * batch + k] for k in range(batch)])
        return 0

    lax.fori_loop(0, count // batch, step, 0)


def remote_products_kernel(splits, whole, pieces, scaled, partial, groups, coords, targets, *refs):
    arrived, refs = refs[:pieces], refs[pieces:]
    *outs, total, count, joined = refs
    group_count = joined.shape[0]
    by_group(arrived, joined)
    total[...] = partial[...]
    for t, g, m in slots_of(groups, count, scaled.shape[0], group_count):
        total[coords[0, 0, 0, t]] += times_t(joined[g, m], scaled[t])
    for g in range(group_count):
        for m in range(MOST):
            total[jnp.maximum(targets[g, m], 0)] += joined[g, MOST + m].astype(F32)
    if whole:
        for out in outs:
            out[...] = total[...].astype(out.dtype)
        return
    me = lax.axis_index("cols")
    quarter = BR // splits
    for k, out in enumerate(outs):
        base = pl.multiple_of((me ^ k) * quarter, quarter)
        out[...] = total[pl.ds(base, quarter)].astype(out.dtype)


def quarter_sum(pieces, inv_root, me):
    quarter = pieces[0].shape[0]
    images, roots = [], []
    for k in range(quarter):
        value = pieces[0][k]
        for piece in pieces[1:]:
            value += piece[k].astype(F32)
        root = inv_root[pl.ds(me * quarter + k, 1), :]
        images.append(value * root)
        roots.append(root)
    return images, roots


def eliminate(gram, right):
    shape = (WIDTH, LANES)
    row = lax.broadcasted_iota(jnp.int32, shape, 0)
    lane = lax.broadcasted_iota(jnp.int32, shape, 1)
    gram = jnp.concatenate([gram, jnp.zeros((WIDTH, LANES - WIDTH), F32)], axis=1)
    for k in range(0, WIDTH, 2):
        first = jnp.broadcast_to(gram[:, k : k + 1], shape)
        second = jnp.broadcast_to(gram[:, k + 1 : k + 2], shape)
        factor = first / first[k : k + 1]
        second = second - factor * second[k : k + 1]
        then = jnp.where(row > k + 1, second / second[k + 1 : k + 2], 0.0)
        link = factor[k + 1 : k + 2]
        factor = jnp.where(row > k, factor, 0.0)

        def step(work):
            top = work[k : k + 1, :]
            return work - factor * top - then * (work[k + 1 : k + 2, :] - link * top)

        gram, right = step(gram), [step(block) for block in right]
    pivots = jnp.sum(jnp.where(row == lane, gram, 0.0), axis=1, keepdims=True)
    root = jnp.broadcast_to(1.0 / jnp.sqrt(pivots), shape)
    return [block * root for block in right]


def middle_factor_kernel(*refs):
    *arrived, inverse = refs
    gram = jnp.zeros((WIDTH, WIDTH), F32)
    for block in [piece[g, 2 * MOST] for piece in arrived for g in range(piece.shape[0])]:
        block = block.astype(F32)
        gram += (block[:, 2 * WIDTH : 3 * WIDTH] + block[:, WIDTH : 2 * WIDTH]) + block[:, :WIDTH]
    eye = lax.broadcasted_iota(jnp.int32, (WIDTH, LANES), 0) == lax.broadcasted_iota(
        jnp.int32, (WIDTH, LANES), 1
    )
    (result,) = eliminate(gram, [eye.astype(F32)])
    inverse[...] = result[:, :WIDTH]


def last_quarter_kernel(splits, vertices, inv_root, inverse, *refs):
    pieces, (image_out, grams) = refs[:splits], refs[splits:]
    images, _ = quarter_sum(pieces, inv_root, lax.axis_index("cols"))
    first = inverse[...]
    gram = jnp.zeros((WIDTH, WIDTH), F32)
    for k, image in enumerate(images):
        value = jnp.dot(first, image, precision=HIGHEST, preferred_element_type=F32)
        image_out[:, k * TILE : (k + 1) * TILE] = value
        gram += lax.dot_general(
            value, value, (((1,), (1,)), ((), ())), precision=HIGHEST, preferred_element_type=F32
        )
    gram = gram / vertices
    block = jnp.concatenate(
        [gram[4 * n : 4 * n + 4] for n in range(4)] + [jnp.zeros((4, LANES - 4 * WIDTH), F32)], axis=1
    )
    for n in range(grams.shape[0]):
        grams[n] = block


def finish_kernel(grams, image, out):
    block = grams[0]
    for n in range(1, grams.shape[0]):
        block = block + grams[n]
    gram = jnp.concatenate([block[:, WIDTH * n : WIDTH * (n + 1)] for n in range(4)], axis=0)
    starts = range(0, out.shape[1], LANES)
    for n, block in zip(starts, eliminate(gram, [image[:, n : n + LANES] for n in starts])):
        out[:, n : n + LANES] = block


def per_device(
    local_weights,
    local_gains,
    local_coords,
    remote_weights,
    remote_gains,
    remote_groups,
    remote_coords,
    start_block,
):
    groups = lax.axis_size("rows")
    splits = lax.axis_size("cols")
    vertices = groups * BR * TILE
    quarter = BR // splits
    local_coords, remote_coords = jnp.swapaxes(local_coords, 2, 3), jnp.swapaxes(remote_coords, 2, 3)
    local_tiles, remote_tiles = local_weights.shape[2], remote_weights.shape[2]
    count = pltpu.SMEM((groups,), jnp.int32)

    partners = [2 * 2**k - 1 for k in range(splits.bit_length() - 1)]

    def swap(value, k):
        return lax.ppermute(value, "cols", [(j, j ^ k) for j in range(splits)])

    def trade(value):
        return lax.all_to_all(value, "rows", split_axis=0, concat_axis=0, tiled=True)

    listing = (remote_weights, remote_gains, remote_groups, remote_coords)
    sums, row_degree = call(
        functools.partial(remote_degree_kernel, groups),
        (shape((groups, 8, TILE)), shape((BR, TILE))),
        [hbm, hbm, hbm, hbm],
        [
            pltpu.VMEM(remote_weights.shape, BF16),
            pltpu.VMEM(remote_gains.shape, F32),
            pltpu.SMEM(remote_groups.shape, jnp.int32),
            pltpu.SMEM(remote_coords.shape, jnp.int32),
            count,
            pltpu.SemaphoreType.DMA((4,)),
        ],
        name="remote_degree",
    )(*[in_hbm(value) for value in listing])
    sums_in = trade(sums)
    local_degree, ready = call(
        local_degree_kernel,
        (shape((BR, TILE)), shape((HELD, TILE, TILE), BF16)),
        [hbm, hbm, hbm],
        [
            pltpu.VMEM((local_tiles - HELD, TILE, TILE), BF16),
            pltpu.VMEM(local_gains.shape, F32),
            pltpu.VMEM(local_coords.shape, jnp.int32),
            pltpu.VMEM((TILE, -(-local_tiles // LANES) * LANES), F32),
            pltpu.VMEM((local_tiles, TILE), F32),
            pltpu.SemaphoreType.DMA((local_tiles // CHUNK,)),
            pltpu.SemaphoreType.DMA((2,)),
        ],
        moved=10**7,
        name="local_degree",
    )(*[in_hbm(value) for value in (local_weights, local_gains, local_coords)])
    targets = sums_in[:, MOST : 2 * MOST, 0].astype(jnp.int32)
    far_scalars = [remote_groups, remote_coords, targets]
    joined = call(
        join_degree_kernel, shape((BR, TILE)), [vmem, vmem, vmem], name="join_degree"
    )(sums_in, row_degree, local_degree)
    joined, remote_gains = lax.optimization_barrier((joined, remote_gains))
    degrees = [joined] + [swap(joined, k) for k in range(1, splits)]
    remote_scaled = scale(remote_weights, remote_gains, "remote_scale")
    def sent_blocks(blocks):
        if by_chips(groups):
            return (shape((groups // 2, blocks, WIDTH, TILE), BF16),) * 2
        return (shape((groups, blocks, WIDTH, TILE), BF16),)

    def staging(blocks):
        return pltpu.VMEM((groups, blocks, WIDTH, TILE), BF16)

    inv_root, x, *sent = call(
        functools.partial(first_block_kernel, splits),
        (shape((BR, TILE)), shape((BR, WIDTH, TILE), BF16)) + sent_blocks(2 * MOST),
        [vmem, vmem, vmem, vmem, vmem] + [vmem] * splits,
        [count, staging(2 * MOST)],
        name="first_block",
    )(start_block, remote_scaled, *far_scalars, *degrees)

    def local_products(x):
        return call(
            local_products_kernel,
            shape((BR, WIDTH, TILE)),
            [vmem, vmem, hbm, vmem, anywhere],
            [
                pltpu.VMEM((local_tiles - HELD, TILE, TILE), BF16),
                pltpu.SemaphoreType.DMA((local_tiles // CHUNK - HELD // CHUNK,)),
                pltpu.SMEM(local_coords.shape, jnp.int32),
                pltpu.SemaphoreType.DMA((1,)),
            ],
            flops=4 * local_tiles * TILE * TILE * WIDTH,
            moved=2 * local_tiles * TILE * TILE,
            name="local_products",
        )(x, ready, local_weights, local_gains, local_coords)

    def product(x, sent, out_shape, whole):
        blocks = sent[0].shape[1]
        if by_chips(groups):
            near, far = sent
            passed = lax.ppermute(far, "rows", [(j, j ^ 1) for j in range(groups)])
            own, *others = call(
                forward_kernel,
                (shape((2, blocks, WIDTH, TILE), BF16),) * (groups // 2),
                [vmem, vmem],
                name="forward",
            )(near, passed)
            arrived = [own] + [
                lax.ppermute(piece, "rows", [(j, j ^ (2 * k)) for j in range(groups)])
                for k, piece in enumerate(others, 1)
            ]
            partial = local_products(x)
        else:
            arrived = [trade(sent[0])]
            partial = local_products(x)
        return arrived, call(
            functools.partial(remote_products_kernel, splits, whole, len(arrived)),
            out_shape,
            [vmem, vmem, vmem, vmem, vmem] + [vmem] * len(arrived),
            [pltpu.VMEM((BR, WIDTH, TILE), F32), count, staging(blocks)],
            name="remote_products",
        )(remote_scaled, partial, *far_scalars, *arrived)

    _, (own, sent) = product(
        x, sent, (shape((BR, WIDTH, TILE)), shape((BR, WIDTH, TILE), BF16)), True
    )
    for k in partners[:-1]:
        own, sent = call(
            pair_sum_kernel,
            (shape((BR, WIDTH, TILE)), shape((BR, WIDTH, TILE), BF16)),
            [vmem, vmem],
            name="pair_sum",
        )(own, swap(sent, k))
    x, *sent = call(
        functools.partial(next_block_kernel, vertices),
        (shape((BR, WIDTH, TILE), BF16),) + sent_blocks(2 * MOST + 1),
        [vmem, vmem, vmem, vmem, vmem, vmem, vmem],
        [count, staging(2 * MOST + 1)],
        name="next_block",
    )(
        remote_scaled,
        inv_root,
        *far_scalars,
        own,
        swap(sent, partners[-1]),
    )
    arrived, sent = product(
        x,
        sent,
        tuple(shape((quarter, WIDTH, TILE), BF16 if k else F32) for k in range(splits)),
        False,
    )
    pieces = [sent[0]] + [swap(sent[k], k) for k in range(1, splits)]
    inverse = call(
        middle_factor_kernel,
        shape((WIDTH, WIDTH)),
        [vmem] * len(arrived),
        name="middle_factor",
    )(*arrived)
    image, grams = call(
        functools.partial(last_quarter_kernel, splits, vertices),
        (shape((WIDTH, quarter * TILE)), shape((groups * splits, 4, LANES))),
        [vmem] * (2 + splits),
        name="last_quarter",
    )(inv_root, inverse, *pieces)
    grams = lax.all_to_all(
        grams, ("rows", "cols"), split_axis=0, concat_axis=0, tiled=True
    )
    return call(finish_kernel, shape((WIDTH, quarter * TILE)), [vmem, vmem], name="finish")(
        grams, image
    )


def solution(mesh):
    in_specs = (
        P("rows", "cols", None, None, None),
        P("rows", "cols", None, None, None),
        P("rows", "cols", None, None),
        P("rows", "cols", None, None, None),
        P("rows", "cols", None, None, None),
        P("rows", "cols", None),
        P("rows", "cols", None, None),
        P(None, "rows"),
    )
    out_specs = P(None, ("rows", "cols"))
    return jax.shard_map(
        per_device, mesh=mesh, in_specs=in_specs, out_specs=out_specs, check_vma=False
    )
```

```python
import functools

import jax
import jax.numpy as jnp
from jax import lax
from jax.experimental import pallas as pl
from jax.experimental.pallas import tpu as pltpu
from jax.sharding import PartitionSpec as P

TILE = 256
WIDTH = 16
BR = 16
MOST = 2
CHUNK = 8
HELD = 16
LANES = 128
F32 = jnp.float32
BF16 = jnp.bfloat16
HIGHEST = lax.Precision.HIGHEST
VMEM_LIMIT = 48 * 1024 * 1024

vmem = pl.BlockSpec(memory_space=pltpu.VMEM)
hbm = pl.BlockSpec(memory_space=pltpu.HBM)
anywhere = pl.BlockSpec(memory_space=pl.ANY)


def shape(dims, dtype=F32):
    return jax.ShapeDtypeStruct(dims, dtype)


def call(kernel, out_shape, in_specs, scratch_shapes=(), flops=10**6, moved=10**6, name=None):
    return pl.pallas_call(
        kernel,
        out_shape=out_shape,
        in_specs=in_specs,
        out_specs=jax.tree.map(lambda _: vmem, out_shape),
        scratch_shapes=scratch_shapes,
        cost_estimate=pl.CostEstimate(flops=flops, bytes_accessed=moved, transcendentals=0),
        compiler_params=pltpu.CompilerParams(vmem_limit_bytes=VMEM_LIMIT),
        name=name,
    )


def times(left, right):
    return lax.dot_general(left, right, (((1,), (0,)), ((), ())), preferred_element_type=F32)


def times_t(left, right):
    return lax.dot_general(left, right, (((1,), (1,)), ((), ())), preferred_element_type=F32)


def in_hbm(value):
    return pltpu.with_memory_space_constraint(value, pltpu.HBM)


def fetch(sources, targets, sems):
    copies = [
        pltpu.make_async_copy(source, target, sems.at[n])
        for n, (source, target) in enumerate(zip(sources, targets))
    ]
    for copy in copies:
        copy.start()

    def wait():
        for copy in copies:
            copy.wait()

    return wait


def slots_of(groups_ref, count_ref, tile_count, group_count):
    for g in range(group_count):
        count_ref[g] = 0
    for t in range(tile_count):
        g = groups_ref[0, 0, t]
        m = count_ref[g]
        count_ref[g] = m + 1
        yield t, g, m


def weighted_sums(size, gains):
    sub = lax.broadcasted_iota(jnp.int32, (8, TILE), 0)
    gains = jnp.abs(gains)
    left = jnp.where(sub == 0, gains[0:1, :], jnp.where(sub == 1, gains[1:2, :], 0.0))
    high = left.astype(BF16).astype(F32)
    halves = jnp.concatenate([high, left - high], axis=0).astype(BF16)
    rows, cols = times_t(halves, size), times(halves, size)
    return (rows[1:2] + rows[9:10]) * gains[0:1, :], (cols[0:1] + cols[8:9]) * gains[1:2, :]


def remote_degree_kernel(
    group_count,
    weights,
    gains,
    groups,
    coords,
    payload,
    row_degree,
    tiles,
    tile_gains,
    tile_groups,
    tile_coords,
    count,
    sems,
):
    wait = fetch(
        (groups, coords, gains, weights), (tile_groups, tile_coords, tile_gains, tiles), sems
    )
    sub = lax.broadcasted_iota(jnp.int32, (8, TILE), 0)
    blank = jnp.where((sub >= MOST) & (sub < 2 * MOST), -1.0, 0.0).astype(F32)
    for g in range(group_count):
        payload[g] = blank
    row_degree[...] = jnp.zeros(row_degree.shape, F32)
    wait()
    places = slots_of(tile_groups, count, weights.shape[2], group_count)
    for t, g, m in places:
        r, c = tile_coords[0, 0, 0, t], tile_coords[0, 0, 1, t]
        by_row, by_col = weighted_sums(jnp.abs(tiles[0, 0, t]), tile_gains[0, 0, t])
        row_degree[pl.ds(r, 1), :] += by_row
        payload[g, pl.ds(m, 1), :] = by_col
        payload[g, pl.ds(MOST + m, 1), :] = jnp.full((1, TILE), c, jnp.int32).astype(F32)


def halves_of(value):
    high = value.astype(BF16)
    return high, (value - high.astype(F32)).astype(BF16)


def add_by_place(places, values):
    shape = (BR, places.shape[1])
    chosen = (lax.broadcasted_iota(jnp.int32, shape, 0) == places).astype(BF16)
    high, low = halves_of(values)
    return times(chosen, high) + times(chosen, low)


def local_degree_kernel(
    weights, gains, coords, degree, ready, tiles, tile_gains, places, by_row, by_col, sems, small_sems
):
    count, held = weights.shape[2], ready.shape[0]

    def copy_of(n, base, target):
        source = weights.at[0, 0, pl.ds(base + n * CHUNK, CHUNK)]
        return pltpu.make_async_copy(
            source, target.at[pl.ds(n * CHUNK, CHUNK)], sems.at[base // CHUNK + n]
        )

    wait = fetch((gains, coords), (tile_gains, places), small_sems)
    parts = ((0, ready), (held, tiles))
    for base, target in parts:
        for n in range(target.shape[0] // CHUNK):
            copy_of(n, base, target).start()
    by_row[...] = jnp.zeros(by_row.shape, F32)
    first = lax.broadcasted_iota(jnp.int32, (8, TILE), 0) == 0
    lane = lax.broadcasted_iota(jnp.int32, by_row.shape, 1)
    wait()

    def step(base, target, n, _):
        copy_of(n, base, target).wait()
        for k in range(CHUNK):
            t = base + n * CHUNK + k
            size = jnp.abs(target[n * CHUNK + k])
            pair = jnp.abs(tile_gains[0, 0, t])
            left = jnp.where(first, pair[0:1, :], 0.0)
            high = left.astype(BF16).astype(F32)
            sums = times(jnp.concatenate([high, left - high], axis=0).astype(BF16), size)
            by_col[pl.ds(t, 1), :] = (sums[0:1] + sums[8:9]) * pair[1:2, :]
            sums = jnp.sum(size.astype(F32) * pair[1:2, :], axis=1, keepdims=True)
            by_row[...] = jnp.where(lane == t, sums, by_row[...])
        return 0

    for base, target in parts:
        lax.fori_loop(0, target.shape[0] // CHUNK, functools.partial(step, base, target), 0)
    row_sums = jnp.transpose(by_row[...])[:count] * jnp.abs(tile_gains[0, 0, :, 0, :])
    degree[...] = add_by_place(places[0, 0, 0:1, :], row_sums) + add_by_place(
        places[0, 0, 1:2, :], by_col[...]
    )


def scale_kernel(raw, gains, scaled):
    row_gain = jnp.transpose(gains[0, 0, :, 0, :])
    for k in range(raw.shape[2]):
        scaled[k] = (
            row_gain[:, k : k + 1] * raw[0, 0, k].astype(F32) * gains[0, 0, k, 1:2, :]
        ).astype(BF16)


def scale(weights, gains, name):
    count = weights.shape[2]
    return pl.pallas_call(
        scale_kernel,
        out_shape=shape((count, TILE, TILE), BF16),
        grid=(count // CHUNK,),
        in_specs=[
            pl.BlockSpec((1, 1, CHUNK, TILE, TILE), lambda n: (0, 0, n, 0, 0)),
            pl.BlockSpec((1, 1, CHUNK, 2, TILE), lambda n: (0, 0, n, 0, 0)),
        ],
        out_specs=pl.BlockSpec((CHUNK, TILE, TILE), lambda n: (n, 0, 0)),
        cost_estimate=pl.CostEstimate(
            flops=2 * count * TILE * TILE, bytes_accessed=4 * count * TILE * TILE, transcendentals=0
        ),
        compiler_params=pltpu.CompilerParams(vmem_limit_bytes=VMEM_LIMIT),
        name=name,
    )(in_hbm(weights), gains)


def join_degree_kernel(arrived, row_degree, local_degree, joined):
    total = row_degree[...] + local_degree[...]
    sub = lax.broadcasted_iota(jnp.int32, total.shape, 0).astype(F32)
    for g in range(arrived.shape[0]):
        block = arrived[g]
        for m in range(MOST):
            hit = sub == block[MOST + m : MOST + m + 1, :]
            total += jnp.where(hit, block[m : m + 1, :], 0.0)
    joined[...] = total


def offsets(count):
    return [0] + list(range(count - 1, 0, -1))


def by_chips(groups):
    return groups // 2 <= 4


def place_of(group, group_count, core):
    if not by_chips(group_count):
        return group
    return ((group + core) % 2) * (group_count // 2) + group // 2


def outgoing(x, scaled, groups, coords, targets, staged, count, gram=None):
    group_count = staged.shape[0]
    core = lax.axis_index("rows") % 2
    for g in range(group_count):
        staged[g, MOST : 2 * MOST] = jnp.zeros((MOST, WIDTH, TILE), BF16)
        if gram is not None:
            staged[g, 2 * MOST] = gram
    for t, g, m in slots_of(groups, count, scaled.shape[0], group_count):
        place = place_of(g, group_count, core)
        staged[place, MOST + m] = times(x[coords[0, 0, 0, t]], scaled[t]).astype(BF16)
    for g in range(group_count):
        place = place_of(g, group_count, core)
        for m in range(MOST):
            staged[place, m] = x[jnp.maximum(targets[g, m], 0)]


def split_out(staged, outs):
    size = outs[0].shape[0]
    for k, out in enumerate(outs):
        out[...] = staged[k * size : (k + 1) * size]


def forward_kernel(near, passed, *pieces):
    chips = near.shape[0]
    me = lax.axis_index("rows")
    chip, core = me // 2, me % 2
    for k, piece in zip(offsets(chips), pieces):
        piece[core] = near[chip ^ k]
        piece[1 - core] = passed[chip ^ k]


def by_group(arrived, joined):
    if len(arrived) == 1:
        joined[...] = arrived[0][...]
        return
    chip = lax.axis_index("rows") // 2
    for k, piece in zip(offsets(len(arrived)), arrived):
        joined[pl.ds((chip ^ k) * 2, 2)] = piece[...]


def first_block_kernel(splits, start, scaled, groups, coords, targets, *refs):
    parts, (inv_root, x, *refs) = refs[:splits], refs[splits:]
    *outs, count, staged = refs
    routes = (groups, coords, targets)
    degree = parts[0][...]
    for part in parts[1:]:
        degree += part[...]
    inv = 1.0 / jnp.sqrt(degree)
    inv_root[...] = inv
    for k in range(BR):
        x[k] = (start[:, k * TILE : (k + 1) * TILE] * inv[k : k + 1, :]).astype(BF16)
    outgoing(x, scaled, *routes, staged, count)
    split_out(staged, outs)


def pair_sum_kernel(mine, theirs, total, sent):
    value = mine[...] + theirs[...].astype(F32)
    total[...] = value
    sent[...] = value.astype(BF16)


def next_block_kernel(
    vertices, scaled, inv_root, groups, coords, targets, mine, theirs, x, *refs
):
    *outs, count, staged = refs
    routes = (groups, coords, targets)
    gram = jnp.zeros((2 * WIDTH, 2 * WIDTH), F32)
    for k in range(BR):
        value = mine[k] + theirs[k].astype(F32)
        root = inv_root[k : k + 1, :]
        image = value * root
        x[k] = (image * root).astype(BF16)
        high = image.astype(BF16)
        halves = jnp.concatenate([high, (image - high.astype(F32)).astype(BF16)], axis=0)
        gram += times_t(halves, halves)
    low = gram[:WIDTH, WIDTH:] + gram[WIDTH:, :WIDTH] + gram[WIDTH:, WIDTH:]
    gram = (gram[:WIDTH, :WIDTH] + low) / vertices
    high = gram.astype(BF16)
    middle = (gram - high.astype(F32)).astype(BF16)
    low = (gram - high.astype(F32) - middle.astype(F32)).astype(BF16)
    block = jnp.concatenate(
        [high, middle, low, jnp.zeros((WIDTH, TILE - 3 * WIDTH), BF16)], axis=1
    )
    outgoing(x, scaled, *routes, staged, count, block)
    split_out(staged, outs)


def local_products_kernel(
    x, ready, weights, gains, coords, partial, tiles, sems, tile_coords, coord_sems
):
    held, count, chunk = ready.shape[0], tiles.shape[0], CHUNK
    batch = 2 * chunk if count % (2 * chunk) == 0 else chunk

    def copy_of(n):
        source = weights.at[0, 0, pl.ds(held + n * chunk, chunk)]
        return pltpu.make_async_copy(source, tiles.at[pl.ds(n * chunk, chunk)], sems.at[n])

    wait = fetch((coords,), (tile_coords,), coord_sems)
    for n in range(count // chunk):
        copy_of(n).start()
    partial[...] = jnp.zeros(partial.shape, F32)
    wait()

    def add(base, raw):
        row_gains = [
            jnp.transpose(gains[0, 0, pl.ds(base + k, CHUNK), 0, :])
            for k in range(0, len(raw), CHUNK)
        ]
        places, results = [], []
        for k, tile in enumerate(raw):
            t = base + k
            r, c = tile_coords[0, 0, 0, t], tile_coords[0, 0, 1, t]
            row_gain = row_gains[k // CHUNK][:, k % CHUNK : k % CHUNK + 1]
            tile = (row_gain * tile().astype(F32) * gains[0, 0, t, 1:2, :]).astype(BF16)
            results.append((times_t(x[c], tile), times(x[r], tile)))
            places.append((r, c))
        for (r, c), (forward, backward) in zip(places, results):
            partial[r] += forward
            partial[c] += backward

    add(0, [lambda k=k: ready[k] for k in range(held)])

    def step(n, _):
        for k in range(batch // chunk):
            copy_of(n * (batch // chunk) + k).wait()
        add(held + n * batch, [lambda k=k: tiles[n * batch + k] for k in range(batch)])
        return 0

    lax.fori_loop(0, count // batch, step, 0)


def remote_products_kernel(splits, whole, pieces, scaled, partial, groups, coords, targets, *refs):
    arrived, refs = refs[:pieces], refs[pieces:]
    *outs, total, count, joined = refs
    group_count = joined.shape[0]
    by_group(arrived, joined)
    total[...] = partial[...]
    for t, g, m in slots_of(groups, count, scaled.shape[0], group_count):
        total[coords[0, 0, 0, t]] += times_t(joined[g, m], scaled[t])
    for g in range(group_count):
        for m in range(MOST):
            total[jnp.maximum(targets[g, m], 0)] += joined[g, MOST + m].astype(F32)
    if whole:
        for out in outs:
            out[...] = total[...].astype(out.dtype)
        return
    me = lax.axis_index("cols")
    quarter = BR // splits
    for k, out in zip(offsets(splits), outs):
        base = pl.multiple_of((me ^ k) * quarter, quarter)
        out[...] = total[pl.ds(base, quarter)].astype(out.dtype)


def quarter_sum(pieces, inv_root, me):
    quarter = pieces[0].shape[0]
    images, roots = [], []
    for k in range(quarter):
        value = pieces[0][k]
        for piece in pieces[1:]:
            value += piece[k].astype(F32)
        root = inv_root[pl.ds(me * quarter + k, 1), :]
        images.append(value * root)
        roots.append(root)
    return images, roots


def eliminate(gram, right):
    shape = (WIDTH, LANES)
    row = lax.broadcasted_iota(jnp.int32, shape, 0)
    lane = lax.broadcasted_iota(jnp.int32, shape, 1)
    gram = jnp.concatenate([gram, jnp.zeros((WIDTH, LANES - WIDTH), F32)], axis=1)
    for k in range(0, WIDTH, 2):
        first = jnp.broadcast_to(gram[:, k : k + 1], shape)
        second = jnp.broadcast_to(gram[:, k + 1 : k + 2], shape)
        factor = first / first[k : k + 1]
        second = second - factor * second[k : k + 1]
        then = jnp.where(row > k + 1, second / second[k + 1 : k + 2], 0.0)
        link = factor[k + 1 : k + 2]
        factor = jnp.where(row > k, factor, 0.0)

        def step(work):
            top = work[k : k + 1, :]
            return work - factor * top - then * (work[k + 1 : k + 2, :] - link * top)

        gram, right = step(gram), [step(block) for block in right]
    pivots = jnp.sum(jnp.where(row == lane, gram, 0.0), axis=1, keepdims=True)
    root = jnp.broadcast_to(1.0 / jnp.sqrt(pivots), shape)
    return [block * root for block in right]


def middle_factor_kernel(*refs):
    *arrived, inverse = refs
    gram = jnp.zeros((WIDTH, WIDTH), F32)
    for block in [piece[g, 2 * MOST] for piece in arrived for g in range(piece.shape[0])]:
        block = block.astype(F32)
        gram += (block[:, 2 * WIDTH : 3 * WIDTH] + block[:, WIDTH : 2 * WIDTH]) + block[:, :WIDTH]
    eye = lax.broadcasted_iota(jnp.int32, (WIDTH, LANES), 0) == lax.broadcasted_iota(
        jnp.int32, (WIDTH, LANES), 1
    )
    (result,) = eliminate(gram, [eye.astype(F32)])
    inverse[...] = result[:, :WIDTH]


def last_quarter_kernel(splits, vertices, inv_root, inverse, *refs):
    pieces, (image_out, grams) = refs[:splits], refs[splits:]
    images, _ = quarter_sum(pieces, inv_root, lax.axis_index("cols"))
    first = inverse[...]
    gram = jnp.zeros((WIDTH, WIDTH), F32)
    for k, image in enumerate(images):
        value = jnp.dot(first, image, precision=HIGHEST, preferred_element_type=F32)
        image_out[:, k * TILE : (k + 1) * TILE] = value
        gram += lax.dot_general(
            value, value, (((1,), (1,)), ((), ())), precision=HIGHEST, preferred_element_type=F32
        )
    gram = gram / vertices
    block = jnp.concatenate([gram[2 * n : 2 * n + 2] for n in range(WIDTH // 2)], axis=1)
    for n in range(grams.shape[0]):
        grams[n] = block


def finish_kernel(grams, image, out):
    block = grams[0]
    for n in range(1, grams.shape[0]):
        block = block + grams[n]
    gram = jnp.concatenate(
        [block[:, WIDTH * n : WIDTH * (n + 1)] for n in range(WIDTH // 2)], axis=0
    )
    starts = range(0, out.shape[1], LANES)
    for n, block in zip(starts, eliminate(gram, [image[:, n : n + LANES] for n in starts])):
        out[:, n : n + LANES] = block


def per_device(
    local_weights,
    local_gains,
    local_coords,
    remote_weights,
    remote_gains,
    remote_groups,
    remote_coords,
    start_block,
):
    groups = lax.axis_size("rows")
    splits = lax.axis_size("cols")
    vertices = groups * BR * TILE
    quarter = BR // splits
    local_coords, remote_coords = jnp.swapaxes(local_coords, 2, 3), jnp.swapaxes(remote_coords, 2, 3)
    local_tiles, remote_tiles = local_weights.shape[2], remote_weights.shape[2]
    count = pltpu.SMEM((groups,), jnp.int32)

    partners = [2 * 2**k - 1 for k in range(splits.bit_length() - 1)]

    def swap(value, k):
        return lax.ppermute(value, "cols", [(j, j ^ k) for j in range(splits)])

    def trade(value):
        return lax.all_to_all(value, "rows", split_axis=0, concat_axis=0, tiled=True)

    listing = (remote_weights, remote_gains, remote_groups, remote_coords)
    sums, row_degree = call(
        functools.partial(remote_degree_kernel, groups),
        (shape((groups, 8, TILE)), shape((BR, TILE))),
        [hbm, hbm, hbm, hbm],
        [
            pltpu.VMEM(remote_weights.shape, BF16),
            pltpu.VMEM(remote_gains.shape, F32),
            pltpu.SMEM(remote_groups.shape, jnp.int32),
            pltpu.SMEM(remote_coords.shape, jnp.int32),
            count,
            pltpu.SemaphoreType.DMA((4,)),
        ],
        name="remote_degree",
    )(*[in_hbm(value) for value in listing])
    sums_in = trade(sums)
    local_degree, ready = call(
        local_degree_kernel,
        (shape((BR, TILE)), shape((HELD, TILE, TILE), BF16)),
        [hbm, hbm, hbm],
        [
            pltpu.VMEM((local_tiles - HELD, TILE, TILE), BF16),
            pltpu.VMEM(local_gains.shape, F32),
            pltpu.VMEM(local_coords.shape, jnp.int32),
            pltpu.VMEM((TILE, -(-local_tiles // LANES) * LANES), F32),
            pltpu.VMEM((local_tiles, TILE), F32),
            pltpu.SemaphoreType.DMA((local_tiles // CHUNK,)),
            pltpu.SemaphoreType.DMA((2,)),
        ],
        moved=10**7,
        name="local_degree",
    )(*[in_hbm(value) for value in (local_weights, local_gains, local_coords)])
    targets = sums_in[:, MOST : 2 * MOST, 0].astype(jnp.int32)
    far_scalars = [remote_groups, remote_coords, targets]
    joined = call(
        join_degree_kernel, shape((BR, TILE)), [vmem, vmem, vmem], name="join_degree"
    )(sums_in, row_degree, local_degree)
    joined, remote_gains = lax.optimization_barrier((joined, remote_gains))
    degrees = [joined] + [swap(joined, k) for k in range(1, splits)]
    remote_scaled = scale(remote_weights, remote_gains, "remote_scale")
    def sent_blocks(blocks):
        if by_chips(groups):
            return (shape((groups // 2, blocks, WIDTH, TILE), BF16),) * 2
        return (shape((groups, blocks, WIDTH, TILE), BF16),)

    def staging(blocks):
        return pltpu.VMEM((groups, blocks, WIDTH, TILE), BF16)

    inv_root, x, *sent = call(
        functools.partial(first_block_kernel, splits),
        (shape((BR, TILE)), shape((BR, WIDTH, TILE), BF16)) + sent_blocks(2 * MOST),
        [vmem, vmem, vmem, vmem, vmem] + [vmem] * splits,
        [count, staging(2 * MOST)],
        name="first_block",
    )(start_block, remote_scaled, *far_scalars, *degrees)

    def local_products(x):
        return call(
            local_products_kernel,
            shape((BR, WIDTH, TILE)),
            [vmem, vmem, hbm, vmem, anywhere],
            [
                pltpu.VMEM((local_tiles - HELD, TILE, TILE), BF16),
                pltpu.SemaphoreType.DMA((local_tiles // CHUNK - HELD // CHUNK,)),
                pltpu.SMEM(local_coords.shape, jnp.int32),
                pltpu.SemaphoreType.DMA((1,)),
            ],
            flops=4 * local_tiles * TILE * TILE * WIDTH,
            moved=2 * local_tiles * TILE * TILE,
            name="local_products",
        )(x, ready, local_weights, local_gains, local_coords)

    def product(x, sent, out_shape, whole):
        blocks = sent[0].shape[1]
        if by_chips(groups):
            near, far = sent
            passed = lax.ppermute(far, "rows", [(j, j ^ 1) for j in range(groups)])
            own, *others = call(
                forward_kernel,
                (shape((2, blocks, WIDTH, TILE), BF16),) * (groups // 2),
                [vmem, vmem],
                name="forward",
            )(near, passed)
            arrived = [own] + [
                lax.ppermute(piece, "rows", [(j, j ^ (2 * k)) for j in range(groups)])
                for k, piece in zip(offsets(groups // 2)[1:], others)
            ]
            partial = local_products(x)
        else:
            arrived = [trade(sent[0])]
            partial = local_products(x)
        return arrived, call(
            functools.partial(remote_products_kernel, splits, whole, len(arrived)),
            out_shape,
            [vmem, vmem, vmem, vmem, vmem] + [vmem] * len(arrived),
            [pltpu.VMEM((BR, WIDTH, TILE), F32), count, staging(blocks)],
            name="remote_products",
        )(remote_scaled, partial, *far_scalars, *arrived)

    _, (own, sent) = product(
        x, sent, (shape((BR, WIDTH, TILE)), shape((BR, WIDTH, TILE), BF16)), True
    )
    for k in partners[:-1]:
        own, sent = call(
            pair_sum_kernel,
            (shape((BR, WIDTH, TILE)), shape((BR, WIDTH, TILE), BF16)),
            [vmem, vmem],
            name="pair_sum",
        )(own, swap(sent, k))
    x, *sent = call(
        functools.partial(next_block_kernel, vertices),
        (shape((BR, WIDTH, TILE), BF16),) + sent_blocks(2 * MOST + 1),
        [vmem, vmem, vmem, vmem, vmem, vmem, vmem],
        [count, staging(2 * MOST + 1)],
        name="next_block",
    )(
        remote_scaled,
        inv_root,
        *far_scalars,
        own,
        swap(sent, partners[-1]),
    )
    arrived, sent = product(
        x,
        sent,
        tuple(shape((quarter, WIDTH, TILE), BF16 if k else F32) for k in range(splits)),
        False,
    )
    pieces = [sent[0]] + [swap(part, k) for k, part in zip(offsets(splits)[1:], sent[1:])]
    inverse = call(
        middle_factor_kernel,
        shape((WIDTH, WIDTH)),
        [vmem] * len(arrived),
        name="middle_factor",
    )(*arrived)
    image, grams = call(
        functools.partial(last_quarter_kernel, splits, vertices),
        (shape((WIDTH, quarter * TILE)), shape((groups * splits, 2, LANES))),
        [vmem] * (2 + splits),
        name="last_quarter",
    )(inv_root, inverse, *pieces)
    grams = lax.all_to_all(
        grams, ("rows", "cols"), split_axis=0, concat_axis=0, tiled=True
    )
    return call(finish_kernel, shape((WIDTH, quarter * TILE)), [vmem, vmem], name="finish")(
        grams, image
    )


def solution(mesh):
    in_specs = (
        P("rows", "cols", None, None, None),
        P("rows", "cols", None, None, None),
        P("rows", "cols", None, None),
        P("rows", "cols", None, None, None),
        P("rows", "cols", None, None, None),
        P("rows", "cols", None),
        P("rows", "cols", None, None),
        P(None, "rows"),
    )
    out_specs = P(None, ("rows", "cols"))
    return jax.shard_map(
        per_device, mesh=mesh, in_specs=in_specs, out_specs=out_specs, check_vma=False
    )
```

```python
import functools

import jax
import jax.numpy as jnp
from jax import lax
from jax.experimental import pallas as pl
from jax.experimental.pallas import tpu as pltpu
from jax.sharding import PartitionSpec as P

TILE = 256
WIDTH = 16
BR = 16
MOST = 2
CHUNK = 8
HEAD = 16
LANES = 128
F32 = jnp.float32
BF16 = jnp.bfloat16
HIGHEST = lax.Precision.HIGHEST
VMEM_LIMIT = 16 * 1024 * 1024

vmem = pl.BlockSpec(memory_space=pltpu.VMEM)
hbm = pl.BlockSpec(memory_space=pltpu.HBM)
anywhere = pl.BlockSpec(memory_space=pl.ANY)


def shape(dims, dtype=F32):
    return jax.ShapeDtypeStruct(dims, dtype)


def call(kernel, out_shape, in_specs, scratch_shapes=(), flops=10**6, moved=10**6, name=None):
    return pl.pallas_call(
        kernel,
        out_shape=out_shape,
        in_specs=in_specs,
        out_specs=jax.tree.map(lambda _: vmem, out_shape),
        scratch_shapes=scratch_shapes,
        cost_estimate=pl.CostEstimate(flops=flops, bytes_accessed=moved, transcendentals=0),
        compiler_params=pltpu.CompilerParams(vmem_limit_bytes=VMEM_LIMIT),
        name=name,
    )


def times(left, right):
    return lax.dot_general(left, right, (((1,), (0,)), ((), ())), preferred_element_type=F32)


def times_t(left, right):
    return lax.dot_general(left, right, (((1,), (1,)), ((), ())), preferred_element_type=F32)


def in_hbm(value):
    return pltpu.with_memory_space_constraint(value, pltpu.HBM)


def fetch(sources, targets, sems):
    copies = [
        pltpu.make_async_copy(source, target, sems.at[n])
        for n, (source, target) in enumerate(zip(sources, targets))
    ]
    for copy in copies:
        copy.start()

    def wait():
        for copy in copies:
            copy.wait()

    return wait


def slots_of(groups_ref, count_ref, tile_count, group_count):
    for g in range(group_count):
        count_ref[g] = 0
    for t in range(tile_count):
        g = groups_ref[0, 0, t]
        m = count_ref[g]
        count_ref[g] = m + 1
        yield t, g, m


def weighted_sums(size, gains):
    sub = lax.broadcasted_iota(jnp.int32, (8, TILE), 0)
    gains = jnp.abs(gains)
    left = jnp.where(sub == 0, gains[0:1, :], jnp.where(sub == 1, gains[1:2, :], 0.0))
    high = left.astype(BF16).astype(F32)
    halves = jnp.concatenate([high, left - high], axis=0).astype(BF16)
    rows, cols = times_t(halves, size), times(halves, size)
    return (rows[1:2] + rows[9:10]) * gains[0:1, :], (cols[0:1] + cols[8:9]) * gains[1:2, :]


def remote_degree_kernel(weights, gains, groups, coords, near_weights, row_degree, tiles, held, *refs):
    *outs, tile_gains, tile_groups, tile_coords, staged, count, sems = refs
    group_count = staged.shape[0]
    wait = fetch(
        (groups, coords, gains, weights.at[0, 0]),
        (tile_groups, tile_coords, tile_gains, tiles),
        sems.at[pl.ds(0, 4)],
    )
    wait_held = fetch(
        (near_weights.at[0, 0, pl.ds(0, held.shape[0])],), (held,), sems.at[pl.ds(4, 1)]
    )
    sub = lax.broadcasted_iota(jnp.int32, (8, TILE), 0)
    blank = jnp.where((sub >= MOST) & (sub < 2 * MOST), -1.0, 0.0).astype(F32)
    for g in range(group_count):
        staged[g] = blank
    row_degree[...] = jnp.zeros(row_degree.shape, F32)
    core = lax.axis_index("rows") % 2
    wait()
    for t, g, m in slots_of(tile_groups, count, tiles.shape[0], group_count):
        place = place_of(g, group_count, core)
        r, c = tile_coords[0, 0, 0, t], tile_coords[0, 0, 1, t]
        by_row, by_col = weighted_sums(jnp.abs(tiles[t]), tile_gains[0, 0, t])
        row_degree[pl.ds(r, 1), :] += by_row
        staged[place, pl.ds(m, 1), :] = by_col
        staged[place, pl.ds(MOST + m, 1), :] = jnp.full((1, TILE), c, jnp.int32).astype(F32)
    split_out(staged, outs)
    wait_held()


def halves_of(value):
    high = value.astype(BF16)
    return high, (value - high.astype(F32)).astype(BF16)


def add_by_place(places, values):
    shape = (BR, places.shape[1])
    chosen = (lax.broadcasted_iota(jnp.int32, shape, 0) == places).astype(BF16)
    high, low = halves_of(values)
    return times(chosen, high) + times(chosen, low)


def local_degree_kernel(
    held, weights, gains, coords, degree, tiles, by_row, by_col, sems
):
    first, count = held.shape[0], weights.shape[2]

    def copy_of(n):
        source = weights.at[0, 0, pl.ds(first + n * CHUNK, CHUNK)]
        return pltpu.make_async_copy(source, tiles.at[pl.ds(n * CHUNK, CHUNK)], sems.at[n])

    for n in range((count - first) // CHUNK):
        copy_of(n).start()
    by_row[...] = jnp.zeros(by_row.shape, F32)
    top = lax.broadcasted_iota(jnp.int32, (8, TILE), 0) == 0
    lane = lax.broadcasted_iota(jnp.int32, by_row.shape, 1)

    def add(t, size):
        pair = jnp.abs(gains[0, 0, t])
        left = jnp.where(top, pair[0:1, :], 0.0)
        high = left.astype(BF16).astype(F32)
        sums = times(jnp.concatenate([high, left - high], axis=0).astype(BF16), size)
        by_col[pl.ds(t, 1), :] = (sums[0:1] + sums[8:9]) * pair[1:2, :]
        sums = jnp.sum(size.astype(F32) * pair[1:2, :], axis=1, keepdims=True)
        by_row[...] = jnp.where(lane == t, sums, by_row[...])

    def held_step(n, _):
        for k in range(CHUNK):
            add(n * CHUNK + k, jnp.abs(held[n * CHUNK + k]))
        return 0

    def step(n, _):
        copy_of(n).wait()
        for k in range(CHUNK):
            add(first + n * CHUNK + k, jnp.abs(tiles[n * CHUNK + k]))
        return 0

    lax.fori_loop(0, first // CHUNK, held_step, 0)
    lax.fori_loop(0, (count - first) // CHUNK, step, 0)
    row_sums = jnp.transpose(by_row[...])[:count] * jnp.abs(gains[0, 0, :, 0, :])
    degree[...] = add_by_place(coords[0, 0, 0:1, :], row_sums) + add_by_place(
        coords[0, 0, 1:2, :], by_col[...]
    )


def scale_kernel(raw, gains, scaled):
    def step(n, _):
        base = n * CHUNK
        row_gain = jnp.transpose(gains[0, 0, pl.ds(base, CHUNK), 0, :])
        for k in range(CHUNK):
            scaled[base + k] = (
                row_gain[:, k : k + 1]
                * raw[base + k].astype(F32)
                * gains[0, 0, base + k, 1:2, :]
            ).astype(BF16)
        return 0

    lax.fori_loop(0, scaled.shape[0] // CHUNK, step, 0)


def scale(raw, gains, name):
    return call(
        scale_kernel, shape(raw.shape, BF16), [vmem, vmem], flops=2 * raw.size, name=name
    )(raw, gains)


def join_degree_kernel(row_degree, local_degree, *refs):
    *arrived, joined, targets, sums = refs
    by_group(arrived, sums)
    targets[...] = sums[...].astype(jnp.int32)
    total = row_degree[...] + local_degree[...]
    sub = lax.broadcasted_iota(jnp.int32, total.shape, 0).astype(F32)
    for g in range(sums.shape[0]):
        block = sums[g]
        for m in range(MOST):
            hit = sub == block[MOST + m : MOST + m + 1, :]
            total += jnp.where(hit, block[m : m + 1, :], 0.0)
    joined[...] = total


def offsets(count):
    return [0] + list(range(count - 1, 0, -1))


def by_chips(groups):
    return groups // 2 <= 4


def place_of(group, group_count, core):
    if not by_chips(group_count):
        return group
    return ((group + core) % 2) * (group_count // 2) + group // 2


def outgoing(x, scaled, groups, coords, targets, staged, count, gram=None):
    group_count = staged.shape[0]
    core = lax.axis_index("rows") % 2
    for g in range(group_count):
        staged[g, MOST : 2 * MOST] = jnp.zeros((MOST, WIDTH, TILE), BF16)
        if gram is not None:
            staged[g, 2 * MOST] = gram
    for t, g, m in slots_of(groups, count, scaled.shape[0], group_count):
        place = place_of(g, group_count, core)
        staged[place, MOST + m] = times(x[coords[0, 0, 0, t]], scaled[t]).astype(BF16)
    for g in range(group_count):
        place = place_of(g, group_count, core)
        for m in range(MOST):
            staged[place, m] = x[jnp.maximum(targets[g, MOST + m, 0], 0)]


def split_out(staged, outs):
    size = outs[0].shape[0]
    for k, out in enumerate(outs):
        out[...] = staged[k * size : (k + 1) * size]


def forward_kernel(near, passed, *refs):
    chips = near.shape[0]
    pieces = refs[-chips:]
    me = lax.axis_index("rows")
    chip, core = me // 2, me % 2
    for k, piece in zip(offsets(chips), pieces):
        piece[core] = near[chip ^ k]
        piece[1 - core] = passed[chip ^ k]


def by_group(arrived, joined):
    if len(arrived) == 1:
        joined[...] = arrived[0][...]
        return
    chip = lax.axis_index("rows") // 2
    for k, piece in zip(offsets(len(arrived)), arrived):
        joined[pl.ds((chip ^ k) * 2, 2)] = piece[...]


def first_block_kernel(splits, start, scaled, groups, coords, targets, later, *refs):
    parts, (inv_root, x, *refs) = refs[:splits], refs[splits:]
    *outs, count, staged = refs
    routes = (groups, coords, targets)
    degree = parts[0][...]
    for part in parts[1:]:
        degree += part[...]
    inv = 1.0 / jnp.sqrt(degree)
    inv_root[...] = inv
    for k in range(BR):
        x[k] = (start[:, k * TILE : (k + 1) * TILE] * inv[k : k + 1, :]).astype(BF16)
    outgoing(x, scaled, *routes, staged, count)
    split_out(staged, outs)


def pair_sum_kernel(mine, theirs, total, sent):
    value = mine[...] + theirs[...].astype(F32)
    total[...] = value
    sent[...] = value.astype(BF16)


def next_block_kernel(
    vertices, scaled, inv_root, groups, coords, targets, mine, theirs, x, *refs
):
    *outs, count, staged = refs
    routes = (groups, coords, targets)
    gram = jnp.zeros((2 * WIDTH, 2 * WIDTH), F32)
    for k in range(BR):
        value = mine[k] + theirs[k].astype(F32)
        root = inv_root[k : k + 1, :]
        image = value * root
        x[k] = (image * root).astype(BF16)
        high = image.astype(BF16)
        halves = jnp.concatenate([high, (image - high.astype(F32)).astype(BF16)], axis=0)
        gram += times_t(halves, halves)
    low = gram[:WIDTH, WIDTH:] + gram[WIDTH:, :WIDTH] + gram[WIDTH:, WIDTH:]
    gram = (gram[:WIDTH, :WIDTH] + low) / vertices
    high = gram.astype(BF16)
    middle = (gram - high.astype(F32)).astype(BF16)
    low = (gram - high.astype(F32) - middle.astype(F32)).astype(BF16)
    block = jnp.concatenate(
        [high, middle, low, jnp.zeros((WIDTH, TILE - 3 * WIDTH), BF16)], axis=1
    )
    outgoing(x, scaled, *routes, staged, count, block)
    split_out(staged, outs)


def local_products_kernel(first, x, tiles, coords, *refs):
    *refs, partial, tile_coords, sems = refs
    gains, earlier = refs or (None, None)
    count = tiles.shape[0]
    batch = 2 * CHUNK if count % (2 * CHUNK) == 0 else CHUNK
    wait = fetch((coords,), (tile_coords,), sems)
    partial[...] = earlier[...] if refs else jnp.zeros(partial.shape, F32)
    wait()

    def step(n, _):
        base = first + n * batch
        if refs:
            row_gains = [
                jnp.transpose(gains[0, 0, pl.ds(base + k, CHUNK), 0, :])
                for k in range(0, batch, CHUNK)
            ]
        places, results = [], []
        for k in range(batch):
            t = base + k
            r, c = tile_coords[0, 0, 0, t], tile_coords[0, 0, 1, t]
            tile = tiles[n * batch + k]
            if refs:
                row_gain = row_gains[k // CHUNK][:, k % CHUNK : k % CHUNK + 1]
                tile = (row_gain * tile.astype(F32) * gains[0, 0, t, 1:2, :]).astype(BF16)
            results.append((times_t(x[c], tile), times(x[r], tile)))
            places.append((r, c))
        for (r, c), (forward, backward) in zip(places, results):
            partial[r] += forward
            partial[c] += backward
        return 0

    lax.fori_loop(0, count // batch, step, 0)


def remote_products_kernel(splits, whole, pieces, scaled, partial, groups, coords, targets, *refs):
    arrived, refs = refs[:pieces], refs[pieces:]
    *outs, total, count, joined = refs
    group_count = joined.shape[0]
    by_group(arrived, joined)
    total[...] = partial[...]
    for t, g, m in slots_of(groups, count, scaled.shape[0], group_count):
        total[coords[0, 0, 0, t]] += times_t(joined[g, m], scaled[t])
    for g in range(group_count):
        for m in range(MOST):
            total[jnp.maximum(targets[g, MOST + m, 0], 0)] += joined[g, MOST + m].astype(F32)
    if whole:
        for out in outs:
            out[...] = total[...].astype(out.dtype)
        return
    me = lax.axis_index("cols")
    quarter = BR // splits
    for k, out in zip(offsets(splits), outs):
        base = pl.multiple_of((me ^ k) * quarter, quarter)
        out[...] = total[pl.ds(base, quarter)].astype(out.dtype)


def quarter_sum(pieces, inv_root, me):
    quarter = pieces[0].shape[0]
    images, roots = [], []
    for k in range(quarter):
        value = pieces[0][k]
        for piece in pieces[1:]:
            value += piece[k].astype(F32)
        root = inv_root[pl.ds(me * quarter + k, 1), :]
        images.append(value * root)
        roots.append(root)
    return images, roots


def eliminate(gram, right):
    shape = (WIDTH, LANES)
    row = lax.broadcasted_iota(jnp.int32, shape, 0)
    lane = lax.broadcasted_iota(jnp.int32, shape, 1)
    gram = jnp.concatenate([gram, jnp.zeros((WIDTH, LANES - WIDTH), F32)], axis=1)
    for k in range(0, WIDTH, 2):
        first = jnp.broadcast_to(gram[:, k : k + 1], shape)
        second = jnp.broadcast_to(gram[:, k + 1 : k + 2], shape)
        factor = first / first[k : k + 1]
        second = second - factor * second[k : k + 1]
        then = jnp.where(row > k + 1, second / second[k + 1 : k + 2], 0.0)
        link = factor[k + 1 : k + 2]
        factor = jnp.where(row > k, factor, 0.0)

        def step(work):
            top = work[k : k + 1, :]
            return work - factor * top - then * (work[k + 1 : k + 2, :] - link * top)

        gram, right = step(gram), [step(block) for block in right]
    pivots = jnp.sum(jnp.where(row == lane, gram, 0.0), axis=1, keepdims=True)
    root = jnp.broadcast_to(1.0 / jnp.sqrt(pivots), shape)
    return [block * root for block in right]


def middle_factor_kernel(*refs):
    *arrived, inverse = refs
    gram = jnp.zeros((WIDTH, WIDTH), F32)
    for block in [piece[g, 2 * MOST] for piece in arrived for g in range(piece.shape[0])]:
        block = block.astype(F32)
        gram += (block[:, 2 * WIDTH : 3 * WIDTH] + block[:, WIDTH : 2 * WIDTH]) + block[:, :WIDTH]
    eye = lax.broadcasted_iota(jnp.int32, (WIDTH, LANES), 0) == lax.broadcasted_iota(
        jnp.int32, (WIDTH, LANES), 1
    )
    (result,) = eliminate(gram, [eye.astype(F32)])
    inverse[...] = result[:, :WIDTH]


def last_quarter_kernel(splits, vertices, inv_root, inverse, *refs):
    pieces, (image_out, grams) = refs[:splits], refs[splits:]
    images, _ = quarter_sum(pieces, inv_root, lax.axis_index("cols"))
    first = inverse[...]
    gram = jnp.zeros((WIDTH, WIDTH), F32)
    for k, image in enumerate(images):
        value = jnp.dot(first, image, precision=HIGHEST, preferred_element_type=F32)
        image_out[:, k * TILE : (k + 1) * TILE] = value
        gram += lax.dot_general(
            value, value, (((1,), (1,)), ((), ())), precision=HIGHEST, preferred_element_type=F32
        )
    gram = gram / vertices
    block = jnp.concatenate([gram[2 * n : 2 * n + 2] for n in range(WIDTH // 2)], axis=1)
    for n in range(grams.shape[0]):
        grams[n] = block


def finish_kernel(grams, image, out):
    block = grams[0]
    for n in range(1, grams.shape[0]):
        block = block + grams[n]
    gram = jnp.concatenate(
        [block[:, WIDTH * n : WIDTH * (n + 1)] for n in range(WIDTH // 2)], axis=0
    )
    starts = range(0, out.shape[1], LANES)
    for n, block in zip(starts, eliminate(gram, [image[:, n : n + LANES] for n in starts])):
        out[:, n : n + LANES] = block


def per_device(
    local_weights,
    local_gains,
    local_coords,
    remote_weights,
    remote_gains,
    remote_groups,
    remote_coords,
    start_block,
):
    groups = lax.axis_size("rows")
    splits = lax.axis_size("cols")
    vertices = groups * BR * TILE
    quarter = BR // splits
    local_coords, remote_coords = jnp.swapaxes(local_coords, 2, 3), jnp.swapaxes(remote_coords, 2, 3)
    local_tiles, remote_tiles = local_weights.shape[2], remote_weights.shape[2]
    count = pltpu.SMEM((groups,), jnp.int32)

    partners = [2 * 2**k - 1 for k in range(splits.bit_length() - 1)]

    def swap(value, k):
        return lax.ppermute(value, "cols", [(j, j ^ k) for j in range(splits)])

    def trade(value):
        return lax.all_to_all(value, "rows", split_axis=0, concat_axis=0, tiled=True)

    def sent_blocks(block, dtype):
        if by_chips(groups):
            return (shape((groups // 2,) + block, dtype),) * 2
        return (shape((groups,) + block, dtype),)

    def exchange(sent, before=()):
        if not by_chips(groups):
            return [trade(sent[0])]
        near, far = sent
        passed = lax.ppermute(far, "rows", [(j, j ^ 1) for j in range(groups)])
        own, *others = call(
            forward_kernel,
            (shape((2,) + near.shape[1:], near.dtype),) * (groups // 2),
            [vmem, vmem] + [anywhere] * len(before),
            name="forward",
        )(near, passed, *before)
        return [own] + [
            lax.ppermute(piece, "rows", [(j, j ^ (2 * k)) for j in range(groups)])
            for k, piece in zip(offsets(groups // 2)[1:], others)
        ]

    listing = (remote_weights, remote_gains, remote_groups, remote_coords, local_weights)
    row_degree, remote_raw, held, *sent = call(
        remote_degree_kernel,
        (
            shape((BR, TILE)),
            shape((remote_tiles, TILE, TILE), BF16),
            shape((HEAD, TILE, TILE), BF16),
        )
        + sent_blocks((8, TILE), F32),
        [hbm] * len(listing),
        [
            pltpu.VMEM(remote_gains.shape, F32),
            pltpu.SMEM(remote_groups.shape, jnp.int32),
            pltpu.SMEM(remote_coords.shape, jnp.int32),
            pltpu.VMEM((groups, 8, TILE), F32),
            count,
            pltpu.SemaphoreType.DMA((5,)),
        ],
        name="remote_degree",
    )(*[in_hbm(value) for value in listing])
    sums_in = exchange(sent)
    local_degree, local_raw = call(
        local_degree_kernel,
        (shape((BR, TILE)), shape((local_tiles - HEAD, TILE, TILE), BF16)),
        [vmem, hbm, vmem, vmem],
        [
            pltpu.VMEM((TILE, -(-local_tiles // LANES) * LANES), F32),
            pltpu.VMEM((local_tiles, TILE), F32),
            pltpu.SemaphoreType.DMA(((local_tiles - HEAD) // CHUNK,)),
        ],
        moved=10**7,
        name="local_degree",
    )(held, in_hbm(local_weights), local_gains, local_coords)
    joined, targets = call(
        join_degree_kernel,
        (shape((BR, TILE)), shape((groups, 8, TILE), jnp.int32)),
        [vmem] * (2 + len(sums_in)),
        [pltpu.VMEM((groups, 8, TILE), F32)],
        name="join_degree",
    )(row_degree, local_degree, *sums_in)
    far_scalars = [remote_groups, remote_coords, targets]
    joined, remote_gains, local_gains = lax.optimization_barrier(
        (joined, remote_gains, local_gains)
    )
    degrees = [joined] + [swap(joined, k) for k in range(1, splits)]
    remote_scaled = scale(remote_raw, remote_gains, "remote_scale")
    local_scaled = scale(held, local_gains, "local_scale")

    def staging(blocks):
        return pltpu.VMEM((groups, blocks, WIDTH, TILE), BF16)

    inv_root, x, *sent = call(
        functools.partial(first_block_kernel, splits),
        (shape((BR, TILE)), shape((BR, WIDTH, TILE), BF16))
        + sent_blocks((2 * MOST, WIDTH, TILE), BF16),
        [vmem, vmem, vmem, vmem, vmem, anywhere] + [vmem] * splits,
        [count, staging(2 * MOST)],
        name="first_block",
    )(start_block, remote_scaled, *far_scalars, local_scaled, *degrees)

    def local_products(first, number, x, tiles, *more):
        return call(
            functools.partial(local_products_kernel, first),
            shape((BR, WIDTH, TILE)),
            [vmem, vmem, anywhere] + [vmem] * len(more),
            [
                pltpu.SMEM(local_coords.shape, jnp.int32),
                pltpu.SemaphoreType.DMA((1,)),
            ],
            flops=4 * number * TILE * TILE * WIDTH,
            moved=2 * number * TILE * TILE,
            name="local_products",
        )(x, tiles, local_coords, *more)

    def product(x, sent, out_shape, whole):
        partial = local_products(0, HEAD, x, local_scaled)
        arrived = exchange(sent, (partial,))
        partial = local_products(HEAD, local_tiles - HEAD, x, local_raw, local_gains, partial)
        return arrived, call(
            functools.partial(remote_products_kernel, splits, whole, len(arrived)),
            out_shape,
            [vmem, vmem, vmem, vmem, vmem] + [vmem] * len(arrived),
            [pltpu.VMEM((BR, WIDTH, TILE), F32), count, staging(sent[0].shape[1])],
            name="remote_products",
        )(remote_scaled, partial, *far_scalars, *arrived)

    _, (own, sent) = product(
        x, sent, (shape((BR, WIDTH, TILE)), shape((BR, WIDTH, TILE), BF16)), True
    )
    for k in partners[:-1]:
        own, sent = call(
            pair_sum_kernel,
            (shape((BR, WIDTH, TILE)), shape((BR, WIDTH, TILE), BF16)),
            [vmem, vmem],
            name="pair_sum",
        )(own, swap(sent, k))
    x, *sent = call(
        functools.partial(next_block_kernel, vertices),
        (shape((BR, WIDTH, TILE), BF16),) + sent_blocks((2 * MOST + 1, WIDTH, TILE), BF16),
        [vmem, vmem, vmem, vmem, vmem, vmem, vmem],
        [count, staging(2 * MOST + 1)],
        name="next_block",
    )(
        remote_scaled,
        inv_root,
        *far_scalars,
        own,
        swap(sent, partners[-1]),
    )
    arrived, sent = product(
        x,
        sent,
        tuple(shape((quarter, WIDTH, TILE), BF16 if k else F32) for k in range(splits)),
        False,
    )
    pieces = [sent[0]] + [swap(part, k) for k, part in zip(offsets(splits)[1:], sent[1:])]
    inverse = call(
        middle_factor_kernel,
        shape((WIDTH, WIDTH)),
        [vmem] * len(arrived),
        name="middle_factor",
    )(*arrived)
    image, grams = call(
        functools.partial(last_quarter_kernel, splits, vertices),
        (shape((WIDTH, quarter * TILE)), shape((groups * splits, 2, LANES))),
        [vmem] * (2 + splits),
        name="last_quarter",
    )(inv_root, inverse, *pieces)
    grams = lax.all_to_all(
        grams, ("rows", "cols"), split_axis=0, concat_axis=0, tiled=True
    )
    return call(finish_kernel, shape((WIDTH, quarter * TILE)), [vmem, vmem], name="finish")(
        grams, image
    )


def solution(mesh):
    in_specs = (
        P("rows", "cols", None, None, None),
        P("rows", "cols", None, None, None),
        P("rows", "cols", None, None),
        P("rows", "cols", None, None, None),
        P("rows", "cols", None, None, None),
        P("rows", "cols", None),
        P("rows", "cols", None, None),
        P(None, "rows"),
    )
    out_specs = P(None, ("rows", "cols"))
    return jax.shard_map(
        per_device, mesh=mesh, in_specs=in_specs, out_specs=out_specs, check_vma=False
    )
```

```python
import functools

import jax
import jax.numpy as jnp
from jax import lax
from jax.experimental import pallas as pl
from jax.experimental.pallas import tpu as pltpu
from jax.sharding import PartitionSpec as P

TILE = 256
WIDTH = 16
BR = 16
MOST = 2
CHUNK = 8
HEAD = 8
LANES = 128
F32 = jnp.float32
BF16 = jnp.bfloat16
HIGHEST = lax.Precision.HIGHEST
VMEM_LIMIT = 16 * 1024 * 1024

vmem = pl.BlockSpec(memory_space=pltpu.VMEM)
hbm = pl.BlockSpec(memory_space=pltpu.HBM)
anywhere = pl.BlockSpec(memory_space=pl.ANY)


def shape(dims, dtype=F32):
    return jax.ShapeDtypeStruct(dims, dtype)


def call(kernel, out_shape, in_specs, scratch_shapes=(), flops=10**6, moved=10**6, name=None):
    return pl.pallas_call(
        kernel,
        out_shape=out_shape,
        in_specs=in_specs,
        out_specs=jax.tree.map(lambda _: vmem, out_shape),
        scratch_shapes=scratch_shapes,
        cost_estimate=pl.CostEstimate(flops=flops, bytes_accessed=moved, transcendentals=0),
        compiler_params=pltpu.CompilerParams(vmem_limit_bytes=VMEM_LIMIT),
        name=name,
    )


def times(left, right):
    return lax.dot_general(left, right, (((1,), (0,)), ((), ())), preferred_element_type=F32)


def times_t(left, right):
    return lax.dot_general(left, right, (((1,), (1,)), ((), ())), preferred_element_type=F32)


def in_hbm(value):
    return pltpu.with_memory_space_constraint(value, pltpu.HBM)


def fetch(sources, targets, sems):
    copies = [
        pltpu.make_async_copy(source, target, sems.at[n])
        for n, (source, target) in enumerate(zip(sources, targets))
    ]
    for copy in copies:
        copy.start()

    def wait():
        for copy in copies:
            copy.wait()

    return wait


def slots_of(groups_ref, count_ref, tile_count, group_count):
    for g in range(group_count):
        count_ref[g] = 0
    for t in range(tile_count):
        g = groups_ref[0, 0, t]
        m = count_ref[g]
        count_ref[g] = m + 1
        yield t, g, m


def weighted_sums(size, gains):
    sub = lax.broadcasted_iota(jnp.int32, (8, TILE), 0)
    gains = jnp.abs(gains)
    left = jnp.where(sub == 0, gains[0:1, :], jnp.where(sub == 1, gains[1:2, :], 0.0))
    high = left.astype(BF16).astype(F32)
    halves = jnp.concatenate([high, left - high], axis=0).astype(BF16)
    rows, cols = times_t(halves, size), times(halves, size)
    return (rows[1:2] + rows[9:10]) * gains[0:1, :], (cols[0:1] + cols[8:9]) * gains[1:2, :]


def remote_degree_kernel(weights, gains, groups, coords, near_weights, row_degree, tiles, held, *refs):
    *outs, tile_gains, tile_groups, tile_coords, staged, count, sems = refs
    group_count = staged.shape[0]
    wait = fetch(
        (groups, coords, gains, weights.at[0, 0]),
        (tile_groups, tile_coords, tile_gains, tiles),
        sems.at[pl.ds(0, 4)],
    )
    wait_held = fetch(
        (near_weights.at[0, 0, pl.ds(0, held.shape[0])],), (held,), sems.at[pl.ds(4, 1)]
    )
    sub = lax.broadcasted_iota(jnp.int32, (8, TILE), 0)
    blank = jnp.where((sub >= MOST) & (sub < 2 * MOST), -1.0, 0.0).astype(F32)
    for g in range(group_count):
        staged[g] = blank
    row_degree[...] = jnp.zeros(row_degree.shape, F32)
    core = lax.axis_index("rows") % 2
    wait()
    for t, g, m in slots_of(tile_groups, count, tiles.shape[0], group_count):
        place = place_of(g, group_count, core)
        r, c = tile_coords[0, 0, 0, t], tile_coords[0, 0, 1, t]
        by_row, by_col = weighted_sums(jnp.abs(tiles[t]), tile_gains[0, 0, t])
        row_degree[pl.ds(r, 1), :] += by_row
        staged[place, pl.ds(m, 1), :] = by_col
        staged[place, pl.ds(MOST + m, 1), :] = jnp.full((1, TILE), c, jnp.int32).astype(F32)
    split_out(staged, outs)
    wait_held()


def halves_of(value):
    high = value.astype(BF16)
    return high, (value - high.astype(F32)).astype(BF16)


def add_by_place(places, values):
    shape = (BR, places.shape[1])
    chosen = (lax.broadcasted_iota(jnp.int32, shape, 0) == places).astype(BF16)
    high, low = halves_of(values)
    return times(chosen, high) + times(chosen, low)


def local_degree_kernel(
    held, weights, gains, coords, degree, tiles, by_row, by_col, sems
):
    first, count = held.shape[0], weights.shape[2]

    def copy_of(n):
        source = weights.at[0, 0, pl.ds(first + n * CHUNK, CHUNK)]
        return pltpu.make_async_copy(source, tiles.at[pl.ds(n * CHUNK, CHUNK)], sems.at[n])

    for n in range((count - first) // CHUNK):
        copy_of(n).start()
    by_row[...] = jnp.zeros(by_row.shape, F32)
    top = lax.broadcasted_iota(jnp.int32, (8, TILE), 0) == 0
    lane = lax.broadcasted_iota(jnp.int32, by_row.shape, 1)

    def add(t, size):
        pair = jnp.abs(gains[0, 0, t])
        left = jnp.where(top, pair[0:1, :], 0.0)
        high = left.astype(BF16).astype(F32)
        sums = times(jnp.concatenate([high, left - high], axis=0).astype(BF16), size)
        by_col[pl.ds(t, 1), :] = (sums[0:1] + sums[8:9]) * pair[1:2, :]
        sums = jnp.sum(size.astype(F32) * pair[1:2, :], axis=1, keepdims=True)
        by_row[...] = jnp.where(lane == t, sums, by_row[...])

    def held_step(n, _):
        for k in range(CHUNK):
            add(n * CHUNK + k, jnp.abs(held[n * CHUNK + k]))
        return 0

    def step(n, _):
        copy_of(n).wait()
        for k in range(CHUNK):
            add(first + n * CHUNK + k, jnp.abs(tiles[n * CHUNK + k]))
        return 0

    lax.fori_loop(0, first // CHUNK, held_step, 0)
    lax.fori_loop(0, (count - first) // CHUNK, step, 0)
    row_sums = jnp.transpose(by_row[...])[:count] * jnp.abs(gains[0, 0, :, 0, :])
    degree[...] = add_by_place(coords[0, 0, 0:1, :], row_sums) + add_by_place(
        coords[0, 0, 1:2, :], by_col[...]
    )


def scale_kernel(raw, gains, scaled):
    def step(n, _):
        base = n * CHUNK
        row_gain = jnp.transpose(gains[0, 0, pl.ds(base, CHUNK), 0, :])
        for k in range(CHUNK):
            scaled[base + k] = (
                row_gain[:, k : k + 1]
                * raw[base + k].astype(F32)
                * gains[0, 0, base + k, 1:2, :]
            ).astype(BF16)
        return 0

    lax.fori_loop(0, scaled.shape[0] // CHUNK, step, 0)


def scale(raw, gains, name):
    return call(
        scale_kernel, shape(raw.shape, BF16), [vmem, vmem], flops=2 * raw.size, name=name
    )(raw, gains)


def join_degree_kernel(row_degree, local_degree, *refs):
    *arrived, joined, targets, sums = refs
    by_group(arrived, sums)
    targets[...] = sums[...].astype(jnp.int32)
    total = row_degree[...] + local_degree[...]
    sub = lax.broadcasted_iota(jnp.int32, total.shape, 0).astype(F32)
    for g in range(sums.shape[0]):
        block = sums[g]
        for m in range(MOST):
            hit = sub == block[MOST + m : MOST + m + 1, :]
            total += jnp.where(hit, block[m : m + 1, :], 0.0)
    joined[...] = total


def offsets(count):
    return [0] + list(range(count - 1, 0, -1))


def by_chips(groups):
    return groups // 2 <= 4


def place_of(group, group_count, core):
    if not by_chips(group_count):
        return group
    return ((group + core) % 2) * (group_count // 2) + group // 2


def outgoing(x, scaled, groups, coords, targets, staged, count, gram=None):
    group_count = staged.shape[0]
    core = lax.axis_index("rows") % 2
    for g in range(group_count):
        staged[g, MOST : 2 * MOST] = jnp.zeros((MOST, WIDTH, TILE), BF16)
        if gram is not None:
            staged[g, 2 * MOST] = gram
    for t, g, m in slots_of(groups, count, scaled.shape[0], group_count):
        place = place_of(g, group_count, core)
        staged[place, MOST + m] = times(x[coords[0, 0, 0, t]], scaled[t]).astype(BF16)
    for g in range(group_count):
        place = place_of(g, group_count, core)
        for m in range(MOST):
            staged[place, m] = x[jnp.maximum(targets[g, MOST + m, 0], 0)]


def split_out(staged, outs):
    size = outs[0].shape[0]
    for k, out in enumerate(outs):
        out[...] = staged[k * size : (k + 1) * size]


def forward_kernel(near, passed, *refs):
    chips = near.shape[0]
    pieces = refs[-chips:]
    me = lax.axis_index("rows")
    chip, core = me // 2, me % 2
    for k, piece in zip(offsets(chips), pieces):
        piece[core] = near[chip ^ k]
        piece[1 - core] = passed[chip ^ k]


def by_group(arrived, joined):
    if len(arrived) == 1:
        joined[...] = arrived[0][...]
        return
    chip = lax.axis_index("rows") // 2
    for k, piece in zip(offsets(len(arrived)), arrived):
        joined[pl.ds((chip ^ k) * 2, 2)] = piece[...]


def first_block_kernel(splits, start, scaled, groups, coords, targets, later, *refs):
    parts, (inv_root, x, *refs) = refs[:splits], refs[splits:]
    *outs, count, staged = refs
    routes = (groups, coords, targets)
    degree = parts[0][...]
    for part in parts[1:]:
        degree += part[...]
    inv = 1.0 / jnp.sqrt(degree)
    inv_root[...] = inv
    for k in range(BR):
        x[k] = (start[:, k * TILE : (k + 1) * TILE] * inv[k : k + 1, :]).astype(BF16)
    outgoing(x, scaled, *routes, staged, count)
    split_out(staged, outs)


def pair_sum_kernel(mine, theirs, total, sent):
    value = mine[...] + theirs[...].astype(F32)
    total[...] = value
    sent[...] = value.astype(BF16)


def next_block_kernel(
    vertices, scaled, inv_root, groups, coords, targets, mine, theirs, x, *refs
):
    *outs, count, staged = refs
    routes = (groups, coords, targets)
    gram = jnp.zeros((2 * WIDTH, 2 * WIDTH), F32)
    for k in range(BR):
        value = mine[k] + theirs[k].astype(F32)
        root = inv_root[k : k + 1, :]
        image = value * root
        x[k] = (image * root).astype(BF16)
        high = image.astype(BF16)
        halves = jnp.concatenate([high, (image - high.astype(F32)).astype(BF16)], axis=0)
        gram += times_t(halves, halves)
    low = gram[:WIDTH, WIDTH:] + gram[WIDTH:, :WIDTH] + gram[WIDTH:, WIDTH:]
    gram = (gram[:WIDTH, :WIDTH] + low) / vertices
    high = gram.astype(BF16)
    middle = (gram - high.astype(F32)).astype(BF16)
    low = (gram - high.astype(F32) - middle.astype(F32)).astype(BF16)
    block = jnp.concatenate(
        [high, middle, low, jnp.zeros((WIDTH, TILE - 3 * WIDTH), BF16)], axis=1
    )
    outgoing(x, scaled, *routes, staged, count, block)
    split_out(staged, outs)


def local_products_kernel(first, x, tiles, coords, *refs):
    *refs, partial, tile_coords, sems = refs
    gains, earlier = refs or (None, None)
    count = tiles.shape[0]
    batch = next(size for size in (20, 16, CHUNK) if count % size == 0)
    wait = fetch((coords,), (tile_coords,), sems)
    partial[...] = earlier[...] if refs else jnp.zeros(partial.shape, F32)
    wait()

    def step(n, _):
        base = first + n * batch
        if refs:
            row_gains = [
                jnp.transpose(gains[0, 0, pl.ds(base + k, min(CHUNK, batch - k)), 0, :])
                for k in range(0, batch, CHUNK)
            ]
        places, results = [], []
        for k in range(batch):
            t = base + k
            r, c = tile_coords[0, 0, 0, t], tile_coords[0, 0, 1, t]
            tile = tiles[n * batch + k]
            if refs:
                row_gain = row_gains[k // CHUNK][:, k % CHUNK : k % CHUNK + 1]
                tile = (row_gain * tile.astype(F32) * gains[0, 0, t, 1:2, :]).astype(BF16)
            results.append((times_t(x[c], tile), times(x[r], tile)))
            places.append((r, c))
        for (r, c), (forward, backward) in zip(places, results):
            partial[r] += forward
            partial[c] += backward
        return 0

    lax.fori_loop(0, count // batch, step, 0)


def remote_products_kernel(splits, whole, pieces, scaled, partial, groups, coords, targets, *refs):
    arrived, refs = refs[:pieces], refs[pieces:]
    *outs, total, count, joined = refs
    group_count = joined.shape[0]
    by_group(arrived, joined)
    total[...] = partial[...]
    for t, g, m in slots_of(groups, count, scaled.shape[0], group_count):
        total[coords[0, 0, 0, t]] += times_t(joined[g, m], scaled[t])
    for g in range(group_count):
        for m in range(MOST):
            total[jnp.maximum(targets[g, MOST + m, 0], 0)] += joined[g, MOST + m].astype(F32)
    if whole:
        for out in outs:
            out[...] = total[...].astype(out.dtype)
        return
    me = lax.axis_index("cols")
    quarter = BR // splits
    for k, out in zip(offsets(splits), outs):
        base = pl.multiple_of((me ^ k) * quarter, quarter)
        out[...] = total[pl.ds(base, quarter)].astype(out.dtype)


def quarter_sum(pieces, inv_root, me):
    quarter = pieces[0].shape[0]
    images, roots = [], []
    for k in range(quarter):
        value = pieces[0][k]
        for piece in pieces[1:]:
            value += piece[k].astype(F32)
        root = inv_root[pl.ds(me * quarter + k, 1), :]
        images.append(value * root)
        roots.append(root)
    return images, roots


def eliminate(gram, right):
    shape = (WIDTH, LANES)
    row = lax.broadcasted_iota(jnp.int32, shape, 0)
    columns = [jnp.broadcast_to(gram[:, k : k + 1], shape) for k in range(WIDTH)]
    pivots = jnp.zeros(shape, F32)
    for k in range(WIDTH):
        pivot = columns[k][k : k + 1]
        pivots = jnp.where(row == k, pivot, pivots)
        factor = jnp.where(row > k, columns[k] * (1.0 / pivot), 0.0)
        for n in range(k + 1, WIDTH):
            columns[n] = columns[n] - factor * columns[n][k : k + 1]
        right = [block - factor * block[k : k + 1] for block in right]
    root = 1.0 / jnp.sqrt(pivots)
    return [block * root for block in right]


def middle_factor_kernel(*refs):
    *arrived, inverse = refs
    gram = jnp.zeros((WIDTH, WIDTH), F32)
    for block in [piece[g, 2 * MOST] for piece in arrived for g in range(piece.shape[0])]:
        block = block.astype(F32)
        gram += (block[:, 2 * WIDTH : 3 * WIDTH] + block[:, WIDTH : 2 * WIDTH]) + block[:, :WIDTH]
    eye = lax.broadcasted_iota(jnp.int32, (WIDTH, LANES), 0) == lax.broadcasted_iota(
        jnp.int32, (WIDTH, LANES), 1
    )
    (result,) = eliminate(gram, [eye.astype(F32)])
    inverse[...] = result[:, :WIDTH]


def last_quarter_kernel(splits, vertices, inv_root, inverse, *refs):
    pieces, (image_out, grams) = refs[:splits], refs[splits:]
    images, _ = quarter_sum(pieces, inv_root, lax.axis_index("cols"))
    first = inverse[...]
    gram = jnp.zeros((WIDTH, WIDTH), F32)
    for k, image in enumerate(images):
        value = jnp.dot(first, image, precision=HIGHEST, preferred_element_type=F32)
        image_out[:, k * TILE : (k + 1) * TILE] = value
        gram += lax.dot_general(
            value, value, (((1,), (1,)), ((), ())), precision=HIGHEST, preferred_element_type=F32
        )
    gram = gram / vertices
    block = jnp.concatenate([gram[2 * n : 2 * n + 2] for n in range(WIDTH // 2)], axis=1)
    for n in range(grams.shape[0]):
        grams[n] = block


def finish_kernel(grams, image, out):
    block = grams[0]
    for n in range(1, grams.shape[0]):
        block = block + grams[n]
    gram = jnp.concatenate(
        [block[:, WIDTH * n : WIDTH * (n + 1)] for n in range(WIDTH // 2)], axis=0
    )
    starts = range(0, out.shape[1], LANES)
    for n, block in zip(starts, eliminate(gram, [image[:, n : n + LANES] for n in starts])):
        out[:, n : n + LANES] = block


def per_device(
    local_weights,
    local_gains,
    local_coords,
    remote_weights,
    remote_gains,
    remote_groups,
    remote_coords,
    start_block,
):
    groups = lax.axis_size("rows")
    splits = lax.axis_size("cols")
    vertices = groups * BR * TILE
    quarter = BR // splits
    local_coords, remote_coords = jnp.swapaxes(local_coords, 2, 3), jnp.swapaxes(remote_coords, 2, 3)
    local_tiles, remote_tiles = local_weights.shape[2], remote_weights.shape[2]
    count = pltpu.SMEM((groups,), jnp.int32)

    partners = [2 * 2**k - 1 for k in range(splits.bit_length() - 1)]

    def swap(value, k):
        return lax.ppermute(value, "cols", [(j, j ^ k) for j in range(splits)])

    def trade(value):
        return lax.all_to_all(value, "rows", split_axis=0, concat_axis=0, tiled=True)

    def sent_blocks(block, dtype):
        if by_chips(groups):
            return (shape((groups // 2,) + block, dtype),) * 2
        return (shape((groups,) + block, dtype),)

    def exchange(sent, before=()):
        if not by_chips(groups):
            return [trade(sent[0])]
        near, far = sent
        passed = lax.ppermute(far, "rows", [(j, j ^ 1) for j in range(groups)])
        own, *others = call(
            forward_kernel,
            (shape((2,) + near.shape[1:], near.dtype),) * (groups // 2),
            [vmem, vmem] + [anywhere] * len(before),
            name="forward",
        )(near, passed, *before)
        return [own] + [
            lax.ppermute(piece, "rows", [(j, j ^ (2 * k)) for j in range(groups)])
            for k, piece in zip(offsets(groups // 2)[1:], others)
        ]

    listing = (remote_weights, remote_gains, remote_groups, remote_coords, local_weights)
    row_degree, remote_raw, held, *sent = call(
        remote_degree_kernel,
        (
            shape((BR, TILE)),
            shape((remote_tiles, TILE, TILE), BF16),
            shape((HEAD, TILE, TILE), BF16),
        )
        + sent_blocks((8, TILE), F32),
        [hbm] * len(listing),
        [
            pltpu.VMEM(remote_gains.shape, F32),
            pltpu.SMEM(remote_groups.shape, jnp.int32),
            pltpu.SMEM(remote_coords.shape, jnp.int32),
            pltpu.VMEM((groups, 8, TILE), F32),
            count,
            pltpu.SemaphoreType.DMA((5,)),
        ],
        name="remote_degree",
    )(*[in_hbm(value) for value in listing])
    sums_in = exchange(sent)
    local_degree, local_raw = call(
        local_degree_kernel,
        (shape((BR, TILE)), shape((local_tiles - HEAD, TILE, TILE), BF16)),
        [vmem, hbm, vmem, vmem],
        [
            pltpu.VMEM((TILE, -(-local_tiles // LANES) * LANES), F32),
            pltpu.VMEM((local_tiles, TILE), F32),
            pltpu.SemaphoreType.DMA(((local_tiles - HEAD) // CHUNK,)),
        ],
        moved=10**7,
        name="local_degree",
    )(held, in_hbm(local_weights), local_gains, local_coords)
    joined, targets = call(
        join_degree_kernel,
        (shape((BR, TILE)), shape((groups, 8, TILE), jnp.int32)),
        [vmem] * (2 + len(sums_in)),
        [pltpu.VMEM((groups, 8, TILE), F32)],
        name="join_degree",
    )(row_degree, local_degree, *sums_in)
    far_scalars = [remote_groups, remote_coords, targets]
    joined, remote_gains, local_gains = lax.optimization_barrier(
        (joined, remote_gains, local_gains)
    )
    degrees = [joined] + [swap(joined, k) for k in range(1, splits)]
    remote_scaled = scale(remote_raw, remote_gains, "remote_scale")
    local_scaled = scale(held, local_gains, "local_scale")

    def staging(blocks):
        return pltpu.VMEM((groups, blocks, WIDTH, TILE), BF16)

    inv_root, x, *sent = call(
        functools.partial(first_block_kernel, splits),
        (shape((BR, TILE)), shape((BR, WIDTH, TILE), BF16))
        + sent_blocks((2 * MOST, WIDTH, TILE), BF16),
        [vmem, vmem, vmem, vmem, vmem, anywhere] + [vmem] * splits,
        [count, staging(2 * MOST)],
        name="first_block",
    )(start_block, remote_scaled, *far_scalars, local_scaled, *degrees)

    def local_products(first, number, x, tiles, *more):
        return call(
            functools.partial(local_products_kernel, first),
            shape((BR, WIDTH, TILE)),
            [vmem, vmem, anywhere] + [vmem] * len(more),
            [
                pltpu.SMEM(local_coords.shape, jnp.int32),
                pltpu.SemaphoreType.DMA((1,)),
            ],
            flops=4 * number * TILE * TILE * WIDTH,
            moved=2 * number * TILE * TILE,
            name="local_products",
        )(x, tiles, local_coords, *more)

    def product(x, sent, out_shape, whole):
        partial = local_products(0, HEAD, x, local_scaled)
        arrived = exchange(sent, (partial,))
        partial = local_products(HEAD, local_tiles - HEAD, x, local_raw, local_gains, partial)
        return arrived, call(
            functools.partial(remote_products_kernel, splits, whole, len(arrived)),
            out_shape,
            [vmem, vmem, vmem, vmem, vmem] + [vmem] * len(arrived),
            [pltpu.VMEM((BR, WIDTH, TILE), F32), count, staging(sent[0].shape[1])],
            name="remote_products",
        )(remote_scaled, partial, *far_scalars, *arrived)

    _, (own, sent) = product(
        x, sent, (shape((BR, WIDTH, TILE)), shape((BR, WIDTH, TILE), BF16)), True
    )
    for k in partners[:-1]:
        own, sent = call(
            pair_sum_kernel,
            (shape((BR, WIDTH, TILE)), shape((BR, WIDTH, TILE), BF16)),
            [vmem, vmem],
            name="pair_sum",
        )(own, swap(sent, k))
    x, *sent = call(
        functools.partial(next_block_kernel, vertices),
        (shape((BR, WIDTH, TILE), BF16),) + sent_blocks((2 * MOST + 1, WIDTH, TILE), BF16),
        [vmem, vmem, vmem, vmem, vmem, vmem, vmem],
        [count, staging(2 * MOST + 1)],
        name="next_block",
    )(
        remote_scaled,
        inv_root,
        *far_scalars,
        own,
        swap(sent, partners[-1]),
    )
    arrived, sent = product(
        x,
        sent,
        tuple(shape((quarter, WIDTH, TILE), BF16 if k else F32) for k in range(splits)),
        False,
    )
    pieces = [sent[0]] + [swap(part, k) for k, part in zip(offsets(splits)[1:], sent[1:])]
    inverse = call(
        middle_factor_kernel,
        shape((WIDTH, WIDTH)),
        [vmem] * len(arrived),
        name="middle_factor",
    )(*arrived)
    image, grams = call(
        functools.partial(last_quarter_kernel, splits, vertices),
        (shape((WIDTH, quarter * TILE)), shape((groups * splits, 2, LANES))),
        [vmem] * (2 + splits),
        name="last_quarter",
    )(inv_root, inverse, *pieces)
    grams = lax.all_to_all(
        grams, ("rows", "cols"), split_axis=0, concat_axis=0, tiled=True
    )
    return call(finish_kernel, shape((WIDTH, quarter * TILE)), [vmem, vmem], name="finish")(
        grams, image
    )


def solution(mesh):
    in_specs = (
        P("rows", "cols", None, None, None),
        P("rows", "cols", None, None, None),
        P("rows", "cols", None, None),
        P("rows", "cols", None, None, None),
        P("rows", "cols", None, None, None),
        P("rows", "cols", None),
        P("rows", "cols", None, None),
        P(None, "rows"),
    )
    out_specs = P(None, ("rows", "cols"))
    return jax.shard_map(
        per_device, mesh=mesh, in_specs=in_specs, out_specs=out_specs, check_vma=False
    )
```

```python
import functools

import jax
import jax.numpy as jnp
from jax import lax
from jax.experimental import pallas as pl
from jax.experimental.pallas import tpu as pltpu
from jax.sharding import PartitionSpec as P

TILE = 256
WIDTH = 16
BR = 16
MOST = 2
CHUNK = 8
HEAD = 8
LANES = 128
F32 = jnp.float32
BF16 = jnp.bfloat16
HIGHEST = lax.Precision.HIGHEST
VMEM_LIMIT = 16 * 1024 * 1024

vmem = pl.BlockSpec(memory_space=pltpu.VMEM)
hbm = pl.BlockSpec(memory_space=pltpu.HBM)
anywhere = pl.BlockSpec(memory_space=pl.ANY)


def shape(dims, dtype=F32):
    return jax.ShapeDtypeStruct(dims, dtype)


def call(kernel, out_shape, in_specs, scratch_shapes=(), flops=10**6, moved=10**6, name=None):
    return pl.pallas_call(
        kernel,
        out_shape=out_shape,
        in_specs=in_specs,
        out_specs=jax.tree.map(lambda _: vmem, out_shape),
        scratch_shapes=scratch_shapes,
        cost_estimate=pl.CostEstimate(flops=flops, bytes_accessed=moved, transcendentals=0),
        compiler_params=pltpu.CompilerParams(vmem_limit_bytes=VMEM_LIMIT),
        name=name,
    )


def times(left, right):
    return lax.dot_general(left, right, (((1,), (0,)), ((), ())), preferred_element_type=F32)


def times_t(left, right):
    return lax.dot_general(left, right, (((1,), (1,)), ((), ())), preferred_element_type=F32)


def in_hbm(value):
    return pltpu.with_memory_space_constraint(value, pltpu.HBM)


def fetch(sources, targets, sems):
    copies = [
        pltpu.make_async_copy(source, target, sems.at[n])
        for n, (source, target) in enumerate(zip(sources, targets))
    ]
    for copy in copies:
        copy.start()

    def wait():
        for copy in copies:
            copy.wait()

    return wait


def slots_of(groups_ref, count_ref, tile_count, group_count):
    for g in range(group_count):
        count_ref[g] = 0
    for t in range(tile_count):
        g = groups_ref[0, 0, t]
        m = count_ref[g]
        count_ref[g] = m + 1
        yield t, g, m


def remote_degree_kernel(weights, gains, groups, coords, near_weights, tiles, held, *refs):
    *outs, tile_gains, tile_groups, tile_coords, staged, count, sems = refs
    group_count = staged.shape[0]
    wait = fetch(
        (groups, coords, gains, weights.at[0, 0]),
        (tile_groups, tile_coords, tile_gains, tiles),
        sems.at[pl.ds(0, 4)],
    )
    wait_held = fetch(
        (near_weights.at[0, 0, pl.ds(0, held.shape[0])],), (held,), sems.at[pl.ds(4, 1)]
    )
    sub = lax.broadcasted_iota(jnp.int32, (8, TILE), 0)
    blank = jnp.where((sub >= MOST) & (sub < 2 * MOST), -1.0, 0.0).astype(F32)
    for g in range(group_count):
        staged[g] = blank
    core = lax.axis_index("rows") % 2
    wait()
    for t, g, m in slots_of(tile_groups, count, tiles.shape[0], group_count):
        place = place_of(g, group_count, core)
        c = tile_coords[0, 0, 1, t]
        staged[place, pl.ds(m, 1), :] = column_sums(jnp.abs(tiles[t]), jnp.abs(tile_gains[0, 0, t]))
        staged[place, pl.ds(MOST + m, 1), :] = jnp.full((1, TILE), c, jnp.int32).astype(F32)
    split_out(staged, outs)
    wait_held()


def halves_of(value):
    high = value.astype(BF16)
    return high, (value - high.astype(F32)).astype(BF16)


def add_by_place(places, values):
    shape = (BR, places.shape[1])
    chosen = (lax.broadcasted_iota(jnp.int32, shape, 0) == places).astype(BF16)
    high, low = halves_of(values)
    return times(chosen, high) + times(chosen, low)


def column_sums(size, pair):
    top = lax.broadcasted_iota(jnp.int32, (8, TILE), 0) == 0
    left = jnp.where(top, pair[0:1, :], 0.0)
    high = left.astype(BF16).astype(F32)
    sums = times(jnp.concatenate([high, left - high], axis=0).astype(BF16), size)
    return (sums[0:1] + sums[8:9]) * pair[1:2, :]


def spread_row_sums(by_row, t, size, pair):
    sums = jnp.sum(size.astype(F32) * pair[1:2, :], axis=1, keepdims=True)
    lane = lax.broadcasted_iota(jnp.int32, by_row.shape, 1)
    by_row[...] = jnp.where(lane == t, sums, by_row[...])


def rows_by_place(by_row, gains, places):
    count = gains.shape[0]
    return add_by_place(places, jnp.transpose(by_row[...])[:count] * jnp.abs(gains))


def early_degree_kernel(
    remote, remote_gains, remote_coords, held, gains, coords, degree, remote_row, by_row, by_col
):
    remote_row[...] = jnp.zeros(remote_row.shape, F32)
    by_row[...] = jnp.zeros(by_row.shape, F32)

    def remote_step(n, _):
        for k in range(CHUNK):
            t = n * CHUNK + k
            pair = jnp.abs(remote_gains[0, 0, t])
            spread_row_sums(remote_row, t, jnp.abs(remote[t]), pair)
        return 0

    lax.fori_loop(0, remote.shape[0] // CHUNK, remote_step, 0)
    count = held.shape[0]
    for t in range(count):
        size, pair = jnp.abs(held[t]), jnp.abs(gains[0, 0, t])
        by_col[t : t + 1, :] = column_sums(size, pair)
        spread_row_sums(by_row, t, size, pair)
    degree[...] = (
        rows_by_place(remote_row, remote_gains[0, 0, :, 0, :], remote_coords[0, 0, 0:1, :])
        + rows_by_place(by_row, gains[0, 0, :count, 0, :], coords[0, 0, 0:1, :count])
        + add_by_place(coords[0, 0, 1:2, :count], by_col[...])
    )


def local_degree_kernel(first, weights, gains, coords, degree, tiles, by_row, by_col, sems):
    count = tiles.shape[0]

    def copy_of(n):
        source = weights.at[0, 0, pl.ds(first + n * CHUNK, CHUNK)]
        return pltpu.make_async_copy(source, tiles.at[pl.ds(n * CHUNK, CHUNK)], sems.at[n])

    for n in range(count // CHUNK):
        copy_of(n).start()
    by_row[...] = jnp.zeros(by_row.shape, F32)

    def step(n, _):
        copy_of(n).wait()
        for k in range(CHUNK):
            t = n * CHUNK + k
            size, pair = jnp.abs(tiles[t]), jnp.abs(gains[0, 0, first + t])
            by_col[pl.ds(t, 1), :] = column_sums(size, pair)
            spread_row_sums(by_row, t, size, pair)
        return 0

    lax.fori_loop(0, count // CHUNK, step, 0)
    degree[...] = rows_by_place(
        by_row, gains[0, 0, first:, 0, :], coords[0, 0, 0:1, first:]
    ) + add_by_place(coords[0, 0, 1:2, first:], by_col[...])


def scale_kernel(raw, gains, scaled):
    def step(n, _):
        base = n * CHUNK
        row_gain = jnp.transpose(gains[0, 0, pl.ds(base, CHUNK), 0, :])
        for k in range(CHUNK):
            scaled[base + k] = (
                row_gain[:, k : k + 1]
                * raw[base + k].astype(F32)
                * gains[0, 0, base + k, 1:2, :]
            ).astype(BF16)
        return 0

    lax.fori_loop(0, scaled.shape[0] // CHUNK, step, 0)


def scale(raw, gains, name):
    return call(
        scale_kernel, shape(raw.shape, BF16), [vmem, vmem], flops=2 * raw.size, name=name
    )(raw, gains)


def join_degree_kernel(early, late, *refs):
    *arrived, joined, targets, sums = refs
    by_group(arrived, sums)
    targets[...] = sums[...].astype(jnp.int32)
    total = early[...] + late[...]
    sub = lax.broadcasted_iota(jnp.int32, total.shape, 0).astype(F32)
    for g in range(sums.shape[0]):
        block = sums[g]
        for m in range(MOST):
            hit = sub == block[MOST + m : MOST + m + 1, :]
            total += jnp.where(hit, block[m : m + 1, :], 0.0)
    joined[...] = total


def offsets(count):
    return [0] + list(range(count - 1, 0, -1))


def by_chips(groups):
    return groups // 2 <= 4


def place_of(group, group_count, core):
    if not by_chips(group_count):
        return group
    return ((group + core) % 2) * (group_count // 2) + group // 2


def outgoing(x, scaled, groups, coords, targets, staged, count, gram=None):
    group_count = staged.shape[0]
    core = lax.axis_index("rows") % 2
    for g in range(group_count):
        staged[g, MOST : 2 * MOST] = jnp.zeros((MOST, WIDTH, TILE), BF16)
        if gram is not None:
            staged[g, 2 * MOST] = gram
    for t, g, m in slots_of(groups, count, scaled.shape[0], group_count):
        place = place_of(g, group_count, core)
        staged[place, MOST + m] = times(x[coords[0, 0, 0, t]], scaled[t]).astype(BF16)
    for g in range(group_count):
        place = place_of(g, group_count, core)
        for m in range(MOST):
            staged[place, m] = x[jnp.maximum(targets[g, MOST + m, 0], 0)]


def split_out(staged, outs):
    size = outs[0].shape[0]
    for k, out in enumerate(outs):
        out[...] = staged[k * size : (k + 1) * size]


def forward_kernel(near, passed, *refs):
    chips = near.shape[0]
    pieces = refs[-chips:]
    me = lax.axis_index("rows")
    chip, core = me // 2, me % 2
    for k, piece in zip(offsets(chips), pieces):
        piece[core] = near[chip ^ k]
        piece[1 - core] = passed[chip ^ k]


def by_group(arrived, joined):
    if len(arrived) == 1:
        joined[...] = arrived[0][...]
        return
    chip = lax.axis_index("rows") // 2
    for k, piece in zip(offsets(len(arrived)), arrived):
        joined[pl.ds((chip ^ k) * 2, 2)] = piece[...]


def first_block_kernel(splits, start, scaled, groups, coords, targets, later, *refs):
    parts, (inv_root, x, *refs) = refs[:splits], refs[splits:]
    *outs, count, staged = refs
    routes = (groups, coords, targets)
    degree = parts[0][...]
    for part in parts[1:]:
        degree += part[...]
    inv = 1.0 / jnp.sqrt(degree)
    inv_root[...] = inv
    for k in range(BR):
        x[k] = (start[:, k * TILE : (k + 1) * TILE] * inv[k : k + 1, :]).astype(BF16)
    outgoing(x, scaled, *routes, staged, count)
    split_out(staged, outs)


def pair_sum_kernel(mine, theirs, total, sent):
    value = mine[...] + theirs[...].astype(F32)
    total[...] = value
    sent[...] = value.astype(BF16)


def next_block_kernel(
    vertices, scaled, inv_root, groups, coords, targets, mine, theirs, x, *refs
):
    *outs, count, staged = refs
    routes = (groups, coords, targets)
    gram = jnp.zeros((2 * WIDTH, 2 * WIDTH), F32)
    for k in range(BR):
        value = mine[k] + theirs[k].astype(F32)
        root = inv_root[k : k + 1, :]
        image = value * root
        x[k] = (image * root).astype(BF16)
        high = image.astype(BF16)
        halves = jnp.concatenate([high, (image - high.astype(F32)).astype(BF16)], axis=0)
        gram += times_t(halves, halves)
    low = gram[:WIDTH, WIDTH:] + gram[WIDTH:, :WIDTH] + gram[WIDTH:, WIDTH:]
    gram = (gram[:WIDTH, :WIDTH] + low) / vertices
    high = gram.astype(BF16)
    middle = (gram - high.astype(F32)).astype(BF16)
    low = (gram - high.astype(F32) - middle.astype(F32)).astype(BF16)
    block = jnp.concatenate(
        [high, middle, low, jnp.zeros((WIDTH, TILE - 3 * WIDTH), BF16)], axis=1
    )
    outgoing(x, scaled, *routes, staged, count, block)
    split_out(staged, outs)


def local_products_kernel(first, x, tiles, coords, *refs):
    *refs, partial, tile_coords, sems = refs
    gains, earlier = refs or (None, None)
    count = tiles.shape[0]
    batch = next(size for size in (20, 16, CHUNK) if count % size == 0)
    wait = fetch((coords,), (tile_coords,), sems)
    partial[...] = earlier[...] if refs else jnp.zeros(partial.shape, F32)
    wait()

    def step(n, _):
        base = first + n * batch
        if refs:
            row_gains = [
                jnp.transpose(gains[0, 0, pl.ds(base + k, min(CHUNK, batch - k)), 0, :])
                for k in range(0, batch, CHUNK)
            ]
        places, results = [], []
        for k in range(batch):
            t = base + k
            r, c = tile_coords[0, 0, 0, t], tile_coords[0, 0, 1, t]
            tile = tiles[n * batch + k]
            if refs:
                row_gain = row_gains[k // CHUNK][:, k % CHUNK : k % CHUNK + 1]
                tile = (row_gain * tile.astype(F32) * gains[0, 0, t, 1:2, :]).astype(BF16)
            results.append((times_t(x[c], tile), times(x[r], tile)))
            places.append((r, c))
        for (r, c), (forward, backward) in zip(places, results):
            partial[r] += forward
            partial[c] += backward
        return 0

    lax.fori_loop(0, count // batch, step, 0)


def remote_products_kernel(splits, whole, pieces, scaled, partial, groups, coords, targets, *refs):
    arrived, refs = refs[:pieces], refs[pieces:]
    *outs, total, count, joined = refs
    group_count = joined.shape[0]
    by_group(arrived, joined)
    total[...] = partial[...]
    for t, g, m in slots_of(groups, count, scaled.shape[0], group_count):
        total[coords[0, 0, 0, t]] += times_t(joined[g, m], scaled[t])
    for g in range(group_count):
        for m in range(MOST):
            total[jnp.maximum(targets[g, MOST + m, 0], 0)] += joined[g, MOST + m].astype(F32)
    if whole:
        for out in outs:
            out[...] = total[...].astype(out.dtype)
        return
    me = lax.axis_index("cols")
    quarter = BR // splits
    for k, out in zip(offsets(splits), outs):
        base = pl.multiple_of((me ^ k) * quarter, quarter)
        out[...] = total[pl.ds(base, quarter)].astype(out.dtype)


def quarter_sum(pieces, inv_root, me):
    quarter = pieces[0].shape[0]
    images, roots = [], []
    for k in range(quarter):
        value = pieces[0][k]
        for piece in pieces[1:]:
            value += piece[k].astype(F32)
        root = inv_root[pl.ds(me * quarter + k, 1), :]
        images.append(value * root)
        roots.append(root)
    return images, roots


def eliminate(gram, right):
    shape = (WIDTH, LANES)
    row = lax.broadcasted_iota(jnp.int32, shape, 0)
    columns = [jnp.broadcast_to(gram[:, k : k + 1], shape) for k in range(WIDTH)]
    pivots = jnp.zeros(shape, F32)
    for k in range(WIDTH):
        pivot = columns[k][k : k + 1]
        pivots = jnp.where(row == k, pivot, pivots)
        factor = jnp.where(row > k, columns[k] * (1.0 / pivot), 0.0)
        for n in range(k + 1, WIDTH):
            columns[n] = columns[n] - factor * columns[n][k : k + 1]
        right = [block - factor * block[k : k + 1] for block in right]
    root = 1.0 / jnp.sqrt(pivots)
    return [block * root for block in right]


def middle_factor_kernel(*refs):
    *arrived, inverse = refs
    gram = jnp.zeros((WIDTH, WIDTH), F32)
    for block in [piece[g, 2 * MOST] for piece in arrived for g in range(piece.shape[0])]:
        block = block.astype(F32)
        gram += (block[:, 2 * WIDTH : 3 * WIDTH] + block[:, WIDTH : 2 * WIDTH]) + block[:, :WIDTH]
    eye = lax.broadcasted_iota(jnp.int32, (WIDTH, LANES), 0) == lax.broadcasted_iota(
        jnp.int32, (WIDTH, LANES), 1
    )
    (result,) = eliminate(gram, [eye.astype(F32)])
    inverse[...] = result[:, :WIDTH]


def last_quarter_kernel(splits, vertices, inv_root, inverse, *refs):
    pieces, (image_out, grams) = refs[:splits], refs[splits:]
    images, _ = quarter_sum(pieces, inv_root, lax.axis_index("cols"))
    image = jnp.dot(
        inverse[...], jnp.concatenate(images, axis=1), precision=HIGHEST, preferred_element_type=F32
    )
    image_out[...] = image
    gram = lax.dot_general(
        image, image, (((1,), (1,)), ((), ())), precision=HIGHEST, preferred_element_type=F32
    )
    gram = gram / vertices
    block = jnp.concatenate([gram[2 * n : 2 * n + 2] for n in range(WIDTH // 2)], axis=1)
    for n in range(grams.shape[0]):
        grams[n] = block


def finish_kernel(grams, image, out):
    block = grams[0]
    for n in range(1, grams.shape[0]):
        block = block + grams[n]
    gram = jnp.concatenate(
        [block[:, WIDTH * n : WIDTH * (n + 1)] for n in range(WIDTH // 2)], axis=0
    )
    starts = range(0, out.shape[1], LANES)
    for n, block in zip(starts, eliminate(gram, [image[:, n : n + LANES] for n in starts])):
        out[:, n : n + LANES] = block


def per_device(
    local_weights,
    local_gains,
    local_coords,
    remote_weights,
    remote_gains,
    remote_groups,
    remote_coords,
    start_block,
):
    groups = lax.axis_size("rows")
    splits = lax.axis_size("cols")
    vertices = groups * BR * TILE
    quarter = BR // splits
    local_coords, remote_coords = jnp.swapaxes(local_coords, 2, 3), jnp.swapaxes(remote_coords, 2, 3)
    local_tiles, remote_tiles = local_weights.shape[2], remote_weights.shape[2]
    count = pltpu.SMEM((groups,), jnp.int32)

    partners = [2 * 2**k - 1 for k in range(splits.bit_length() - 1)]

    def swap(value, k):
        return lax.ppermute(value, "cols", [(j, j ^ k) for j in range(splits)])

    def trade(value):
        return lax.all_to_all(value, "rows", split_axis=0, concat_axis=0, tiled=True)

    def sent_blocks(block, dtype):
        if by_chips(groups):
            return (shape((groups // 2,) + block, dtype),) * 2
        return (shape((groups,) + block, dtype),)

    def exchange(sent, before=()):
        if not by_chips(groups):
            return [trade(sent[0])]
        near, far = sent
        passed = lax.ppermute(far, "rows", [(j, j ^ 1) for j in range(groups)])
        own, *others = call(
            forward_kernel,
            (shape((2,) + near.shape[1:], near.dtype),) * (groups // 2),
            [vmem, vmem] + [anywhere] * len(before),
            name="forward",
        )(near, passed, *before)
        return [own] + [
            lax.ppermute(piece, "rows", [(j, j ^ (2 * k)) for j in range(groups)])
            for k, piece in zip(offsets(groups // 2)[1:], others)
        ]

    listing = (remote_weights, remote_gains, remote_groups, remote_coords, local_weights)
    remote_raw, held, *sent = call(
        remote_degree_kernel,
        (
            shape((remote_tiles, TILE, TILE), BF16),
            shape((HEAD, TILE, TILE), BF16),
        )
        + sent_blocks((8, TILE), F32),
        [hbm] * len(listing),
        [
            pltpu.VMEM(remote_gains.shape, F32),
            pltpu.SMEM(remote_groups.shape, jnp.int32),
            pltpu.SMEM(remote_coords.shape, jnp.int32),
            pltpu.VMEM((groups, 8, TILE), F32),
            count,
            pltpu.SemaphoreType.DMA((5,)),
        ],
        name="remote_degree",
    )(*[in_hbm(value) for value in listing])
    lanes = pltpu.VMEM((TILE, LANES), F32)
    early_degree = call(
        early_degree_kernel,
        shape((BR, TILE)),
        [vmem] * 6,
        [lanes, lanes, pltpu.VMEM((HEAD, TILE), F32)],
        name="early_degree",
    )(remote_raw, remote_gains, remote_coords, held, local_gains, local_coords)
    sums_in = exchange(sent, (early_degree,))
    late_degree, local_raw = call(
        functools.partial(local_degree_kernel, HEAD),
        (shape((BR, TILE)), shape((local_tiles - HEAD, TILE, TILE), BF16)),
        [hbm, vmem, vmem],
        [
            lanes,
            pltpu.VMEM((local_tiles - HEAD, TILE), F32),
            pltpu.SemaphoreType.DMA(((local_tiles - HEAD) // CHUNK,)),
        ],
        moved=10**7,
        name="local_degree",
    )(in_hbm(local_weights), local_gains, local_coords)
    joined, targets = call(
        join_degree_kernel,
        (shape((BR, TILE)), shape((groups, 8, TILE), jnp.int32)),
        [vmem] * (2 + len(sums_in)),
        [pltpu.VMEM((groups, 8, TILE), F32)],
        name="join_degree",
    )(early_degree, late_degree, *sums_in)
    far_scalars = [remote_groups, remote_coords, targets]
    joined, remote_gains, local_gains = lax.optimization_barrier(
        (joined, remote_gains, local_gains)
    )
    degrees = [joined] + [swap(joined, k) for k in range(1, splits)]
    remote_scaled = scale(remote_raw, remote_gains, "remote_scale")
    local_scaled = scale(held, local_gains, "local_scale")

    def staging(blocks):
        return pltpu.VMEM((groups, blocks, WIDTH, TILE), BF16)

    inv_root, x, *sent = call(
        functools.partial(first_block_kernel, splits),
        (shape((BR, TILE)), shape((BR, WIDTH, TILE), BF16))
        + sent_blocks((2 * MOST, WIDTH, TILE), BF16),
        [vmem, vmem, vmem, vmem, vmem, anywhere] + [vmem] * splits,
        [count, staging(2 * MOST)],
        name="first_block",
    )(start_block, remote_scaled, *far_scalars, local_scaled, *degrees)

    def local_products(first, number, x, tiles, *more):
        return call(
            functools.partial(local_products_kernel, first),
            shape((BR, WIDTH, TILE)),
            [vmem, vmem, anywhere] + [vmem] * len(more),
            [
                pltpu.SMEM(local_coords.shape, jnp.int32),
                pltpu.SemaphoreType.DMA((1,)),
            ],
            flops=4 * number * TILE * TILE * WIDTH,
            moved=2 * number * TILE * TILE,
            name="local_products",
        )(x, tiles, local_coords, *more)

    def product(x, sent, out_shape, whole):
        partial = local_products(0, HEAD, x, local_scaled)
        arrived = exchange(sent, (partial,))
        partial = local_products(HEAD, local_tiles - HEAD, x, local_raw, local_gains, partial)
        return arrived, call(
            functools.partial(remote_products_kernel, splits, whole, len(arrived)),
            out_shape,
            [vmem, vmem, vmem, vmem, vmem] + [vmem] * len(arrived),
            [pltpu.VMEM((BR, WIDTH, TILE), F32), count, staging(sent[0].shape[1])],
            name="remote_products",
        )(remote_scaled, partial, *far_scalars, *arrived)

    _, (own, sent) = product(
        x, sent, (shape((BR, WIDTH, TILE)), shape((BR, WIDTH, TILE), BF16)), True
    )
    for k in partners[:-1]:
        own, sent = call(
            pair_sum_kernel,
            (shape((BR, WIDTH, TILE)), shape((BR, WIDTH, TILE), BF16)),
            [vmem, vmem],
            name="pair_sum",
        )(own, swap(sent, k))
    x, *sent = call(
        functools.partial(next_block_kernel, vertices),
        (shape((BR, WIDTH, TILE), BF16),) + sent_blocks((2 * MOST + 1, WIDTH, TILE), BF16),
        [vmem, vmem, vmem, vmem, vmem, vmem, vmem],
        [count, staging(2 * MOST + 1)],
        name="next_block",
    )(
        remote_scaled,
        inv_root,
        *far_scalars,
        own,
        swap(sent, partners[-1]),
    )
    arrived, sent = product(
        x,
        sent,
        tuple(shape((quarter, WIDTH, TILE), BF16 if k else F32) for k in range(splits)),
        False,
    )
    pieces = [sent[0]] + [swap(part, k) for k, part in zip(offsets(splits)[1:], sent[1:])]
    inverse = call(
        middle_factor_kernel,
        shape((WIDTH, WIDTH)),
        [vmem] * len(arrived),
        name="middle_factor",
    )(*arrived)
    image, grams = call(
        functools.partial(last_quarter_kernel, splits, vertices),
        (shape((WIDTH, quarter * TILE)), shape((groups * splits, 2, LANES))),
        [vmem] * (2 + splits),
        name="last_quarter",
    )(inv_root, inverse, *pieces)
    grams = lax.all_to_all(
        grams, ("rows", "cols"), split_axis=0, concat_axis=0, tiled=True
    )
    return call(finish_kernel, shape((WIDTH, quarter * TILE)), [vmem, vmem], name="finish")(
        grams, image
    )


def solution(mesh):
    in_specs = (
        P("rows", "cols", None, None, None),
        P("rows", "cols", None, None, None),
        P("rows", "cols", None, None),
        P("rows", "cols", None, None, None),
        P("rows", "cols", None, None, None),
        P("rows", "cols", None),
        P("rows", "cols", None, None),
        P(None, "rows"),
    )
    out_specs = P(None, ("rows", "cols"))
    return jax.shard_map(
        per_device, mesh=mesh, in_specs=in_specs, out_specs=out_specs, check_vma=False
    )
```

```python
import functools

import jax
import jax.numpy as jnp
from jax import lax
from jax.experimental import pallas as pl
from jax.experimental.pallas import tpu as pltpu
from jax.sharding import PartitionSpec as P

TILE = 256
WIDTH = 16
BR = 16
MOST = 2
CHUNK = 8
HEAD = 8
LANES = 128
F32 = jnp.float32
BF16 = jnp.bfloat16
HIGHEST = lax.Precision.HIGHEST
VMEM_LIMIT = 16 * 1024 * 1024

vmem = pl.BlockSpec(memory_space=pltpu.VMEM)
hbm = pl.BlockSpec(memory_space=pltpu.HBM)
anywhere = pl.BlockSpec(memory_space=pl.ANY)


def shape(dims, dtype=F32):
    return jax.ShapeDtypeStruct(dims, dtype)


def call(kernel, out_shape, in_specs, scratch_shapes=(), flops=10**6, moved=10**6, name=None):
    return pl.pallas_call(
        kernel,
        out_shape=out_shape,
        in_specs=in_specs,
        out_specs=jax.tree.map(lambda _: vmem, out_shape),
        scratch_shapes=scratch_shapes,
        cost_estimate=pl.CostEstimate(flops=flops, bytes_accessed=moved, transcendentals=0),
        compiler_params=pltpu.CompilerParams(vmem_limit_bytes=VMEM_LIMIT),
        name=name,
    )


def times(left, right):
    return lax.dot_general(left, right, (((1,), (0,)), ((), ())), preferred_element_type=F32)


def times_t(left, right):
    return lax.dot_general(left, right, (((1,), (1,)), ((), ())), preferred_element_type=F32)


def in_hbm(value):
    return pltpu.with_memory_space_constraint(value, pltpu.HBM)


def fetch(sources, targets, sems):
    copies = [
        pltpu.make_async_copy(source, target, sems.at[n])
        for n, (source, target) in enumerate(zip(sources, targets))
    ]
    for copy in copies:
        copy.start()

    def wait():
        for copy in copies:
            copy.wait()

    return wait


def slots_of(groups_ref, count_ref, tile_count, group_count):
    for g in range(group_count):
        count_ref[g] = 0
    for t in range(tile_count):
        g = groups_ref[0, 0, t]
        m = count_ref[g]
        count_ref[g] = m + 1
        yield t, g, m


def remote_degree_kernel(weights, gains, groups, coords, near_weights, tiles, held, *refs):
    *outs, tile_gains, tile_groups, tile_coords, staged, count, sems = refs
    group_count = staged.shape[0]
    wait = fetch(
        (groups, coords, gains, weights.at[0, 0]),
        (tile_groups, tile_coords, tile_gains, tiles),
        sems.at[pl.ds(0, 4)],
    )
    wait_held = fetch(
        (near_weights.at[0, 0, pl.ds(0, held.shape[0])],), (held,), sems.at[pl.ds(4, 1)]
    )
    sub = lax.broadcasted_iota(jnp.int32, (8, TILE), 0)
    blank = jnp.where((sub >= MOST) & (sub < 2 * MOST), -1.0, 0.0).astype(F32)
    for g in range(group_count):
        staged[g] = blank
    core = lax.axis_index("rows") % 2
    wait()
    for t, g, m in slots_of(tile_groups, count, tiles.shape[0], group_count):
        place = place_of(g, group_count, core)
        c = tile_coords[0, 0, 1, t]
        staged[place, pl.ds(m, 1), :] = column_sums(jnp.abs(tiles[t]), jnp.abs(tile_gains[0, 0, t]))
        staged[place, pl.ds(MOST + m, 1), :] = jnp.full((1, TILE), c, jnp.int32).astype(F32)
    split_out(staged, outs)
    wait_held()


def halves_of(value):
    high = value.astype(BF16)
    return high, (value - high.astype(F32)).astype(BF16)


def add_by_place(places, values):
    shape = (BR, places.shape[1])
    chosen = (lax.broadcasted_iota(jnp.int32, shape, 0) == places).astype(BF16)
    high, low = halves_of(values)
    return times(chosen, high) + times(chosen, low)


def column_sums(size, pair):
    top = lax.broadcasted_iota(jnp.int32, (8, TILE), 0) == 0
    left = jnp.where(top, pair[0:1, :], 0.0)
    high = left.astype(BF16).astype(F32)
    sums = times(jnp.concatenate([high, left - high], axis=0).astype(BF16), size)
    return (sums[0:1] + sums[8:9]) * pair[1:2, :]


def spread_row_sums(by_row, t, size, pair):
    sums = jnp.sum(size.astype(F32) * pair[1:2, :], axis=1, keepdims=True)
    lane = lax.broadcasted_iota(jnp.int32, by_row.shape, 1)
    by_row[...] = jnp.where(lane == t, sums, by_row[...])


def rows_by_place(by_row, gains, places):
    count = gains.shape[0]
    return add_by_place(places, jnp.transpose(by_row[...])[:count] * jnp.abs(gains))


def early_degree_kernel(
    remote, remote_gains, remote_coords, held, gains, coords, degree, remote_row, by_row, by_col
):
    remote_row[...] = jnp.zeros(remote_row.shape, F32)
    by_row[...] = jnp.zeros(by_row.shape, F32)

    def remote_step(n, _):
        for k in range(CHUNK):
            t = n * CHUNK + k
            pair = jnp.abs(remote_gains[0, 0, t])
            spread_row_sums(remote_row, t, jnp.abs(remote[t]), pair)
        return 0

    lax.fori_loop(0, remote.shape[0] // CHUNK, remote_step, 0)
    count = held.shape[0]
    for t in range(count):
        size, pair = jnp.abs(held[t]), jnp.abs(gains[0, 0, t])
        by_col[t : t + 1, :] = column_sums(size, pair)
        spread_row_sums(by_row, t, size, pair)
    degree[...] = (
        rows_by_place(remote_row, remote_gains[0, 0, :, 0, :], remote_coords[0, 0, 0:1, :])
        + rows_by_place(by_row, gains[0, 0, :count, 0, :], coords[0, 0, 0:1, :count])
        + add_by_place(coords[0, 0, 1:2, :count], by_col[...])
    )


def local_degree_kernel(first, weights, gains, coords, degree, tiles, by_row, by_col, sems):
    count = tiles.shape[0]

    def copy_of(n):
        source = weights.at[0, 0, pl.ds(first + n * CHUNK, CHUNK)]
        return pltpu.make_async_copy(source, tiles.at[pl.ds(n * CHUNK, CHUNK)], sems.at[n])

    for n in range(count // CHUNK):
        copy_of(n).start()
    by_row[...] = jnp.zeros(by_row.shape, F32)

    def step(n, _):
        copy_of(n).wait()
        for k in range(CHUNK):
            t = n * CHUNK + k
            size, pair = jnp.abs(tiles[t]), jnp.abs(gains[0, 0, first + t])
            by_col[pl.ds(t, 1), :] = column_sums(size, pair)
            spread_row_sums(by_row, t, size, pair)
        return 0

    lax.fori_loop(0, count // CHUNK, step, 0)
    degree[...] = rows_by_place(
        by_row, gains[0, 0, first:, 0, :], coords[0, 0, 0:1, first:]
    ) + add_by_place(coords[0, 0, 1:2, first:], by_col[...])


def scale_kernel(raw, gains, scaled):
    def step(n, _):
        base = n * CHUNK
        row_gain = jnp.transpose(gains[0, 0, pl.ds(base, CHUNK), 0, :])
        for k in range(CHUNK):
            scaled[base + k] = (
                row_gain[:, k : k + 1]
                * raw[base + k].astype(F32)
                * gains[0, 0, base + k, 1:2, :]
            ).astype(BF16)
        return 0

    lax.fori_loop(0, scaled.shape[0] // CHUNK, step, 0)


def scale(raw, gains, name):
    return call(
        scale_kernel, shape(raw.shape, BF16), [vmem, vmem], flops=2 * raw.size, name=name
    )(raw, gains)


def join_degree_kernel(early, late, *refs):
    *arrived, joined, targets, sums = refs
    by_group(arrived, sums)
    targets[...] = sums[...].astype(jnp.int32)
    total = early[...] + late[...]
    sub = lax.broadcasted_iota(jnp.int32, total.shape, 0).astype(F32)
    for g in range(sums.shape[0]):
        block = sums[g]
        for m in range(MOST):
            hit = sub == block[MOST + m : MOST + m + 1, :]
            total += jnp.where(hit, block[m : m + 1, :], 0.0)
    joined[...] = total


def offsets(count):
    return [0] + list(range(count - 1, 0, -1))


def by_chips(groups):
    return groups // 2 <= 4


def place_of(group, group_count, core):
    if not by_chips(group_count):
        return group
    return ((group + core) % 2) * (group_count // 2) + group // 2


def outgoing(x, scaled, groups, coords, targets, staged, count, gram=None):
    group_count = staged.shape[0]
    core = lax.axis_index("rows") % 2
    for g in range(group_count):
        staged[g, MOST : 2 * MOST] = jnp.zeros((MOST, WIDTH, TILE), BF16)
        if gram is not None:
            staged[g, 2 * MOST] = gram
    for t, g, m in slots_of(groups, count, scaled.shape[0], group_count):
        place = place_of(g, group_count, core)
        staged[place, MOST + m] = times(x[coords[0, 0, 0, t]], scaled[t]).astype(BF16)
    for g in range(group_count):
        place = place_of(g, group_count, core)
        for m in range(MOST):
            staged[place, m] = x[jnp.maximum(targets[g, MOST + m, 0], 0)]


def split_out(staged, outs):
    size = outs[0].shape[0]
    for k, out in enumerate(outs):
        out[...] = staged[k * size : (k + 1) * size]


def forward_kernel(near, passed, *refs):
    chips = near.shape[0]
    pieces = refs[-chips:]
    me = lax.axis_index("rows")
    chip, core = me // 2, me % 2
    for k, piece in zip(offsets(chips), pieces):
        piece[core] = near[chip ^ k]
        piece[1 - core] = passed[chip ^ k]


def by_group(arrived, joined):
    if len(arrived) == 1:
        joined[...] = arrived[0][...]
        return
    chip = lax.axis_index("rows") // 2
    for k, piece in zip(offsets(len(arrived)), arrived):
        joined[pl.ds((chip ^ k) * 2, 2)] = piece[...]


def first_block_kernel(splits, start, scaled, groups, coords, targets, later, *refs):
    parts, (inv_root, x, *refs) = refs[:splits], refs[splits:]
    *outs, count, staged = refs
    routes = (groups, coords, targets)
    degree = parts[0][...]
    for part in parts[1:]:
        degree += part[...]
    inv = 1.0 / jnp.sqrt(degree)
    inv_root[...] = inv
    for k in range(BR):
        x[k] = (start[:, k * TILE : (k + 1) * TILE] * inv[k : k + 1, :]).astype(BF16)
    outgoing(x, scaled, *routes, staged, count)
    split_out(staged, outs)


def pair_sum_kernel(mine, theirs, total, sent):
    value = mine[...] + theirs[...].astype(F32)
    total[...] = value
    sent[...] = value.astype(BF16)


def next_block_kernel(
    vertices, scaled, inv_root, groups, coords, targets, mine, theirs, x, *refs
):
    *outs, count, staged = refs
    routes = (groups, coords, targets)
    gram = jnp.zeros((2 * WIDTH, 2 * WIDTH), F32)
    for k in range(BR):
        value = mine[k] + theirs[k].astype(F32)
        root = inv_root[k : k + 1, :]
        image = value * root
        x[k] = (image * root).astype(BF16)
        high = image.astype(BF16)
        halves = jnp.concatenate([high, (image - high.astype(F32)).astype(BF16)], axis=0)
        gram += times_t(halves, halves)
    low = gram[:WIDTH, WIDTH:] + gram[WIDTH:, :WIDTH] + gram[WIDTH:, WIDTH:]
    gram = (gram[:WIDTH, :WIDTH] + low) / vertices
    high = gram.astype(BF16)
    middle = (gram - high.astype(F32)).astype(BF16)
    low = (gram - high.astype(F32) - middle.astype(F32)).astype(BF16)
    block = jnp.concatenate(
        [high, middle, low, jnp.zeros((WIDTH, TILE - 3 * WIDTH), BF16)], axis=1
    )
    outgoing(x, scaled, *routes, staged, count, block)
    split_out(staged, outs)


def local_products_kernel(first, x, tiles, coords, *refs):
    *refs, partial, table = refs
    gains, earlier = refs or (None, None)
    count = tiles.shape[0]
    batch = next(size for size in (20, 16, CHUNK) if count % size == 0)
    partial[...] = earlier[...] if refs else jnp.zeros(partial.shape, F32)
    for t in range(first, first + count):
        for side in range(2):
            table[side, t] = coords[0, 0, side, t]

    def step(n, _):
        base = first + n * batch
        if refs:
            row_gains = [
                jnp.transpose(gains[0, 0, pl.ds(base + k, min(CHUNK, batch - k)), 0, :])
                for k in range(0, batch, CHUNK)
            ]
        places, results = [], []
        for k in range(batch):
            t = base + k
            r, c = table[0, t], table[1, t]
            tile = tiles[n * batch + k]
            if refs:
                row_gain = row_gains[k // CHUNK][:, k % CHUNK : k % CHUNK + 1]
                tile = (row_gain * tile.astype(F32) * gains[0, 0, t, 1:2, :]).astype(BF16)
            results.append((times_t(x[c], tile), times(x[r], tile)))
            places.append((r, c))
        for (r, c), (forward, backward) in zip(places, results):
            partial[r] += forward
            partial[c] += backward
        return 0

    lax.fori_loop(0, count // batch, step, 0)


def remote_products_kernel(splits, whole, pieces, scaled, partial, groups, coords, targets, *refs):
    arrived, refs = refs[:pieces], refs[pieces:]
    *outs, total, count, joined = refs
    group_count = joined.shape[0]
    by_group(arrived, joined)
    total[...] = partial[...]
    for t, g, m in slots_of(groups, count, scaled.shape[0], group_count):
        total[coords[0, 0, 0, t]] += times_t(joined[g, m], scaled[t])
    for g in range(group_count):
        for m in range(MOST):
            total[jnp.maximum(targets[g, MOST + m, 0], 0)] += joined[g, MOST + m].astype(F32)
    if whole:
        for out in outs:
            out[...] = total[...].astype(out.dtype)
        return
    me = lax.axis_index("cols")
    quarter = BR // splits
    for k, out in zip(offsets(splits), outs):
        base = pl.multiple_of((me ^ k) * quarter, quarter)
        out[...] = total[pl.ds(base, quarter)].astype(out.dtype)


def quarter_sum(pieces, inv_root, me):
    quarter = pieces[0].shape[0]
    images, roots = [], []
    for k in range(quarter):
        value = pieces[0][k]
        for piece in pieces[1:]:
            value += piece[k].astype(F32)
        root = inv_root[pl.ds(me * quarter + k, 1), :]
        images.append(value * root)
        roots.append(root)
    return images, roots


def eliminate(gram, right):
    shape = (WIDTH, LANES)
    row = lax.broadcasted_iota(jnp.int32, shape, 0)
    columns = [jnp.broadcast_to(gram[:, k : k + 1], shape) for k in range(WIDTH)]
    pivots = jnp.zeros(shape, F32)
    for k in range(WIDTH):
        pivot = columns[k][k : k + 1]
        pivots = jnp.where(row == k, pivot, pivots)
        factor = jnp.where(row > k, columns[k] * (1.0 / pivot), 0.0)
        for n in range(k + 1, WIDTH):
            columns[n] = columns[n] - factor * columns[n][k : k + 1]
        right = [block - factor * block[k : k + 1] for block in right]
    root = 1.0 / jnp.sqrt(pivots)
    return [block * root for block in right]


def middle_factor_kernel(*refs):
    *arrived, inverse = refs
    gram = jnp.zeros((WIDTH, WIDTH), F32)
    for block in [piece[g, 2 * MOST] for piece in arrived for g in range(piece.shape[0])]:
        block = block.astype(F32)
        gram += (block[:, 2 * WIDTH : 3 * WIDTH] + block[:, WIDTH : 2 * WIDTH]) + block[:, :WIDTH]
    eye = lax.broadcasted_iota(jnp.int32, (WIDTH, LANES), 0) == lax.broadcasted_iota(
        jnp.int32, (WIDTH, LANES), 1
    )
    (result,) = eliminate(gram, [eye.astype(F32)])
    inverse[...] = result[:, :WIDTH]


def last_quarter_kernel(splits, vertices, inv_root, inverse, *refs):
    pieces, (image_out, grams) = refs[:splits], refs[splits:]
    images, _ = quarter_sum(pieces, inv_root, lax.axis_index("cols"))
    image = jnp.dot(
        inverse[...], jnp.concatenate(images, axis=1), precision=HIGHEST, preferred_element_type=F32
    )
    image_out[...] = image
    gram = lax.dot_general(
        image, image, (((1,), (1,)), ((), ())), precision=HIGHEST, preferred_element_type=F32
    )
    gram = gram / vertices
    block = jnp.concatenate([gram[2 * n : 2 * n + 2] for n in range(WIDTH // 2)], axis=1)
    for n in range(grams.shape[0]):
        grams[n] = block


def finish_kernel(grams, image, out):
    block = grams[0]
    for n in range(1, grams.shape[0]):
        block = block + grams[n]
    gram = jnp.concatenate(
        [block[:, WIDTH * n : WIDTH * (n + 1)] for n in range(WIDTH // 2)], axis=0
    )
    starts = range(0, out.shape[1], LANES)
    for n, block in zip(starts, eliminate(gram, [image[:, n : n + LANES] for n in starts])):
        out[:, n : n + LANES] = block


def per_device(
    local_weights,
    local_gains,
    local_coords,
    remote_weights,
    remote_gains,
    remote_groups,
    remote_coords,
    start_block,
):
    groups = lax.axis_size("rows")
    splits = lax.axis_size("cols")
    vertices = groups * BR * TILE
    quarter = BR // splits
    local_coords, remote_coords = jnp.swapaxes(local_coords, 2, 3), jnp.swapaxes(remote_coords, 2, 3)
    local_tiles, remote_tiles = local_weights.shape[2], remote_weights.shape[2]
    count = pltpu.SMEM((groups,), jnp.int32)

    partners = [2 * 2**k - 1 for k in range(splits.bit_length() - 1)]

    def swap(value, k):
        return lax.ppermute(value, "cols", [(j, j ^ k) for j in range(splits)])

    def trade(value):
        return lax.all_to_all(value, "rows", split_axis=0, concat_axis=0, tiled=True)

    def sent_blocks(block, dtype):
        if by_chips(groups):
            return (shape((groups // 2,) + block, dtype),) * 2
        return (shape((groups,) + block, dtype),)

    def exchange(sent, before=()):
        if not by_chips(groups):
            return [trade(sent[0])]
        near, far = sent
        passed = lax.ppermute(far, "rows", [(j, j ^ 1) for j in range(groups)])
        own, *others = call(
            forward_kernel,
            (shape((2,) + near.shape[1:], near.dtype),) * (groups // 2),
            [vmem, vmem] + [anywhere] * len(before),
            name="forward",
        )(near, passed, *before)
        return [own] + [
            lax.ppermute(piece, "rows", [(j, j ^ (2 * k)) for j in range(groups)])
            for k, piece in zip(offsets(groups // 2)[1:], others)
        ]

    listing = (remote_weights, remote_gains, remote_groups, remote_coords, local_weights)
    remote_raw, held, *sent = call(
        remote_degree_kernel,
        (
            shape((remote_tiles, TILE, TILE), BF16),
            shape((HEAD, TILE, TILE), BF16),
        )
        + sent_blocks((8, TILE), F32),
        [hbm] * len(listing),
        [
            pltpu.VMEM(remote_gains.shape, F32),
            pltpu.SMEM(remote_groups.shape, jnp.int32),
            pltpu.SMEM(remote_coords.shape, jnp.int32),
            pltpu.VMEM((groups, 8, TILE), F32),
            count,
            pltpu.SemaphoreType.DMA((5,)),
        ],
        name="remote_degree",
    )(*[in_hbm(value) for value in listing])
    lanes = pltpu.VMEM((TILE, LANES), F32)
    early_degree = call(
        early_degree_kernel,
        shape((BR, TILE)),
        [vmem] * 6,
        [lanes, lanes, pltpu.VMEM((HEAD, TILE), F32)],
        name="early_degree",
    )(remote_raw, remote_gains, remote_coords, held, local_gains, local_coords)
    sums_in = exchange(sent, (early_degree,))
    late_degree, local_raw = call(
        functools.partial(local_degree_kernel, HEAD),
        (shape((BR, TILE)), shape((local_tiles - HEAD, TILE, TILE), BF16)),
        [hbm, vmem, vmem],
        [
            lanes,
            pltpu.VMEM((local_tiles - HEAD, TILE), F32),
            pltpu.SemaphoreType.DMA(((local_tiles - HEAD) // CHUNK,)),
        ],
        moved=10**7,
        name="local_degree",
    )(in_hbm(local_weights), local_gains, local_coords)
    joined, targets = call(
        join_degree_kernel,
        (shape((BR, TILE)), shape((groups, 8, TILE), jnp.int32)),
        [vmem] * (2 + len(sums_in)),
        [pltpu.VMEM((groups, 8, TILE), F32)],
        name="join_degree",
    )(early_degree, late_degree, *sums_in)
    far_scalars = [remote_groups, remote_coords, targets]
    joined, remote_gains, local_gains = lax.optimization_barrier(
        (joined, remote_gains, local_gains)
    )
    degrees = [joined] + [swap(joined, k) for k in range(1, splits)]
    remote_scaled = scale(remote_raw, remote_gains, "remote_scale")
    local_scaled = scale(held, local_gains, "local_scale")

    def staging(blocks):
        return pltpu.VMEM((groups, blocks, WIDTH, TILE), BF16)

    inv_root, x, *sent = call(
        functools.partial(first_block_kernel, splits),
        (shape((BR, TILE)), shape((BR, WIDTH, TILE), BF16))
        + sent_blocks((2 * MOST, WIDTH, TILE), BF16),
        [vmem, vmem, vmem, vmem, vmem, anywhere] + [vmem] * splits,
        [count, staging(2 * MOST)],
        name="first_block",
    )(start_block, remote_scaled, *far_scalars, local_scaled, *degrees)

    def local_products(first, number, x, tiles, *more):
        return call(
            functools.partial(local_products_kernel, first),
            shape((BR, WIDTH, TILE)),
            [vmem, vmem, vmem] + [vmem] * len(more),
            [pltpu.SMEM((2, local_tiles), jnp.int32)],
            flops=4 * number * TILE * TILE * WIDTH,
            moved=2 * number * TILE * TILE,
            name="local_products",
        )(x, tiles, local_coords, *more)

    def product(x, sent, out_shape, whole):
        partial = local_products(0, HEAD, x, local_scaled)
        arrived = exchange(sent, (partial,))
        partial = local_products(HEAD, local_tiles - HEAD, x, local_raw, local_gains, partial)
        return arrived, call(
            functools.partial(remote_products_kernel, splits, whole, len(arrived)),
            out_shape,
            [vmem, vmem, vmem, vmem, vmem] + [vmem] * len(arrived),
            [pltpu.VMEM((BR, WIDTH, TILE), F32), count, staging(sent[0].shape[1])],
            name="remote_products",
        )(remote_scaled, partial, *far_scalars, *arrived)

    _, (own, sent) = product(
        x, sent, (shape((BR, WIDTH, TILE)), shape((BR, WIDTH, TILE), BF16)), True
    )
    for k in partners[:-1]:
        own, sent = call(
            pair_sum_kernel,
            (shape((BR, WIDTH, TILE)), shape((BR, WIDTH, TILE), BF16)),
            [vmem, vmem],
            name="pair_sum",
        )(own, swap(sent, k))
    x, *sent = call(
        functools.partial(next_block_kernel, vertices),
        (shape((BR, WIDTH, TILE), BF16),) + sent_blocks((2 * MOST + 1, WIDTH, TILE), BF16),
        [vmem, vmem, vmem, vmem, vmem, vmem, vmem],
        [count, staging(2 * MOST + 1)],
        name="next_block",
    )(
        remote_scaled,
        inv_root,
        *far_scalars,
        own,
        swap(sent, partners[-1]),
    )
    arrived, sent = product(
        x,
        sent,
        tuple(shape((quarter, WIDTH, TILE), BF16 if k else F32) for k in range(splits)),
        False,
    )
    pieces = [sent[0]] + [swap(part, k) for k, part in zip(offsets(splits)[1:], sent[1:])]
    inverse = call(
        middle_factor_kernel,
        shape((WIDTH, WIDTH)),
        [vmem] * len(arrived),
        name="middle_factor",
    )(*arrived)
    image, grams = call(
        functools.partial(last_quarter_kernel, splits, vertices),
        (shape((WIDTH, quarter * TILE)), shape((groups * splits, 2, LANES))),
        [vmem] * (2 + splits),
        name="last_quarter",
    )(inv_root, inverse, *pieces)
    grams = lax.all_to_all(
        grams, ("rows", "cols"), split_axis=0, concat_axis=0, tiled=True
    )
    return call(finish_kernel, shape((WIDTH, quarter * TILE)), [vmem, vmem], name="finish")(
        grams, image
    )


def solution(mesh):
    in_specs = (
        P("rows", "cols", None, None, None),
        P("rows", "cols", None, None, None),
        P("rows", "cols", None, None),
        P("rows", "cols", None, None, None),
        P("rows", "cols", None, None, None),
        P("rows", "cols", None),
        P("rows", "cols", None, None),
        P(None, "rows"),
    )
    out_specs = P(None, ("rows", "cols"))
    return jax.shard_map(
        per_device, mesh=mesh, in_specs=in_specs, out_specs=out_specs, check_vma=False
    )
```

```python
import functools

import jax
import jax.numpy as jnp
from jax import lax
from jax.experimental import pallas as pl
from jax.experimental.pallas import tpu as pltpu
from jax.sharding import PartitionSpec as P

TILE = 256
WIDTH = 16
BR = 16
MOST = 2
CHUNK = 8
HEAD = 8
LANES = 128
F32 = jnp.float32
BF16 = jnp.bfloat16
HIGHEST = lax.Precision.HIGHEST
VMEM_LIMIT = 16 * 1024 * 1024

vmem = pl.BlockSpec(memory_space=pltpu.VMEM)
hbm = pl.BlockSpec(memory_space=pltpu.HBM)
anywhere = pl.BlockSpec(memory_space=pl.ANY)


def shape(dims, dtype=F32):
    return jax.ShapeDtypeStruct(dims, dtype)


def call(kernel, out_shape, in_specs, scratch_shapes=(), flops=10**6, moved=10**6, name=None):
    return pl.pallas_call(
        kernel,
        out_shape=out_shape,
        in_specs=in_specs,
        out_specs=jax.tree.map(lambda _: vmem, out_shape),
        scratch_shapes=scratch_shapes,
        cost_estimate=pl.CostEstimate(flops=flops, bytes_accessed=moved, transcendentals=0),
        compiler_params=pltpu.CompilerParams(vmem_limit_bytes=VMEM_LIMIT),
        name=name,
    )


def times(left, right):
    return lax.dot_general(left, right, (((1,), (0,)), ((), ())), preferred_element_type=F32)


def times_t(left, right):
    return lax.dot_general(left, right, (((1,), (1,)), ((), ())), preferred_element_type=F32)


def in_hbm(value):
    return pltpu.with_memory_space_constraint(value, pltpu.HBM)


def fetch(sources, targets, sems):
    copies = [
        pltpu.make_async_copy(source, target, sems.at[n])
        for n, (source, target) in enumerate(zip(sources, targets))
    ]
    for copy in copies:
        copy.start()

    def wait():
        for copy in copies:
            copy.wait()

    return wait


def slots_of(groups_ref, count_ref, tile_count, group_count):
    seen = []
    for t in range(tile_count):
        g = groups_ref[0, 0, t]
        m = sum((earlier == g).astype(jnp.int32) for earlier in seen) if seen else 0
        seen.append(g)
        yield t, g, m


def remote_degree_kernel(weights, gains, groups, coords, near_weights, tiles, held, *refs):
    *outs, tile_gains, tile_groups, tile_coords, staged, count, sems = refs
    group_count = staged.shape[0]
    wait = fetch(
        (groups, coords, gains, weights.at[0, 0]),
        (tile_groups, tile_coords, tile_gains, tiles),
        sems.at[pl.ds(0, 4)],
    )
    wait_held = fetch(
        (near_weights.at[0, 0, pl.ds(0, held.shape[0])],), (held,), sems.at[pl.ds(4, 1)]
    )
    sub = lax.broadcasted_iota(jnp.int32, (8, TILE), 0)
    blank = jnp.where((sub >= MOST) & (sub < 2 * MOST), -1.0, 0.0).astype(F32)
    for g in range(group_count):
        staged[g] = blank
    core = lax.axis_index("rows") % 2
    wait()
    for t, g, m in slots_of(tile_groups, count, tiles.shape[0], group_count):
        place = place_of(g, group_count, core)
        c = tile_coords[0, 0, 1, t]
        staged[place, pl.ds(m, 1), :] = column_sums(jnp.abs(tiles[t]), jnp.abs(tile_gains[0, 0, t]))
        staged[place, pl.ds(MOST + m, 1), :] = jnp.full((1, TILE), c, jnp.int32).astype(F32)
    split_out(staged, outs)
    wait_held()


def halves_of(value):
    high = value.astype(BF16)
    return high, (value - high.astype(F32)).astype(BF16)


def add_by_place(places, values):
    shape = (BR, places.shape[1])
    chosen = (lax.broadcasted_iota(jnp.int32, shape, 0) == places).astype(BF16)
    high, low = halves_of(values)
    return times(chosen, high) + times(chosen, low)


def column_sums(size, pair):
    top = lax.broadcasted_iota(jnp.int32, (8, TILE), 0) == 0
    left = jnp.where(top, pair[0:1, :], 0.0)
    high = left.astype(BF16).astype(F32)
    sums = times(jnp.concatenate([high, left - high], axis=0).astype(BF16), size)
    return (sums[0:1] + sums[8:9]) * pair[1:2, :]


def spread_row_sums(by_row, t, size, pair):
    sums = jnp.sum(size.astype(F32) * pair[1:2, :], axis=1, keepdims=True)
    lane = lax.broadcasted_iota(jnp.int32, by_row.shape, 1)
    by_row[...] = jnp.where(lane == t, sums, by_row[...])


def rows_by_place(by_row, gains, places):
    count = gains.shape[0]
    return add_by_place(places, jnp.transpose(by_row[...])[:count] * jnp.abs(gains))


def early_degree_kernel(
    remote, remote_gains, remote_coords, held, gains, coords, degree, remote_row, by_row, by_col
):
    remote_row[...] = jnp.zeros(remote_row.shape, F32)
    by_row[...] = jnp.zeros(by_row.shape, F32)

    def remote_step(n, _):
        for k in range(CHUNK):
            t = n * CHUNK + k
            pair = jnp.abs(remote_gains[0, 0, t])
            spread_row_sums(remote_row, t, jnp.abs(remote[t]), pair)
        return 0

    lax.fori_loop(0, remote.shape[0] // CHUNK, remote_step, 0)
    count = held.shape[0]
    for t in range(count):
        size, pair = jnp.abs(held[t]), jnp.abs(gains[0, 0, t])
        by_col[t : t + 1, :] = column_sums(size, pair)
        spread_row_sums(by_row, t, size, pair)
    degree[...] = (
        rows_by_place(remote_row, remote_gains[0, 0, :, 0, :], remote_coords[0, 0, 0:1, :])
        + rows_by_place(by_row, gains[0, 0, :count, 0, :], coords[0, 0, 0:1, :count])
        + add_by_place(coords[0, 0, 1:2, :count], by_col[...])
    )


def local_degree_kernel(first, weights, gains, coords, degree, tiles, by_row, by_col, sems):
    count = tiles.shape[0]

    def copy_of(n):
        source = weights.at[0, 0, pl.ds(first + n * CHUNK, CHUNK)]
        return pltpu.make_async_copy(source, tiles.at[pl.ds(n * CHUNK, CHUNK)], sems.at[n])

    for n in range(count // CHUNK):
        copy_of(n).start()
    by_row[...] = jnp.zeros(by_row.shape, F32)

    def step(n, _):
        copy_of(n).wait()
        for k in range(CHUNK):
            t = n * CHUNK + k
            size, pair = jnp.abs(tiles[t]), jnp.abs(gains[0, 0, first + t])
            by_col[pl.ds(t, 1), :] = column_sums(size, pair)
            spread_row_sums(by_row, t, size, pair)
        return 0

    lax.fori_loop(0, count // CHUNK, step, 0)
    degree[...] = rows_by_place(
        by_row, gains[0, 0, first:, 0, :], coords[0, 0, 0:1, first:]
    ) + add_by_place(coords[0, 0, 1:2, first:], by_col[...])


def scale_kernel(raw, gains, scaled):
    def step(n, _):
        base = n * CHUNK
        row_gain = jnp.transpose(gains[0, 0, pl.ds(base, CHUNK), 0, :])
        for k in range(CHUNK):
            scaled[base + k] = (
                row_gain[:, k : k + 1]
                * raw[base + k].astype(F32)
                * gains[0, 0, base + k, 1:2, :]
            ).astype(BF16)
        return 0

    lax.fori_loop(0, scaled.shape[0] // CHUNK, step, 0)


def scale(raw, gains, name):
    return call(
        scale_kernel, shape(raw.shape, BF16), [vmem, vmem], flops=2 * raw.size, name=name
    )(raw, gains)


def join_degree_kernel(early, late, *refs):
    *arrived, joined, targets, sums = refs
    by_group(arrived, sums)
    targets[...] = sums[...].astype(jnp.int32)
    total = early[...] + late[...]
    sub = lax.broadcasted_iota(jnp.int32, total.shape, 0).astype(F32)
    for g in range(sums.shape[0]):
        block = sums[g]
        for m in range(MOST):
            hit = sub == block[MOST + m : MOST + m + 1, :]
            total += jnp.where(hit, block[m : m + 1, :], 0.0)
    joined[...] = total


def offsets(count):
    return [0] + list(range(count - 1, 0, -1))


def by_chips(groups):
    return groups // 2 <= 4


def place_of(group, group_count, core):
    if not by_chips(group_count):
        return group
    return ((group + core) % 2) * (group_count // 2) + group // 2


def outgoing(x, scaled, groups, coords, targets, staged, count, gram=None):
    group_count = staged.shape[0]
    core = lax.axis_index("rows") % 2
    for g in range(group_count):
        staged[g, MOST : 2 * MOST] = jnp.zeros((MOST, WIDTH, TILE), BF16)
        if gram is not None:
            staged[g, 2 * MOST] = gram
    for t, g, m in slots_of(groups, count, scaled.shape[0], group_count):
        place = place_of(g, group_count, core)
        staged[place, MOST + m] = times(x[coords[0, 0, 0, t]], scaled[t]).astype(BF16)
    for g in range(group_count):
        place = place_of(g, group_count, core)
        for m in range(MOST):
            staged[place, m] = x[jnp.maximum(targets[g, MOST + m, 0], 0)]


def split_out(staged, outs):
    size = outs[0].shape[0]
    for k, out in enumerate(outs):
        out[...] = staged[k * size : (k + 1) * size]


def forward_kernel(near, passed, *refs):
    chips = near.shape[0]
    pieces = refs[-chips:]
    me = lax.axis_index("rows")
    chip, core = me // 2, me % 2
    for k, piece in zip(offsets(chips), pieces):
        piece[core] = near[chip ^ k]
        piece[1 - core] = passed[chip ^ k]


def by_group(arrived, joined):
    if len(arrived) == 1:
        joined[...] = arrived[0][...]
        return
    chip = lax.axis_index("rows") // 2
    for k, piece in zip(offsets(len(arrived)), arrived):
        joined[pl.ds((chip ^ k) * 2, 2)] = piece[...]


def first_block_kernel(splits, start, scaled, groups, coords, targets, later, *refs):
    parts, (inv_root, x, *refs) = refs[:splits], refs[splits:]
    *outs, count, staged = refs
    routes = (groups, coords, targets)
    degree = parts[0][...]
    for part in parts[1:]:
        degree += part[...]
    inv = 1.0 / jnp.sqrt(degree)
    inv_root[...] = inv
    for k in range(BR):
        x[k] = (start[:, k * TILE : (k + 1) * TILE] * inv[k : k + 1, :]).astype(BF16)
    outgoing(x, scaled, *routes, staged, count)
    split_out(staged, outs)


def pair_sum_kernel(mine, theirs, total, sent):
    value = mine[...] + theirs[...].astype(F32)
    total[...] = value
    sent[...] = value.astype(BF16)


def next_block_kernel(
    vertices, scaled, inv_root, groups, coords, targets, mine, theirs, x, *refs
):
    *outs, count, staged = refs
    routes = (groups, coords, targets)
    gram = jnp.zeros((2 * WIDTH, 2 * WIDTH), F32)
    for k in range(BR):
        value = mine[k] + theirs[k].astype(F32)
        root = inv_root[k : k + 1, :]
        image = value * root
        x[k] = (image * root).astype(BF16)
        high = image.astype(BF16)
        halves = jnp.concatenate([high, (image - high.astype(F32)).astype(BF16)], axis=0)
        gram += times_t(halves, halves)
    low = gram[:WIDTH, WIDTH:] + gram[WIDTH:, :WIDTH] + gram[WIDTH:, WIDTH:]
    gram = (gram[:WIDTH, :WIDTH] + low) / vertices
    high = gram.astype(BF16)
    middle = (gram - high.astype(F32)).astype(BF16)
    low = (gram - high.astype(F32) - middle.astype(F32)).astype(BF16)
    block = jnp.concatenate(
        [high, middle, low, jnp.zeros((WIDTH, TILE - 3 * WIDTH), BF16)], axis=1
    )
    outgoing(x, scaled, *routes, staged, count, block)
    split_out(staged, outs)


def local_products_kernel(first, x, tiles, coords, *refs):
    *refs, partial, table = refs
    gains, earlier = refs or (None, None)
    count = tiles.shape[0]
    batch = next(size for size in (20, 16, CHUNK) if count % size == 0)
    partial[...] = earlier[...] if refs else jnp.zeros(partial.shape, F32)
    for t in range(first, first + count):
        for side in range(2):
            table[side, t] = coords[0, 0, side, t]

    def step(n, _):
        base = first + n * batch
        if refs:
            row_gains = [
                jnp.transpose(gains[0, 0, pl.ds(base + k, min(CHUNK, batch - k)), 0, :])
                for k in range(0, batch, CHUNK)
            ]
        places, results = [], []
        for k in range(batch):
            t = base + k
            r, c = table[0, t], table[1, t]
            tile = tiles[n * batch + k]
            if refs:
                row_gain = row_gains[k // CHUNK][:, k % CHUNK : k % CHUNK + 1]
                tile = (row_gain * tile.astype(F32) * gains[0, 0, t, 1:2, :]).astype(BF16)
            results.append((times_t(x[c], tile), times(x[r], tile)))
            places.append((r, c))
        for (r, c), (forward, backward) in zip(places, results):
            partial[r] += forward
            partial[c] += backward
        return 0

    lax.fori_loop(0, count // batch, step, 0)


def remote_products_kernel(splits, whole, pieces, scaled, partial, groups, coords, targets, *refs):
    arrived, refs = refs[:pieces], refs[pieces:]
    *outs, total, count, joined = refs
    group_count = joined.shape[0]
    by_group(arrived, joined)
    total[...] = partial[...]
    for t, g, m in slots_of(groups, count, scaled.shape[0], group_count):
        total[coords[0, 0, 0, t]] += times_t(joined[g, m], scaled[t])
    for g in range(group_count):
        for m in range(MOST):
            total[jnp.maximum(targets[g, MOST + m, 0], 0)] += joined[g, MOST + m].astype(F32)
    if whole:
        for out in outs:
            out[...] = total[...].astype(out.dtype)
        return
    me = lax.axis_index("cols")
    quarter = BR // splits
    for k, out in zip(offsets(splits), outs):
        base = pl.multiple_of((me ^ k) * quarter, quarter)
        out[...] = total[pl.ds(base, quarter)].astype(out.dtype)


def quarter_sum(pieces, inv_root, me):
    quarter = pieces[0].shape[0]
    images, roots = [], []
    for k in range(quarter):
        value = pieces[0][k]
        for piece in pieces[1:]:
            value += piece[k].astype(F32)
        root = inv_root[pl.ds(me * quarter + k, 1), :]
        images.append(value * root)
        roots.append(root)
    return images, roots


def eliminate(gram, right):
    shape = (WIDTH, LANES)
    row = lax.broadcasted_iota(jnp.int32, shape, 0)
    columns = [jnp.broadcast_to(gram[:, k : k + 1], shape) for k in range(WIDTH)]
    pivots = jnp.zeros(shape, F32)
    for k in range(WIDTH):
        pivot = columns[k][k : k + 1]
        pivots = jnp.where(row == k, pivot, pivots)
        factor = jnp.where(row > k, columns[k] * (1.0 / pivot), 0.0)
        for n in range(k + 1, WIDTH):
            columns[n] = columns[n] - factor * columns[n][k : k + 1]
        right = [block - factor * block[k : k + 1] for block in right]
    root = 1.0 / jnp.sqrt(pivots)
    return [block * root for block in right]


def middle_factor_kernel(*refs):
    *arrived, inverse = refs
    gram = jnp.zeros((WIDTH, WIDTH), F32)
    for block in [piece[g, 2 * MOST] for piece in arrived for g in range(piece.shape[0])]:
        block = block.astype(F32)
        gram += (block[:, 2 * WIDTH : 3 * WIDTH] + block[:, WIDTH : 2 * WIDTH]) + block[:, :WIDTH]
    eye = lax.broadcasted_iota(jnp.int32, (WIDTH, LANES), 0) == lax.broadcasted_iota(
        jnp.int32, (WIDTH, LANES), 1
    )
    (result,) = eliminate(gram, [eye.astype(F32)])
    inverse[...] = result[:, :WIDTH]


def last_quarter_kernel(splits, vertices, inv_root, inverse, *refs):
    pieces, (image_out, grams) = refs[:splits], refs[splits:]
    images, _ = quarter_sum(pieces, inv_root, lax.axis_index("cols"))
    image = jnp.dot(
        inverse[...], jnp.concatenate(images, axis=1), precision=HIGHEST, preferred_element_type=F32
    )
    image_out[...] = image
    gram = lax.dot_general(
        image, image, (((1,), (1,)), ((), ())), precision=HIGHEST, preferred_element_type=F32
    )
    gram = gram / vertices
    block = jnp.concatenate([gram[2 * n : 2 * n + 2] for n in range(WIDTH // 2)], axis=1)
    for n in range(grams.shape[0]):
        grams[n] = block


def finish_kernel(grams, image, out):
    block = grams[0]
    for n in range(1, grams.shape[0]):
        block = block + grams[n]
    gram = jnp.concatenate(
        [block[:, WIDTH * n : WIDTH * (n + 1)] for n in range(WIDTH // 2)], axis=0
    )
    starts = range(0, out.shape[1], LANES)
    for n, block in zip(starts, eliminate(gram, [image[:, n : n + LANES] for n in starts])):
        out[:, n : n + LANES] = block


def per_device(
    local_weights,
    local_gains,
    local_coords,
    remote_weights,
    remote_gains,
    remote_groups,
    remote_coords,
    start_block,
):
    groups = lax.axis_size("rows")
    splits = lax.axis_size("cols")
    vertices = groups * BR * TILE
    quarter = BR // splits
    local_coords, remote_coords = jnp.swapaxes(local_coords, 2, 3), jnp.swapaxes(remote_coords, 2, 3)
    local_tiles, remote_tiles = local_weights.shape[2], remote_weights.shape[2]
    count = pltpu.SMEM((groups,), jnp.int32)

    partners = [2 * 2**k - 1 for k in range(splits.bit_length() - 1)]

    def swap(value, k):
        return lax.ppermute(value, "cols", [(j, j ^ k) for j in range(splits)])

    def trade(value):
        return lax.all_to_all(value, "rows", split_axis=0, concat_axis=0, tiled=True)

    def sent_blocks(block, dtype):
        if by_chips(groups):
            return (shape((groups // 2,) + block, dtype),) * 2
        return (shape((groups,) + block, dtype),)

    def exchange(sent, before=()):
        if not by_chips(groups):
            return [trade(sent[0])]
        near, far = sent
        passed = lax.ppermute(far, "rows", [(j, j ^ 1) for j in range(groups)])
        own, *others = call(
            forward_kernel,
            (shape((2,) + near.shape[1:], near.dtype),) * (groups // 2),
            [vmem, vmem] + [anywhere] * len(before),
            name="forward",
        )(near, passed, *before)
        return [own] + [
            lax.ppermute(piece, "rows", [(j, j ^ (2 * k)) for j in range(groups)])
            for k, piece in zip(offsets(groups // 2)[1:], others)
        ]

    listing = (remote_weights, remote_gains, remote_groups, remote_coords, local_weights)
    remote_raw, held, *sent = call(
        remote_degree_kernel,
        (
            shape((remote_tiles, TILE, TILE), BF16),
            shape((HEAD, TILE, TILE), BF16),
        )
        + sent_blocks((8, TILE), F32),
        [hbm] * len(listing),
        [
            pltpu.VMEM(remote_gains.shape, F32),
            pltpu.SMEM(remote_groups.shape, jnp.int32),
            pltpu.SMEM(remote_coords.shape, jnp.int32),
            pltpu.VMEM((groups, 8, TILE), F32),
            count,
            pltpu.SemaphoreType.DMA((5,)),
        ],
        name="remote_degree",
    )(*[in_hbm(value) for value in listing])
    lanes = pltpu.VMEM((TILE, LANES), F32)
    early_degree = call(
        early_degree_kernel,
        shape((BR, TILE)),
        [vmem] * 6,
        [lanes, lanes, pltpu.VMEM((HEAD, TILE), F32)],
        name="early_degree",
    )(remote_raw, remote_gains, remote_coords, held, local_gains, local_coords)
    sums_in = exchange(sent, (early_degree,))
    late_degree, local_raw = call(
        functools.partial(local_degree_kernel, HEAD),
        (shape((BR, TILE)), shape((local_tiles - HEAD, TILE, TILE), BF16)),
        [hbm, vmem, vmem],
        [
            lanes,
            pltpu.VMEM((local_tiles - HEAD, TILE), F32),
            pltpu.SemaphoreType.DMA(((local_tiles - HEAD) // CHUNK,)),
        ],
        moved=10**7,
        name="local_degree",
    )(in_hbm(local_weights), local_gains, local_coords)
    joined, targets = call(
        join_degree_kernel,
        (shape((BR, TILE)), shape((groups, 8, TILE), jnp.int32)),
        [vmem] * (2 + len(sums_in)),
        [pltpu.VMEM((groups, 8, TILE), F32)],
        name="join_degree",
    )(early_degree, late_degree, *sums_in)
    far_scalars = [remote_groups, remote_coords, targets]
    joined, remote_gains, local_gains = lax.optimization_barrier(
        (joined, remote_gains, local_gains)
    )
    degrees = [joined] + [swap(joined, k) for k in range(1, splits)]
    remote_scaled = scale(remote_raw, remote_gains, "remote_scale")
    local_scaled = scale(held, local_gains, "local_scale")

    def staging(blocks):
        return pltpu.VMEM((groups, blocks, WIDTH, TILE), BF16)

    inv_root, x, *sent = call(
        functools.partial(first_block_kernel, splits),
        (shape((BR, TILE)), shape((BR, WIDTH, TILE), BF16))
        + sent_blocks((2 * MOST, WIDTH, TILE), BF16),
        [vmem, vmem, vmem, vmem, vmem, anywhere] + [vmem] * splits,
        [count, staging(2 * MOST)],
        name="first_block",
    )(start_block, remote_scaled, *far_scalars, local_scaled, *degrees)

    def local_products(first, number, x, tiles, *more):
        return call(
            functools.partial(local_products_kernel, first),
            shape((BR, WIDTH, TILE)),
            [vmem, vmem, vmem] + [vmem] * len(more),
            [pltpu.SMEM((2, local_tiles), jnp.int32)],
            flops=4 * number * TILE * TILE * WIDTH,
            moved=2 * number * TILE * TILE,
            name="local_products",
        )(x, tiles, local_coords, *more)

    def product(x, sent, out_shape, whole):
        partial = local_products(0, HEAD, x, local_scaled)
        arrived = exchange(sent, (partial,))
        partial = local_products(HEAD, local_tiles - HEAD, x, local_raw, local_gains, partial)
        return arrived, call(
            functools.partial(remote_products_kernel, splits, whole, len(arrived)),
            out_shape,
            [vmem, vmem, vmem, vmem, vmem] + [vmem] * len(arrived),
            [pltpu.VMEM((BR, WIDTH, TILE), F32), count, staging(sent[0].shape[1])],
            name="remote_products",
        )(remote_scaled, partial, *far_scalars, *arrived)

    _, (own, sent) = product(
        x, sent, (shape((BR, WIDTH, TILE)), shape((BR, WIDTH, TILE), BF16)), True
    )
    for k in partners[:-1]:
        own, sent = call(
            pair_sum_kernel,
            (shape((BR, WIDTH, TILE)), shape((BR, WIDTH, TILE), BF16)),
            [vmem, vmem],
            name="pair_sum",
        )(own, swap(sent, k))
    x, *sent = call(
        functools.partial(next_block_kernel, vertices),
        (shape((BR, WIDTH, TILE), BF16),) + sent_blocks((2 * MOST + 1, WIDTH, TILE), BF16),
        [vmem, vmem, vmem, vmem, vmem, vmem, vmem],
        [count, staging(2 * MOST + 1)],
        name="next_block",
    )(
        remote_scaled,
        inv_root,
        *far_scalars,
        own,
        swap(sent, partners[-1]),
    )
    arrived, sent = product(
        x,
        sent,
        tuple(shape((quarter, WIDTH, TILE), BF16 if k else F32) for k in range(splits)),
        False,
    )
    pieces = [sent[0]] + [swap(part, k) for k, part in zip(offsets(splits)[1:], sent[1:])]
    inverse = call(
        middle_factor_kernel,
        shape((WIDTH, WIDTH)),
        [vmem] * len(arrived),
        name="middle_factor",
    )(*arrived)
    image, grams = call(
        functools.partial(last_quarter_kernel, splits, vertices),
        (shape((WIDTH, quarter * TILE)), shape((groups * splits, 2, LANES))),
        [vmem] * (2 + splits),
        name="last_quarter",
    )(inv_root, inverse, *pieces)
    grams = lax.all_to_all(
        grams, ("rows", "cols"), split_axis=0, concat_axis=0, tiled=True
    )
    return call(finish_kernel, shape((WIDTH, quarter * TILE)), [vmem, vmem], name="finish")(
        grams, image
    )


def solution(mesh):
    in_specs = (
        P("rows", "cols", None, None, None),
        P("rows", "cols", None, None, None),
        P("rows", "cols", None, None),
        P("rows", "cols", None, None, None),
        P("rows", "cols", None, None, None),
        P("rows", "cols", None),
        P("rows", "cols", None, None),
        P(None, "rows"),
    )
    out_specs = P(None, ("rows", "cols"))
    return jax.shard_map(
        per_device, mesh=mesh, in_specs=in_specs, out_specs=out_specs, check_vma=False
    )
```
